32 devices in a mesh: groups: 2 (over x), tm: 8 (over z, y), block: 2 (over core).
Axes of the slice: x: 2, y: 2, z: 4, core: 2. Of those that a mesh axis runs over, the one named last changes fastest.
Arguments:
- scaled_residual_maps: bfloat16 [32, 128, 16, 512], P(('groups', 'tm'), 'block'), parts along dimension 0, may hold values from -1.5 to 1.5
- measurement_stencil: bfloat16 [16, 7, 7], replicated, may hold values from -0.21875 to 0.21875
- observed_partition: int32 [32, 128], P(('groups', 'tm'), 'block'), parts along dimension 0, may hold values from 0 to 1
- active_probe_total: int32 [32, 2], P(('groups', 'tm'), 'block'), parts along dimension 0, may hold values from 1 to 64, as said below
- filtering_operator: bfloat16 [32, 2, 512, 512], P(('groups', 'tm'), 'block'), parts along dimension 0
- updated_covariance: bfloat16 [32, 2, 512, 512], P(('groups', 'tm'), 'block'), parts along dimension 0
- backward_factor: bfloat16 [32, 2, 512, 512], P(('groups', 'tm'), 'block'), parts along dimension 0
- propagator: bfloat16 [2, 512, 512], P('block'), may hold values from -0.25 to 0.25
- initial_mean: float32 [4, 512], P(('groups', 'block')), parts along dimension 0, may hold values from -6 to 6
Outputs:
- updated_means: float32 [32, 2, 512], P(('groups', 'tm'), 'block'), parts along dimension 0
- smoothed: float32 [32, 2, 512], P(('groups', 'tm'), 'block'), parts along dimension 0
The draws below stay inside these ranges and needn't reach their ends.
There are 2 independent parts, one for each index of `groups`. The reference program is written for one: setup_inputs(seed, part) draws one part's arguments, and reference() takes and returns one part's arrays. A program takes and returns all parts, laid end to end along the dimension named above; an argument that names none is the same for every part. Nothing has to cross between parts.
Inputs may be any that keep to these rules, and one draw needn't show every extreme that they name: active_probe_total[t, k] is the number of leading slots of index k of block at step t that carry a sensor; some entry equals 64.
All inputs are finite; a program needn't handle non-finite values.
Results may differ from the reference program's by a relative error of at most 0.0003.
Values sent between devices are 32-bit elements; how exact they have to be, the bound alone decides.
No kernel may reach another device: no remote copies, remote signals or barrier semaphores. Data moves between devices by JAX's collectives and lax.ppermute only.
A program may use at most 192 MiB of HBM per device.

```python
import jax
import jax.numpy as jnp
from jax import lax

UNKNOWNS_EACH = 512
GH = 16
GW = 32
CH = 16
KS = 7
NSEN_DEV = 64
HORIZON_LENGTH = 16
PARTS_EACH_TICK = 2
NSEN = 128


def decaying(key):
    first, latter_operand, third, fourth = jax.random.split(key, 4)
    low = 8.0
    span = jax.random.uniform(first, (1, PARTS_EACH_TICK, UNKNOWNS_EACH, 1), jnp.float32, jnp.log(low), jnp.log(16.0 * HORIZON_LENGTH))
    observation_moments = jax.random.randint(latter_operand, (3,), 0, HORIZON_LENGTH)
    probe_measurement_batch = jnp.any(lax.broadcasted_iota(jnp.int32, (HORIZON_LENGTH, 3), 0) == observation_moments[None, :], axis=1)
    training_objective = jax.random.uniform(third, (HORIZON_LENGTH, PARTS_EACH_TICK, UNKNOWNS_EACH, 1), jnp.float32, 0.2, 0.5)
    retain_markers = jnp.where(probe_measurement_batch[:, None, None, None], 1.0 - training_objective, 1.0)
    diag = 0.97 * jnp.exp(-jnp.exp(-span)) * retain_markers
    noise = jax.random.normal(fourth, (HORIZON_LENGTH, PARTS_EACH_TICK, UNKNOWNS_EACH, UNKNOWNS_EACH), jnp.float32) * (0.2 * UNKNOWNS_EACH ** (-0.5))
    eye = lax.broadcasted_iota(jnp.int32, (UNKNOWNS_EACH, UNKNOWNS_EACH), 0) == lax.broadcasted_iota(jnp.int32, (UNKNOWNS_EACH, UNKNOWNS_EACH), 1)
    return jnp.where(eye, diag, noise).astype(jnp.bfloat16)


def draw_filtering_operator(key, part):
    return decaying(jax.random.fold_in(key, 11))


def draw_backward_factor(key, part):
    return decaying(jax.random.fold_in(key, 23))


def draw_updated_covariance(key, part):
    first, latter_operand = jax.random.split(jax.random.fold_in(key, 37))
    diag = jnp.exp(jax.random.uniform(first, (HORIZON_LENGTH, PARTS_EACH_TICK, UNKNOWNS_EACH, 1), jnp.float32, jnp.log(0.1), jnp.log(0.4)))
    noise = jax.random.normal(latter_operand, (HORIZON_LENGTH, PARTS_EACH_TICK, UNKNOWNS_EACH, UNKNOWNS_EACH), jnp.float32) * (0.06 * UNKNOWNS_EACH ** (-0.5))
    paired = (noise + jnp.swapaxes(noise, -1, -2)) * 0.7071
    eye = lax.broadcasted_iota(jnp.int32, (UNKNOWNS_EACH, UNKNOWNS_EACH), 0) == lax.broadcasted_iota(jnp.int32, (UNKNOWNS_EACH, UNKNOWNS_EACH), 1)
    return jnp.where(eye, diag, paired).astype(jnp.bfloat16)


def draw_active_probe_total(key, part):
    first, latter_operand = jax.random.split(jax.random.fold_in(key, 41))
    counts = jax.random.randint(first, (HORIZON_LENGTH, PARTS_EACH_TICK), 1, NSEN_DEV + 1)
    spot = jax.random.randint(latter_operand, (), 0, HORIZON_LENGTH * PARTS_EACH_TICK)
    flat = lax.broadcasted_iota(jnp.int32, (HORIZON_LENGTH, PARTS_EACH_TICK), 0) * PARTS_EACH_TICK + lax.broadcasted_iota(jnp.int32, (HORIZON_LENGTH, PARTS_EACH_TICK), 1)
    return jnp.where(flat == spot, NSEN_DEV, counts).astype(jnp.int32)


def plant(drawn, stream_key, least, top_value):
    longest = drawn.shape.index(max(drawn.shape))
    spots = []
    for shift in (0, 1):
        where = [jax.random.randint(jax.random.fold_in(stream_key, axis), (), 0, length) for axis, length in enumerate(drawn.shape)]
        where[longest] = (where[longest] + shift) % drawn.shape[longest]
        spots.append(tuple(where))
    return drawn.at[spots[0]].set(least).at[spots[1]].set(top_value)


def shard_levels(own_key, shape, shards, smallest, top_value):
    loudness = 1.0
    for position, blocks in shards:
        draws = jax.random.uniform(jax.random.fold_in(jax.random.fold_in(own_key, 6), position), (blocks,), jnp.float32, smallest / len(shards), top_value / len(shards))
        loudness = loudness * jnp.repeat(jnp.exp(draws), shape[position] // blocks).reshape((-1,) + (1,) * (len(shape) - 1 - position))
    return loudness


def bell_draw(own_key, dims, width, limit, pieces=(), kind=jnp.bfloat16):
    drawn = jax.random.normal(own_key, dims, jnp.float32) * width
    if len(pieces) > 0:
        drawn = shard_levels(own_key, dims, pieces, -0.22, 0.18) * drawn
    return jnp.clip(drawn, min=-limit, max=limit).astype(kind)


def setup_inputs(seed: int = 0, part: int = 0) -> dict:
    arg_keys = jax.random.split(jax.random.key(seed), 10)
    own_keys = jax.random.split(jax.random.fold_in(arg_keys[9], part), 10)
    return {
        "scaled_residual_maps": bell_draw(own_keys[0], (HORIZON_LENGTH, NSEN, CH, UNKNOWNS_EACH), 0.25, 1.5, ((0, 8), (1, 2))),
        "measurement_stencil": bell_draw(arg_keys[1], (CH, KS, KS), (CH * KS * KS) ** -0.5, 0.21875),
        "observed_partition": plant(jax.random.randint(own_keys[2], (HORIZON_LENGTH, NSEN), 0, PARTS_EACH_TICK), jax.random.fold_in(own_keys[2], 1), 0, PARTS_EACH_TICK - 1).astype(jnp.int32),
        "active_probe_total": draw_active_probe_total(jax.random.fold_in(jax.random.fold_in(arg_keys[9], part), 71), part),
        "filtering_operator": draw_filtering_operator(jax.random.fold_in(jax.random.fold_in(arg_keys[9], part), 71), part),
        "updated_covariance": draw_updated_covariance(jax.random.fold_in(jax.random.fold_in(arg_keys[9], part), 71), part),
        "backward_factor": draw_backward_factor(jax.random.fold_in(jax.random.fold_in(arg_keys[9], part), 71), part),
        "propagator": bell_draw(arg_keys[7], (PARTS_EACH_TICK, UNKNOWNS_EACH, UNKNOWNS_EACH), UNKNOWNS_EACH ** -0.5, 0.25, ((0, 2),)),
        "initial_mean": bell_draw(own_keys[8], (PARTS_EACH_TICK, UNKNOWNS_EACH), 1.0, 6.0, ((0, 2),), jnp.float32),
    }


EXACT_ARITHMETIC = lax.Precision.HIGHEST


def reference(scaled_residual_maps, measurement_stencil, observed_partition, active_probe_total, filtering_operator, updated_covariance, backward_factor, propagator, initial_mean):
    flipped = measurement_stencil[:, ::-1, ::-1][None].astype(jnp.float32)
    slot = jnp.arange(NSEN).astype(jnp.int32)
    owner = (slot // NSEN_DEV).astype(jnp.int32)
    blocks = jnp.arange(PARTS_EACH_TICK).astype(jnp.int32)

    def step_info(packed):
        frame, aim, count = packed
        grid = frame.reshape(NSEN, CH, GH, GW).astype(jnp.float32)
        adjoint = lax.conv_general_dilated(grid, flipped, (1, 1), "SAME", dimension_numbers=("NCHW", "OIHW", "NCHW"), precision=EXACT_ARITHMETIC)
        adjoint = adjoint.reshape(NSEN, UNKNOWNS_EACH)
        alive = (slot % NSEN_DEV) < count[owner]
        weight = jnp.where((aim[:, None] == blocks[None, :]) & alive[:, None], 1.0, 0.0).astype(jnp.float32)
        return jnp.einsum("sn,sc->nc", weight, adjoint, precision=EXACT_ARITHMETIC)

    info = lax.map(step_info, (scaled_residual_maps, observed_partition, active_probe_total))
    inputs = jnp.einsum("gupl,gul->gup", updated_covariance.astype(jnp.float32), info, precision=EXACT_ARITHMETIC)

    def forward(state, packed):
        matrix, vector = packed
        state = jnp.einsum("bij,bj->bi", matrix.astype(jnp.float32), state, precision=EXACT_ARITHMETIC) + vector
        return state, state

    unused, updated_means = lax.scan(forward, initial_mean.astype(jnp.float32), (filtering_operator, inputs))
    propagate_mean = jnp.einsum("pmz,ypz->ypm", propagator.astype(jnp.float32), updated_means, precision=EXACT_ARITHMETIC)
    displacements = updated_means - jnp.einsum("gupl,gul->gup", backward_factor.astype(jnp.float32), propagate_mean, precision=EXACT_ARITHMETIC)

    def backward(state, packed):
        matrix, vector = packed
        state = jnp.einsum("bij,bj->bi", matrix.astype(jnp.float32), state, precision=EXACT_ARITHMETIC) + vector
        return state, state

    unused_last, early = lax.scan(backward, updated_means[-1], (backward_factor[:-1], displacements[:-1]), reverse=True)
    smoothed = jnp.concatenate([early, updated_means[-1:]], axis=0)
    return updated_means, smoothed
```

```python
import functools

import jax
import jax.numpy as jnp
from jax import lax
from jax.experimental import pallas as pl
from jax.experimental.pallas import tpu as pltpu
from jax.sharding import PartitionSpec as P

GH = 16
VMEM = pl.BlockSpec(memory_space=pltpu.VMEM)
PARAMS = pltpu.CompilerParams(vmem_limit_bytes=16 * 2**20)


def pieces(row, rows=8, count=3):
    at = lax.broadcasted_iota(jnp.int32, (rows, row.shape[1]), 0)
    block = jnp.zeros((rows, row.shape[1]), jnp.float32)
    rest = row
    for i in range(count):
        piece = rest.astype(jnp.bfloat16).astype(jnp.float32)
        block = jnp.where(at == i, piece, block)
        rest = rest - piece
    return block.astype(jnp.bfloat16)


def times(matrix, row):
    product = lax.dot_general(
        pieces(row), matrix, (((1,), (1,)), ((), ())), preferred_element_type=jnp.float32
    )
    return jnp.sum(product, axis=0, keepdims=True)


def info_kernel(maps_hbm, stencil_ref, observed_ref, active_ref, mine_ref, theirs_ref, maps, taps, sems):
    steps, rows, cells = maps.shape
    slots = observed_ref.shape[1]
    channels, side, _ = stencil_ref.shape
    half = side // 2
    copies = []
    for t in range(steps):
        copies.append(pltpu.make_async_copy(maps_hbm.at[t], maps.at[t], sems.at[t]))
        copies[-1].start()

    repeat = jnp.where(
        lax.broadcasted_iota(jnp.int32, (channels, rows), 1) % channels
        == lax.broadcasted_iota(jnp.int32, (channels, rows), 0),
        1.0,
        0.0,
    ).astype(jnp.bfloat16)
    taps[...] = jnp.zeros_like(taps)
    for p in range(side):
        taps[p * 8 : p * 8 + side, :] = lax.dot_general(
            stencil_ref[:, p, :], repeat, (((0,), (0,)), ((), ())), preferred_element_type=jnp.float32
        )
    spread = jnp.where(
        lax.broadcasted_iota(jnp.int32, (slots, rows), 1) // channels
        == lax.broadcasted_iota(jnp.int32, (slots, rows), 0),
        1.0,
        0.0,
    ).astype(jnp.bfloat16)

    cell = lax.broadcasted_iota(jnp.int32, (8, cells), 1)
    width = cells // GH
    down = cell // width
    across = cell % width
    tap = lax.broadcasted_iota(jnp.int32, (8, cells), 0)
    column = across - tap + half
    column_inside = (column >= 0) & (column < width) & (tap < side)
    me = lax.axis_index("block")
    for t in range(steps):
        owner = lax.broadcasted_iota(jnp.int32, (8, slots), 0)
        slot = lax.broadcasted_iota(jnp.int32, (8, slots), 1)
        live = (observed_ref[t : t + 1, :] == owner) & (slot < active_ref[t, 0])
        weight = jnp.dot(
            jnp.where(live, 1.0, 0.0).astype(jnp.bfloat16), spread, preferred_element_type=jnp.float32
        )
        left = jnp.concatenate([taps[...] * weight[b : b + 1, :] for b in range(2)], axis=0)
        copies[t].wait()
        shifted = jnp.dot(left.astype(jnp.bfloat16), maps[t], preferred_element_type=jnp.float32)
        found = []
        for b in range(2):
            total = jnp.zeros((8, cells), jnp.float32)
            for p in range(side):
                at = (b * side + p) * 8
                part = pltpu.roll(shifted[at : at + 8, :], ((p - half) * width) % cells, 1)
                row = down - p + half
                total = total + jnp.where((row >= 0) & (row < GH), part, 0.0)
            sides = jnp.zeros((8, cells), jnp.float32)
            for q in range(side):
                part = pltpu.roll(total, (q - half) % cells, 1)
                sides = jnp.where(column_inside & (tap == q), part, sides)
            found.append(jnp.sum(sides, axis=0, keepdims=True))
        mine_ref[t : t + 1, :] = jnp.where(me == 0, found[0], found[1])
        theirs_ref[t : t + 1, :] = jnp.where(me == 0, found[1], found[0])


def sensor_info(scaled_residual_maps, measurement_stencil, observed_partition, active_probe_total):
    steps, slots, channels, cells = scaled_residual_maps.shape
    side = measurement_stencil.shape[1]
    mine, theirs = pl.pallas_call(
        info_kernel,
        out_shape=[jax.ShapeDtypeStruct((steps, cells), jnp.float32)] * 2,
        in_specs=[
            pl.BlockSpec(memory_space=pl.ANY),
            VMEM,
            VMEM,
            pl.BlockSpec(memory_space=pltpu.SMEM),
        ],
        out_specs=[VMEM] * 2,
        scratch_shapes=[
            pltpu.VMEM((steps, slots * channels, cells), jnp.bfloat16),
            pltpu.VMEM((side * 8, slots * channels), jnp.float32),
            pltpu.SemaphoreType.DMA((steps,)),
        ],
        compiler_params=PARAMS,
        name="sensor_info",
    )(
        scaled_residual_maps.reshape(steps, slots * channels, cells),
        measurement_stencil,
        observed_partition,
        active_probe_total,
    )
    return mine, lax.ppermute(theirs, "block", [(0, 1), (1, 0)])


def inputs_kernel(mine_ref, other_ref, covariance_ref, operator_ref, start_ref, inputs_ref, states_ref, send_ref):
    state = start_ref[...]
    for t in range(mine_ref.shape[0]):
        drive = times(covariance_ref[t], mine_ref[t : t + 1, :] + other_ref[t : t + 1, :])
        inputs_ref[t : t + 1, :] = drive
        state = times(operator_ref[t], state) + drive
        states_ref[t : t + 1, :] = state
    send_ref[...] = state


def hop_kernel(turn, reverse, came_ref, matrices_ref, offsets_ref, kept_ref, states_ref, send_ref):
    here = lax.axis_index("tm") == turn

    @pl.when(here)
    def _():
        state = came_ref[...]
        order = range(matrices_ref.shape[0])
        for t in reversed(order) if reverse else order:
            state = times(matrices_ref[t], state) + offsets_ref[t : t + 1, :]
            states_ref[t : t + 1, :] = state
        send_ref[...] = state

    @pl.when(jnp.logical_not(here))
    def _():
        states_ref[...] = kept_ref[...]
        send_ref[...] = came_ref[...]


def turn_kernel(last, means_ref, gain_ref, propagator_ref, offsets_ref, states_ref, send_ref):
    steps = means_ref.shape[0]
    for t in range(steps):
        moved = times(gain_ref[t], times(propagator_ref[...], means_ref[t : t + 1, :]))
        offsets_ref[t : t + 1, :] = means_ref[t : t + 1, :] - moved
    state = means_ref[steps - 1 : steps, :]
    states_ref[steps - 1 : steps, :] = state
    for t in reversed(range(steps - 1)):
        state = times(gain_ref[t], state) + offsets_ref[t : t + 1, :]
        states_ref[t : t + 1, :] = state
    send_ref[...] = state


def call(kernel, name, outs, *args):
    return pl.pallas_call(
        kernel,
        out_shape=[jax.ShapeDtypeStruct(shape, jnp.float32) for shape in outs],
        in_specs=[VMEM] * len(args),
        out_specs=[VMEM] * len(outs),
        compiler_params=PARAMS,
        name=name,
    )(*args)


def hop(row, source, target, places):
    pairs = []
    for core in range(2):
        pairs += [(source * 2 + core, target * 2 + core), (target * 2 + core, source * 2 + core)]
    for place in range(places):
        if place not in (source, target):
            pairs += [(place * 2, place * 2 + 1), (place * 2 + 1, place * 2)]
    return lax.ppermute(row, ("tm", "block"), pairs)


def local(
    scaled_residual_maps,
    measurement_stencil,
    observed_partition,
    active_probe_total,
    filtering_operator,
    updated_covariance,
    backward_factor,
    propagator,
    initial_mean,
):
    steps, size = filtering_operator.shape[0], filtering_operator.shape[-1]
    places = lax.axis_size("tm")
    many, one = (steps, size), (1, size)
    operator = filtering_operator.reshape(steps, size, size)
    covariance = updated_covariance.reshape(steps, size, size)
    gain = backward_factor.reshape(steps, size, size)
    mine, other = sensor_info(
        scaled_residual_maps, measurement_stencil, observed_partition, active_probe_total
    )
    inputs, means, send = call(
        inputs_kernel, "inputs", (many, many, one), mine, other, covariance, operator, initial_mean
    )
    for place in range(1, places):
        came = hop(send, place - 1, place, places)
        means, send = call(
            functools.partial(hop_kernel, place, False), "forward", (many, one), came, operator, inputs, means
        )
    offsets, states, send = call(
        functools.partial(turn_kernel, places - 1),
        "turn",
        (many, many, one),
        means,
        gain,
        propagator.reshape(size, size),
    )
    for place in reversed(range(places - 1)):
        came = hop(send, place + 1, place, places)
        states, send = call(
            functools.partial(hop_kernel, place, True), "backward", (many, one), came, gain, offsets, states
        )
    return (means.reshape(steps, 1, size), states.reshape(steps, 1, size))


def solution(mesh):
    placed = (
        P(("groups", "tm"), "block", None, None),
        P(),
        P(("groups", "tm"), "block"),
        P(("groups", "tm"), "block"),
        P(("groups", "tm"), "block", None, None),
        P(("groups", "tm"), "block", None, None),
        P(("groups", "tm"), "block", None, None),
        P("block", None, None),
        P(("groups", "block"), None),
    )
    return jax.shard_map(
        local,
        mesh=mesh,
        in_specs=placed,
        out_specs=(P(("groups", "tm"), "block", None), P(("groups", "tm"), "block", None)),
        check_vma=False,
    )
```

```python
import functools

import jax
import jax.numpy as jnp
from jax import lax
from jax.experimental import pallas as pl
from jax.experimental.pallas import tpu as pltpu
from jax.sharding import PartitionSpec as P

GH = 16
MAP_COPIES = 4
VMEM = pl.BlockSpec(memory_space=pltpu.VMEM)
PARAMS = pltpu.CompilerParams(vmem_limit_bytes=16 * 2**20)


def pieces(row, rows=8, count=3):
    at = lax.broadcasted_iota(jnp.int32, (rows, row.shape[1]), 0)
    block = jnp.zeros((rows, row.shape[1]), jnp.float32)
    rest = row
    for i in range(count):
        piece = rest.astype(jnp.bfloat16).astype(jnp.float32)
        block = jnp.where(at == i, piece, block)
        rest = rest - piece
    return block.astype(jnp.bfloat16)


def times(matrix, row):
    product = lax.dot_general(
        pieces(row), matrix, (((1,), (1,)), ((), ())), preferred_element_type=jnp.float32
    )
    return jnp.sum(product, axis=0, keepdims=True)


def info_kernel(
    maps_hbm,
    stencil_hbm,
    observed_hbm,
    active_hbm,
    mine_ref,
    theirs_ref,
    maps,
    stencil_ref,
    observed_ref,
    active_ref,
    taps,
    map_sems,
    sems,
):
    steps, rows, cells = maps.shape
    slots = observed_ref.shape[1]
    side, _, channels = stencil_ref.shape
    half = side // 2
    small = []
    for i, (source, target) in enumerate(
        ((stencil_hbm, stencil_ref), (observed_hbm, observed_ref), (active_hbm, active_ref))
    ):
        small.append(pltpu.make_async_copy(source, target, sems.at[i]))
        small[-1].start()
    part = rows // MAP_COPIES
    copies = []
    for t in range(steps):
        for i in range(MAP_COPIES):
            at = pl.ds(i * part, part)
            copies.append(
                pltpu.make_async_copy(maps_hbm.at[t, at], maps.at[t, at], map_sems.at[t, i])
            )
            copies[-1].start()

    repeat = jnp.where(
        lax.broadcasted_iota(jnp.int32, (channels, rows), 1) % channels
        == lax.broadcasted_iota(jnp.int32, (channels, rows), 0),
        1.0,
        0.0,
    ).astype(jnp.bfloat16)
    taps[...] = jnp.zeros_like(taps)
    spread = jnp.where(
        lax.broadcasted_iota(jnp.int32, (slots, rows), 1) // channels
        == lax.broadcasted_iota(jnp.int32, (slots, rows), 0),
        1.0,
        0.0,
    ).astype(jnp.bfloat16)

    cell = lax.broadcasted_iota(jnp.int32, (8, cells), 1)
    width = cells // GH
    down = cell // width
    across = cell % width
    tap = lax.broadcasted_iota(jnp.int32, (8, cells), 0)
    column = across - tap + half
    column_inside = (column >= 0) & (column < width) & (tap < side)
    me = lax.axis_index("block")
    for copy in small:
        copy.wait()
    for p in range(side):
        taps[p * 8 : p * 8 + side, :] = jnp.dot(
            stencil_ref[p], repeat, preferred_element_type=jnp.float32
        )
    for t in range(steps):
        owner = lax.broadcasted_iota(jnp.int32, (8, slots), 0)
        slot = lax.broadcasted_iota(jnp.int32, (8, slots), 1)
        live = (observed_ref[t : t + 1, :] == owner) & (slot < active_ref[0:1, t : t + 1])
        weight = jnp.dot(
            jnp.where(live, 1.0, 0.0).astype(jnp.bfloat16), spread, preferred_element_type=jnp.float32
        )
        left = jnp.concatenate([taps[...] * weight[b : b + 1, :] for b in range(2)], axis=0)
        for copy in copies[t * MAP_COPIES : (t + 1) * MAP_COPIES]:
            copy.wait()
        shifted = jnp.dot(left.astype(jnp.bfloat16), maps[t], preferred_element_type=jnp.float32)
        found = []
        for b in range(2):
            total = jnp.zeros((8, cells), jnp.float32)
            for p in range(side):
                at = (b * side + p) * 8
                part = pltpu.roll(shifted[at : at + 8, :], ((p - half) * width) % cells, 1)
                row = down - p + half
                total = total + jnp.where((row >= 0) & (row < GH), part, 0.0)
            sides = jnp.zeros((8, cells), jnp.float32)
            for q in range(side):
                part = pltpu.roll(total, (q - half) % cells, 1)
                sides = jnp.where(column_inside & (tap == q), part, sides)
            found.append(jnp.sum(sides, axis=0, keepdims=True))
        mine_ref[t : t + 1, :] = jnp.where(me == 0, found[0], found[1])
        theirs_ref[t : t + 1, :] = jnp.where(me == 0, found[1], found[0])


def sensor_info(scaled_residual_maps, measurement_stencil, observed_partition, active_probe_total):
    steps, slots, channels, cells = scaled_residual_maps.shape
    side = measurement_stencil.shape[1]
    mine, theirs = pl.pallas_call(
        info_kernel,
        out_shape=[jax.ShapeDtypeStruct((steps, cells), jnp.float32)] * 2,
        in_specs=[pl.BlockSpec(memory_space=pltpu.HBM)] * 4,
        out_specs=[VMEM] * 2,
        scratch_shapes=[
            pltpu.VMEM((steps, slots * channels, cells), jnp.bfloat16),
            pltpu.VMEM((side, side, channels), jnp.bfloat16),
            pltpu.VMEM((steps, slots), jnp.int32),
            pltpu.VMEM((1, steps), jnp.int32),
            pltpu.VMEM((side * 8, slots * channels), jnp.float32),
            pltpu.SemaphoreType.DMA((steps, MAP_COPIES)),
            pltpu.SemaphoreType.DMA((3,)),
        ],
        compiler_params=PARAMS,
        name="sensor_info",
    )(
        *(
            pltpu.with_memory_space_constraint(array, pltpu.HBM)
            for array in (
                scaled_residual_maps.reshape(steps, slots * channels, cells),
                measurement_stencil.transpose(1, 2, 0),
                observed_partition,
                active_probe_total.T,
            )
        )
    )
    return mine, lax.ppermute(theirs, "block", [(0, 1), (1, 0)])


def inputs_kernel(mine_ref, other_ref, covariance_ref, operator_ref, start_ref, inputs_ref, states_ref, send_ref):
    state = start_ref[...]
    for t in range(mine_ref.shape[0]):
        drive = times(covariance_ref[t], mine_ref[t : t + 1, :] + other_ref[t : t + 1, :])
        inputs_ref[t : t + 1, :] = drive
        state = times(operator_ref[t], state) + drive
        states_ref[t : t + 1, :] = state
    send_ref[...] = state


def hop_kernel(turn, reverse, came_ref, matrices_ref, offsets_ref, kept_ref, states_ref, send_ref):
    here = lax.axis_index("tm") == turn

    @pl.when(here)
    def _():
        state = came_ref[...]
        order = range(matrices_ref.shape[0])
        for t in reversed(order) if reverse else order:
            state = times(matrices_ref[t], state) + offsets_ref[t : t + 1, :]
            states_ref[t : t + 1, :] = state
        send_ref[...] = state

    @pl.when(jnp.logical_not(here))
    def _():
        states_ref[...] = kept_ref[...]
        send_ref[...] = came_ref[...]


def turn_kernel(last, means_ref, gain_ref, propagator_ref, offsets_ref, states_ref, send_ref):
    steps = means_ref.shape[0]
    for t in range(steps):
        moved = times(gain_ref[t], times(propagator_ref[...], means_ref[t : t + 1, :]))
        offsets_ref[t : t + 1, :] = means_ref[t : t + 1, :] - moved
    state = means_ref[steps - 1 : steps, :]
    states_ref[steps - 1 : steps, :] = state
    for t in reversed(range(steps - 1)):
        state = times(gain_ref[t], state) + offsets_ref[t : t + 1, :]
        states_ref[t : t + 1, :] = state
    send_ref[...] = state


def call(kernel, name, outs, *args):
    return pl.pallas_call(
        kernel,
        out_shape=[jax.ShapeDtypeStruct(shape, jnp.float32) for shape in outs],
        in_specs=[VMEM] * len(args),
        out_specs=[VMEM] * len(outs),
        compiler_params=PARAMS,
        name=name,
    )(*args)


def hop(row, source, target, places):
    pairs = []
    for core in range(2):
        pairs += [(source * 2 + core, target * 2 + core), (target * 2 + core, source * 2 + core)]
    for place in range(places):
        if place not in (source, target):
            pairs += [(place * 2, place * 2 + 1), (place * 2 + 1, place * 2)]
    return lax.ppermute(row, ("tm", "block"), pairs)


def local(
    scaled_residual_maps,
    measurement_stencil,
    observed_partition,
    active_probe_total,
    filtering_operator,
    updated_covariance,
    backward_factor,
    propagator,
    initial_mean,
):
    steps, size = filtering_operator.shape[0], filtering_operator.shape[-1]
    places = lax.axis_size("tm")
    many, one = (steps, size), (1, size)
    operator = filtering_operator.reshape(steps, size, size)
    covariance = updated_covariance.reshape(steps, size, size)
    gain = backward_factor.reshape(steps, size, size)
    mine, other = sensor_info(
        scaled_residual_maps, measurement_stencil, observed_partition, active_probe_total
    )
    inputs, means, send = call(
        inputs_kernel, "inputs", (many, many, one), mine, other, covariance, operator, initial_mean
    )
    for place in range(1, places):
        came = hop(send, place - 1, place, places)
        means, send = call(
            functools.partial(hop_kernel, place, False), "forward", (many, one), came, operator, inputs, means
        )
    offsets, states, send = call(
        functools.partial(turn_kernel, places - 1),
        "turn",
        (many, many, one),
        means,
        gain,
        propagator.reshape(size, size),
    )
    for place in reversed(range(places - 1)):
        came = hop(send, place + 1, place, places)
        states, send = call(
            functools.partial(hop_kernel, place, True), "backward", (many, one), came, gain, offsets, states
        )
    return (means.reshape(steps, 1, size), states.reshape(steps, 1, size))


def solution(mesh):
    placed = (
        P(("groups", "tm"), "block", None, None),
        P(),
        P(("groups", "tm"), "block"),
        P(("groups", "tm"), "block"),
        P(("groups", "tm"), "block", None, None),
        P(("groups", "tm"), "block", None, None),
        P(("groups", "tm"), "block", None, None),
        P("block", None, None),
        P(("groups", "block"), None),
    )
    return jax.shard_map(
        local,
        mesh=mesh,
        in_specs=placed,
        out_specs=(P(("groups", "tm"), "block", None), P(("groups", "tm"), "block", None)),
        check_vma=False,
    )
```

```python
import functools

import jax
import jax.numpy as jnp
from jax import lax
from jax.experimental import pallas as pl
from jax.experimental.pallas import tpu as pltpu
from jax.sharding import PartitionSpec as P

GH = 16
MAP_COPIES = 4
VMEM = pl.BlockSpec(memory_space=pltpu.VMEM)
PARAMS = pltpu.CompilerParams(vmem_limit_bytes=16 * 2**20)


def pieces(row, rows=8, count=3):
    at = lax.broadcasted_iota(jnp.int32, (rows, row.shape[1]), 0)
    block = jnp.zeros((rows, row.shape[1]), jnp.float32)
    rest = row
    for i in range(count):
        piece = rest.astype(jnp.bfloat16).astype(jnp.float32)
        block = jnp.where(at == i, piece, block)
        rest = rest - piece
    return block.astype(jnp.bfloat16)


def times(matrix, row):
    product = lax.dot_general(
        pieces(row), matrix, (((1,), (1,)), ((), ())), preferred_element_type=jnp.float32
    )
    return jnp.sum(product, axis=0, keepdims=True)


def info_kernel(
    maps_hbm,
    stencil_hbm,
    observed_hbm,
    active_hbm,
    mine_ref,
    theirs_ref,
    maps,
    stencil_ref,
    observed_ref,
    active_ref,
    taps,
    map_sems,
    sems,
):
    steps, rows, cells = maps.shape
    slots = observed_ref.shape[1]
    side, _, channels = stencil_ref.shape
    half = side // 2
    small = []
    for i, (source, target) in enumerate(
        ((stencil_hbm, stencil_ref), (observed_hbm, observed_ref), (active_hbm, active_ref))
    ):
        small.append(pltpu.make_async_copy(source, target, sems.at[i]))
        small[-1].start()
    part = rows // MAP_COPIES
    copies = []
    for t in range(steps):
        for i in range(MAP_COPIES):
            at = pl.ds(i * part, part)
            copies.append(
                pltpu.make_async_copy(maps_hbm.at[t, at], maps.at[t, at], map_sems.at[t, i])
            )
            copies[-1].start()

    repeat = jnp.where(
        lax.broadcasted_iota(jnp.int32, (channels, rows), 1) % channels
        == lax.broadcasted_iota(jnp.int32, (channels, rows), 0),
        1.0,
        0.0,
    ).astype(jnp.bfloat16)
    taps[...] = jnp.zeros_like(taps)
    spread = jnp.where(
        lax.broadcasted_iota(jnp.int32, (slots, rows), 1) // channels
        == lax.broadcasted_iota(jnp.int32, (slots, rows), 0),
        1.0,
        0.0,
    ).astype(jnp.bfloat16)

    cell = lax.broadcasted_iota(jnp.int32, (8, cells), 1)
    width = cells // GH
    down = cell // width
    across = cell % width
    tap = lax.broadcasted_iota(jnp.int32, (8, cells), 0)
    column = across - tap + half
    column_inside = (column >= 0) & (column < width) & (tap < side)
    me = lax.axis_index("block")
    for copy in small:
        copy.wait()
    for p in range(side):
        taps[p * 8 : p * 8 + side, :] = jnp.dot(
            stencil_ref[p], repeat, preferred_element_type=jnp.float32
        )
    for t in range(steps):
        owner = lax.broadcasted_iota(jnp.int32, (8, slots), 0)
        slot = lax.broadcasted_iota(jnp.int32, (8, slots), 1)
        live = (observed_ref[t : t + 1, :] == owner) & (slot < active_ref[0:1, t : t + 1])
        weight = jnp.dot(
            jnp.where(live, 1.0, 0.0).astype(jnp.bfloat16), spread, preferred_element_type=jnp.float32
        )
        left = jnp.concatenate([taps[...] * weight[b : b + 1, :] for b in range(2)], axis=0)
        for copy in copies[t * MAP_COPIES : (t + 1) * MAP_COPIES]:
            copy.wait()
        shifted = jnp.dot(left.astype(jnp.bfloat16), maps[t], preferred_element_type=jnp.float32)
        found = []
        for b in range(2):
            total = jnp.zeros((8, cells), jnp.float32)
            for p in range(side):
                at = (b * side + p) * 8
                part = pltpu.roll(shifted[at : at + 8, :], ((p - half) * width) % cells, 1)
                row = down - p + half
                total = total + jnp.where((row >= 0) & (row < GH), part, 0.0)
            sides = jnp.zeros((8, cells), jnp.float32)
            for q in range(side):
                part = pltpu.roll(total, (q - half) % cells, 1)
                sides = jnp.where(column_inside & (tap == q), part, sides)
            found.append(jnp.sum(sides, axis=0, keepdims=True))
        mine_ref[t : t + 1, :] = jnp.where(me == 0, found[0], found[1])
        theirs_ref[t : t + 1, :] = jnp.where(me == 0, found[1], found[0])


def sensor_info(scaled_residual_maps, measurement_stencil, observed_partition, active_probe_total):
    steps, slots, channels, cells = scaled_residual_maps.shape
    side = measurement_stencil.shape[1]
    mine, theirs = pl.pallas_call(
        info_kernel,
        out_shape=[jax.ShapeDtypeStruct((steps, cells), jnp.float32)] * 2,
        in_specs=[pl.BlockSpec(memory_space=pltpu.HBM)] * 4,
        out_specs=[VMEM] * 2,
        scratch_shapes=[
            pltpu.VMEM((steps, slots * channels, cells), jnp.bfloat16),
            pltpu.VMEM((side, side, channels), jnp.bfloat16),
            pltpu.VMEM((steps, slots), jnp.int32),
            pltpu.VMEM((1, steps), jnp.int32),
            pltpu.VMEM((side * 8, slots * channels), jnp.float32),
            pltpu.SemaphoreType.DMA((steps, MAP_COPIES)),
            pltpu.SemaphoreType.DMA((3,)),
        ],
        compiler_params=PARAMS,
        name="sensor_info",
    )(
        *(
            pltpu.with_memory_space_constraint(array, pltpu.HBM)
            for array in (
                scaled_residual_maps.reshape(steps, slots * channels, cells),
                measurement_stencil.transpose(1, 2, 0),
                observed_partition,
                active_probe_total.T,
            )
        )
    )
    return mine, lax.ppermute(theirs, "block", [(0, 1), (1, 0)])


def inputs_kernel(mine_ref, other_ref, covariance_ref, operator_ref, start_ref, inputs_ref, states_ref, send_ref):
    state = start_ref[...]
    for t in range(mine_ref.shape[0]):
        drive = times(covariance_ref[t], mine_ref[t : t + 1, :] + other_ref[t : t + 1, :])
        inputs_ref[t : t + 1, :] = drive
        state = times(operator_ref[t], state) + drive
        states_ref[t : t + 1, :] = state
    send_ref[...] = state


def hop_kernel(turn, came_ref, matrices_ref, offsets_ref, kept_ref, states_ref, send_ref):
    here = lax.axis_index("tm") == turn

    @pl.when(here)
    def _():
        state = came_ref[...]
        for t in range(matrices_ref.shape[0]):
            state = times(matrices_ref[t], state) + offsets_ref[t : t + 1, :]
            states_ref[t : t + 1, :] = state
        send_ref[...] = state

    @pl.when(jnp.logical_not(here))
    def _():
        states_ref[...] = kept_ref[...]
        send_ref[...] = came_ref[...]


def compose_kernel(after_ref, gain_ref, composed_ref):
    del after_ref
    steps = gain_ref.shape[0]
    product = gain_ref[0].astype(jnp.float32)
    for t in range(1, steps):
        product = sum(
            jnp.dot(part, gain_ref[t], preferred_element_type=jnp.float32)
            for part in (halves(product) if t > 1 else [gain_ref[0]])
        )
    composed_ref[...] = product


def halves(matrix):
    high = matrix.astype(jnp.bfloat16)
    return [high, (matrix - high.astype(jnp.float32)).astype(jnp.bfloat16)]


def split_kernel(near_ref, far_ref, near_parts_ref, far_parts_ref):
    for source, target in ((near_ref, near_parts_ref), (far_ref, far_parts_ref)):
        target[0], target[1] = halves(source[...])


def times_parts(parts_ref, row):
    block = pieces(row)
    product = sum(
        lax.dot_general(block, parts_ref[i], (((1,), (1,)), ((), ())), preferred_element_type=jnp.float32)
        for i in range(2)
    )
    return jnp.sum(product, axis=0, keepdims=True)


def turn_kernel(last, means_ref, gain_ref, propagator_ref, offsets_ref, states_ref, send_ref):
    steps = means_ref.shape[0]
    for t in range(steps):
        moved = times(gain_ref[t], times(propagator_ref[...], means_ref[t : t + 1, :]))
        offsets_ref[t : t + 1, :] = means_ref[t : t + 1, :] - moved
    end = slice(steps - 1, steps)
    state = jnp.where(lax.axis_index("tm") == last, means_ref[end, :], offsets_ref[end, :])
    states_ref[end, :] = state
    for t in reversed(range(steps - 1)):
        state = times(gain_ref[t], state) + offsets_ref[t : t + 1, :]
        states_ref[t : t + 1, :] = state
    send_ref[...] = state


def smooth(state, gain_ref, offsets_ref, states_ref, send_ref):
    for t in reversed(range(gain_ref.shape[0])):
        state = times(gain_ref[t], state) + offsets_ref[t : t + 1, :]
        states_ref[t : t + 1, :] = state
    send_ref[...] = state


def first_back_kernel(
    places, last_ref, far_ref, near_ref, far_parts_ref, near_parts_ref, gain_ref, offsets_ref, kept_ref,
    states_ref, send_ref,
):
    here = lax.axis_index("tm")

    @pl.when(here == places - 4)
    def _():
        state = times_parts(far_parts_ref, last_ref[...]) + far_ref[...]
        state = times_parts(near_parts_ref, state) + near_ref[...]
        smooth(state, gain_ref, offsets_ref, states_ref, send_ref)

    @pl.when(here == places - 2)
    def _():
        smooth(near_ref[...], gain_ref, offsets_ref, states_ref, send_ref)

    @pl.when((here != places - 4) & (here != places - 2))
    def _():
        states_ref[...] = kept_ref[...]
        send_ref[...] = near_ref[...]


def back_kernel(
    target, stray, two_ref, one_ref, near_ref, near_parts_ref, gain_ref, offsets_ref, kept_ref,
    states_ref, send_ref,
):
    here = lax.axis_index("tm")

    @pl.when(here == target)
    def _():
        state = times_parts(near_parts_ref, two_ref[...]) + near_ref[...]
        smooth(state, gain_ref, offsets_ref, states_ref, send_ref)

    @pl.when(here == target + 1)
    def _():
        smooth(one_ref[...], gain_ref, offsets_ref, states_ref, send_ref)

    @pl.when(here == stray)
    def _():
        smooth(two_ref[...], gain_ref, offsets_ref, states_ref, send_ref)

    @pl.when((here != target) & (here != target + 1) & (here != stray))
    def _():
        states_ref[...] = kept_ref[...]
        send_ref[...] = two_ref[...]


def call(kernel, name, outs, *args):
    return pl.pallas_call(
        kernel,
        out_shape=[jax.ShapeDtypeStruct(shape, jnp.float32) for shape in outs],
        in_specs=[VMEM] * len(args),
        out_specs=[VMEM] * len(outs),
        compiler_params=PARAMS,
        name=name,
    )(*args)


def swap(row, pairs, places):
    route = {}
    for place in range(places):
        for core in range(2):
            route[place * 2 + core] = place * 2 + 1 - core
    for one, two in pairs:
        for core in range(2):
            route[one * 2 + core] = two * 2 + core
            route[two * 2 + core] = one * 2 + core
    return lax.ppermute(row, ("tm", "block"), sorted(route.items()))


def local(
    scaled_residual_maps,
    measurement_stencil,
    observed_partition,
    active_probe_total,
    filtering_operator,
    updated_covariance,
    backward_factor,
    propagator,
    initial_mean,
):
    steps, size = filtering_operator.shape[0], filtering_operator.shape[-1]
    places = lax.axis_size("tm")
    many, one = (steps, size), (1, size)
    operator = filtering_operator.reshape(steps, size, size)
    covariance = updated_covariance.reshape(steps, size, size)
    gain = backward_factor.reshape(steps, size, size)
    mine, other = sensor_info(
        scaled_residual_maps, measurement_stencil, observed_partition, active_probe_total
    )
    inputs, means, send = call(
        inputs_kernel, "inputs", (many, many, one), mine, other, covariance, operator, initial_mean
    )
    composed = call(compose_kernel, "compose", ((size, size),), mine, gain)[0]
    near = lax.ppermute(composed, "tm", [(place + 1, place) for place in range(0, places, 2)])
    far = lax.ppermute(composed, "tm", [(places - 2, places - 4)])
    for place in range(1, places):
        came = swap(send, [(place - 1, place)], places)
        means, send = call(
            functools.partial(hop_kernel, place), "forward", (many, one), came, operator, inputs, means
        )
    offsets, states, send = call(
        functools.partial(turn_kernel, places - 1),
        "turn",
        (many, many, one),
        means,
        gain,
        propagator.reshape(size, size),
    )
    last = swap(send, [(places - 1, places - 4)], places)
    far_offset = swap(send, [(places - 2, places - 4)], places)
    near_offset = swap(send, [(place, place + 1) for place in range(0, places, 2)], places)
    near_parts, far_parts = pl.pallas_call(
        split_kernel,
        out_shape=[jax.ShapeDtypeStruct((2, size, size), jnp.bfloat16)] * 2,
        in_specs=[VMEM] * 2,
        out_specs=[VMEM] * 2,
        compiler_params=PARAMS,
        name="split",
    )(near, far)
    states, send = call(
        functools.partial(first_back_kernel, places),
        "first_back",
        (many, (1, size)),
        last,
        far_offset,
        near_offset,
        far_parts,
        near_parts,
        gain,
        offsets,
        states,
    )
    for target in range(places - 6, -1, -2):
        stray = places - 3 if target == places - 6 else -1
        two = swap(send, [(target + 2, target)] + ([(stray + 1, stray)] if stray >= 0 else []), places)
        one = swap(send, [(target + 2, target + 1)], places)
        states, send = call(
            functools.partial(back_kernel, target, stray),
            "back",
            (many, (1, size)),
            two,
            one,
            near_offset,
            near_parts,
            gain,
            offsets,
            states,
        )
    return (means.reshape(steps, 1, size), states.reshape(steps, 1, size))


def solution(mesh):
    placed = (
        P(("groups", "tm"), "block", None, None),
        P(),
        P(("groups", "tm"), "block"),
        P(("groups", "tm"), "block"),
        P(("groups", "tm"), "block", None, None),
        P(("groups", "tm"), "block", None, None),
        P(("groups", "tm"), "block", None, None),
        P("block", None, None),
        P(("groups", "block"), None),
    )
    return jax.shard_map(
        local,
        mesh=mesh,
        in_specs=placed,
        out_specs=(P(("groups", "tm"), "block", None), P(("groups", "tm"), "block", None)),
        check_vma=False,
    )
```

```python
import functools

import jax
import jax.numpy as jnp
from jax import lax
from jax.experimental import pallas as pl
from jax.experimental.pallas import tpu as pltpu
from jax.sharding import PartitionSpec as P

GH = 16
MAP_COPIES = 4
VMEM = pl.BlockSpec(memory_space=pltpu.VMEM)
PARAMS = pltpu.CompilerParams(vmem_limit_bytes=16 * 2**20)


def pieces(row, rows=8, count=3):
    at = lax.broadcasted_iota(jnp.int32, (rows, row.shape[1]), 0)
    block = jnp.zeros((rows, row.shape[1]), jnp.float32)
    rest = row
    for i in range(count):
        piece = rest.astype(jnp.bfloat16).astype(jnp.float32)
        block = jnp.where(at == i, piece, block)
        rest = rest - piece
    return block.astype(jnp.bfloat16)


def times(matrix, row):
    product = lax.dot_general(
        pieces(row), matrix, (((1,), (1,)), ((), ())), preferred_element_type=jnp.float32
    )
    return jnp.sum(product, axis=0, keepdims=True)


def info_kernel(
    maps_hbm,
    stencil_hbm,
    observed_hbm,
    active_hbm,
    mine_ref,
    theirs_ref,
    maps,
    stencil_ref,
    observed_ref,
    active_ref,
    taps,
    map_sems,
    sems,
):
    steps, rows, cells = maps.shape
    slots = observed_ref.shape[1]
    side, _, channels = stencil_ref.shape
    half = side // 2
    small = []
    for i, (source, target) in enumerate(
        ((stencil_hbm, stencil_ref), (observed_hbm, observed_ref), (active_hbm, active_ref))
    ):
        small.append(pltpu.make_async_copy(source, target, sems.at[i]))
        small[-1].start()
    part = rows // MAP_COPIES
    copies = []
    for t in range(steps):
        for i in range(MAP_COPIES):
            at = pl.ds(i * part, part)
            copies.append(
                pltpu.make_async_copy(maps_hbm.at[t, at], maps.at[t, at], map_sems.at[t, i])
            )
            copies[-1].start()

    repeat = jnp.where(
        lax.broadcasted_iota(jnp.int32, (channels, rows), 1) % channels
        == lax.broadcasted_iota(jnp.int32, (channels, rows), 0),
        1.0,
        0.0,
    ).astype(jnp.bfloat16)
    taps[...] = jnp.zeros_like(taps)
    spread = jnp.where(
        lax.broadcasted_iota(jnp.int32, (slots, rows), 1) // channels
        == lax.broadcasted_iota(jnp.int32, (slots, rows), 0),
        1.0,
        0.0,
    ).astype(jnp.bfloat16)

    cell = lax.broadcasted_iota(jnp.int32, (8, cells), 1)
    width = cells // GH
    down = cell // width
    across = cell % width
    tap = lax.broadcasted_iota(jnp.int32, (8, cells), 0)
    column = across - tap + half
    column_inside = (column >= 0) & (column < width) & (tap < side)
    me = lax.axis_index("block")
    for copy in small:
        copy.wait()
    for p in range(side):
        taps[p * 8 : p * 8 + side, :] = jnp.dot(
            stencil_ref[p], repeat, preferred_element_type=jnp.float32
        )
    for t in range(steps):
        owner = lax.broadcasted_iota(jnp.int32, (8, slots), 0)
        slot = lax.broadcasted_iota(jnp.int32, (8, slots), 1)
        live = (observed_ref[t : t + 1, :] == owner) & (slot < active_ref[0:1, t : t + 1])
        weight = jnp.dot(
            jnp.where(live, 1.0, 0.0).astype(jnp.bfloat16), spread, preferred_element_type=jnp.float32
        )
        left = jnp.concatenate([taps[...] * weight[b : b + 1, :] for b in range(2)], axis=0)
        for copy in copies[t * MAP_COPIES : (t + 1) * MAP_COPIES]:
            copy.wait()
        shifted = jnp.dot(left.astype(jnp.bfloat16), maps[t], preferred_element_type=jnp.float32)
        found = []
        for b in range(2):
            total = jnp.zeros((8, cells), jnp.float32)
            for p in range(side):
                at = (b * side + p) * 8
                part = pltpu.roll(shifted[at : at + 8, :], ((p - half) * width) % cells, 1)
                row = down - p + half
                total = total + jnp.where((row >= 0) & (row < GH), part, 0.0)
            sides = jnp.zeros((8, cells), jnp.float32)
            for q in range(side):
                part = pltpu.roll(total, (q - half) % cells, 1)
                sides = jnp.where(column_inside & (tap == q), part, sides)
            found.append(jnp.sum(sides, axis=0, keepdims=True))
        mine_ref[t : t + 1, :] = jnp.where(me == 0, found[0], found[1])
        theirs_ref[t : t + 1, :] = jnp.where(me == 0, found[1], found[0])


def sensor_info(scaled_residual_maps, measurement_stencil, observed_partition, active_probe_total):
    steps, slots, channels, cells = scaled_residual_maps.shape
    side = measurement_stencil.shape[1]
    mine, theirs = pl.pallas_call(
        info_kernel,
        out_shape=[jax.ShapeDtypeStruct((steps, cells), jnp.float32)] * 2,
        in_specs=[pl.BlockSpec(memory_space=pltpu.HBM)] * 4,
        out_specs=[VMEM] * 2,
        scratch_shapes=[
            pltpu.VMEM((steps, slots * channels, cells), jnp.bfloat16),
            pltpu.VMEM((side, side, channels), jnp.bfloat16),
            pltpu.VMEM((steps, slots), jnp.int32),
            pltpu.VMEM((1, steps), jnp.int32),
            pltpu.VMEM((side * 8, slots * channels), jnp.float32),
            pltpu.SemaphoreType.DMA((steps, MAP_COPIES)),
            pltpu.SemaphoreType.DMA((3,)),
        ],
        compiler_params=PARAMS,
        name="sensor_info",
    )(
        *(
            pltpu.with_memory_space_constraint(array, pltpu.HBM)
            for array in (
                scaled_residual_maps.reshape(steps, slots * channels, cells),
                measurement_stencil.transpose(1, 2, 0),
                observed_partition,
                active_probe_total.T,
            )
        )
    )
    return mine, lax.ppermute(theirs, "block", [(0, 1), (1, 0)])


def inputs_kernel(mine_ref, other_ref, covariance_ref, operator_ref, start_ref, inputs_ref, states_ref, send_ref):
    state = start_ref[...]
    for t in range(mine_ref.shape[0]):
        drive = times(covariance_ref[t], mine_ref[t : t + 1, :] + other_ref[t : t + 1, :])
        inputs_ref[t : t + 1, :] = drive
        state = times(operator_ref[t], state) + drive
        states_ref[t : t + 1, :] = state
    send_ref[...] = state


def hop_kernel(turn, came_ref, matrices_ref, offsets_ref, kept_ref, states_ref, send_ref):
    here = lax.axis_index("tm") == turn

    @pl.when(here)
    def _():
        state = came_ref[...]
        for t in range(matrices_ref.shape[0]):
            state = times(matrices_ref[t], state) + offsets_ref[t : t + 1, :]
            states_ref[t : t + 1, :] = state
        send_ref[...] = state

    @pl.when(jnp.logical_not(here))
    def _():
        states_ref[...] = kept_ref[...]
        send_ref[...] = came_ref[...]


def compose_kernel(after_ref, gain_ref, composed_ref):
    del after_ref
    steps = gain_ref.shape[0]
    product = gain_ref[0].astype(jnp.float32)
    for t in range(1, steps):
        product = sum(
            jnp.dot(part, gain_ref[t], preferred_element_type=jnp.float32)
            for part in (halves(product) if t > 1 else [gain_ref[0]])
        )
    composed_ref[...] = product


def halves(matrix):
    high = matrix.astype(jnp.bfloat16)
    return [high, (matrix - high.astype(jnp.float32)).astype(jnp.bfloat16)]


def split_kernel(near_ref, far_ref, near_parts_ref, far_parts_ref):
    for source, target in ((near_ref, near_parts_ref), (far_ref, far_parts_ref)):
        target[0], target[1] = halves(source[...])


def times_parts(parts_ref, row):
    block = pieces(row)
    product = sum(
        lax.dot_general(block, parts_ref[i], (((1,), (1,)), ((), ())), preferred_element_type=jnp.float32)
        for i in range(2)
    )
    return jnp.sum(product, axis=0, keepdims=True)


def turn_kernel(last, means_ref, gain_ref, propagator_ref, offsets_ref, states_ref, send_ref):
    steps = means_ref.shape[0]
    for t in range(steps):
        moved = times(gain_ref[t], times(propagator_ref[...], means_ref[t : t + 1, :]))
        offsets_ref[t : t + 1, :] = means_ref[t : t + 1, :] - moved
    end = slice(steps - 1, steps)
    state = jnp.where(lax.axis_index("tm") == last, means_ref[end, :], offsets_ref[end, :])
    states_ref[end, :] = state
    for t in reversed(range(steps - 1)):
        state = times(gain_ref[t], state) + offsets_ref[t : t + 1, :]
        states_ref[t : t + 1, :] = state
    send_ref[...] = state


def smooth(state, gain_ref, offsets_ref, states_ref, send_ref):
    for t in reversed(range(gain_ref.shape[0])):
        state = times(gain_ref[t], state) + offsets_ref[t : t + 1, :]
        states_ref[t : t + 1, :] = state
    send_ref[...] = state


def first_back_kernel(
    places, last_ref, far_ref, near_ref, far_parts_ref, near_parts_ref, gain_ref, offsets_ref, kept_ref,
    states_ref, send_ref,
):
    here = lax.axis_index("tm")

    @pl.when(here == places - 4)
    def _():
        state = times_parts(far_parts_ref, last_ref[...]) + far_ref[...]
        state = times_parts(near_parts_ref, state) + near_ref[...]
        smooth(state, gain_ref, offsets_ref, states_ref, send_ref)

    @pl.when(here == places - 2)
    def _():
        smooth(near_ref[...], gain_ref, offsets_ref, states_ref, send_ref)

    @pl.when((here != places - 4) & (here != places - 2))
    def _():
        states_ref[...] = kept_ref[...]
        send_ref[...] = near_ref[...]


def back_kernel(
    target, stray, two_ref, one_ref, near_ref, near_parts_ref, gain_ref, offsets_ref, kept_ref,
    states_ref, send_ref,
):
    here = lax.axis_index("tm")

    @pl.when(here == target)
    def _():
        state = times_parts(near_parts_ref, two_ref[...]) + near_ref[...]
        smooth(state, gain_ref, offsets_ref, states_ref, send_ref)

    @pl.when(here == target + 1)
    def _():
        smooth(one_ref[...], gain_ref, offsets_ref, states_ref, send_ref)

    @pl.when(here == stray)
    def _():
        smooth(two_ref[...], gain_ref, offsets_ref, states_ref, send_ref)

    @pl.when((here != target) & (here != target + 1) & (here != stray))
    def _():
        states_ref[...] = kept_ref[...]
        send_ref[...] = two_ref[...]


def call(kernel, name, outs, *args):
    return pl.pallas_call(
        kernel,
        out_shape=[jax.ShapeDtypeStruct(shape, jnp.float32) for shape in outs],
        in_specs=[VMEM] * len(args),
        out_specs=[VMEM] * len(outs),
        compiler_params=PARAMS,
        name=name,
    )(*args)


def pass_row(row, rings, places):
    route = {}
    for place in range(places):
        for core in range(2):
            route[place * 2 + core] = place * 2 + 1 - core
    for ring in rings:
        for i, place in enumerate(ring):
            for core in range(2):
                route[place * 2 + core] = ring[(i + 1) % len(ring)] * 2 + core
    return lax.ppermute(row, ("tm", "block"), sorted(route.items()))


def ring_up(place, places):
    if place % 2 or place == places - 2:
        return (place, place + 1)
    return (place, place + 1, place - 2 if place else 2)


def local(
    scaled_residual_maps,
    measurement_stencil,
    observed_partition,
    active_probe_total,
    filtering_operator,
    updated_covariance,
    backward_factor,
    propagator,
    initial_mean,
):
    steps, size = filtering_operator.shape[0], filtering_operator.shape[-1]
    places = lax.axis_size("tm")
    many, one = (steps, size), (1, size)
    operator = filtering_operator.reshape(steps, size, size)
    covariance = updated_covariance.reshape(steps, size, size)
    gain = backward_factor.reshape(steps, size, size)
    mine, other = sensor_info(
        scaled_residual_maps, measurement_stencil, observed_partition, active_probe_total
    )
    inputs, means, send = call(
        inputs_kernel, "inputs", (many, many, one), mine, other, covariance, operator, initial_mean
    )
    composed = call(compose_kernel, "compose", ((size, size),), send, gain)[0]
    near = lax.ppermute(composed, "tm", [(place + 1, place) for place in range(0, places - 2, 2)])
    far = lax.ppermute(composed, "tm", [(places - 2, places - 4)])
    for place in range(1, places):
        came = pass_row(send, [ring_up(place - 1, places)], places)
        means, send = call(
            functools.partial(hop_kernel, place), "forward", (many, one), came, operator, inputs, means
        )
    offsets, states, send = call(
        functools.partial(turn_kernel, places - 1),
        "turn",
        (many, many, one),
        means,
        gain,
        propagator.reshape(size, size),
    )
    last = pass_row(send, [(places - 1, places - 4)], places)
    far_offset = pass_row(send, [(places - 2, places - 4)], places)
    near_offset = pass_row(send, [(place, place + 1) for place in range(0, places, 2)], places)
    near_parts, far_parts = pl.pallas_call(
        split_kernel,
        out_shape=[jax.ShapeDtypeStruct((2, size, size), jnp.bfloat16)] * 2,
        in_specs=[VMEM] * 2,
        out_specs=[VMEM] * 2,
        compiler_params=PARAMS,
        name="split",
    )(near, far)
    states, send = call(
        functools.partial(first_back_kernel, places),
        "first_back",
        (many, (1, size)),
        last,
        far_offset,
        near_offset,
        far_parts,
        near_parts,
        gain,
        offsets,
        states,
    )
    for target in range(places - 6, -1, -2):
        stray = places - 3 if target == places - 6 else -1
        two = pass_row(send, [(target + 2, target)] + ([(stray + 1, stray)] if stray >= 0 else []), places)
        one = pass_row(send, [(target + 2, target + 1)], places)
        states, send = call(
            functools.partial(back_kernel, target, stray),
            "back",
            (many, (1, size)),
            two,
            one,
            near_offset,
            near_parts,
            gain,
            offsets,
            states,
        )
    return (means.reshape(steps, 1, size), states.reshape(steps, 1, size))


def solution(mesh):
    placed = (
        P(("groups", "tm"), "block", None, None),
        P(),
        P(("groups", "tm"), "block"),
        P(("groups", "tm"), "block"),
        P(("groups", "tm"), "block", None, None),
        P(("groups", "tm"), "block", None, None),
        P(("groups", "tm"), "block", None, None),
        P("block", None, None),
        P(("groups", "block"), None),
    )
    return jax.shard_map(
        local,
        mesh=mesh,
        in_specs=placed,
        out_specs=(P(("groups", "tm"), "block", None), P(("groups", "tm"), "block", None)),
        check_vma=False,
    )
```

```python
import functools

import jax
import jax.numpy as jnp
from jax import lax
from jax.experimental import pallas as pl
from jax.experimental.pallas import tpu as pltpu
from jax.sharding import PartitionSpec as P

GH = 16
MAP_COPIES = 4
MATRIX_COST = 60.0
VMEM = pl.BlockSpec(memory_space=pltpu.VMEM)
PARAMS = pltpu.CompilerParams(vmem_limit_bytes=16 * 2**20)


def pieces(rows, count=3):
    height = -(-len(rows) * count // 8) * 8
    at = lax.broadcasted_iota(jnp.int32, (height, rows[0].shape[1]), 0)
    block = jnp.zeros(at.shape, jnp.float32)
    for k, rest in enumerate(rows):
        for i in range(count):
            piece = rest.astype(jnp.bfloat16).astype(jnp.float32)
            block = jnp.where(at == k * count + i, piece, block)
            rest = rest - piece
    return block.astype(jnp.bfloat16)


def times(matrices, *rows):
    block = pieces(rows)
    product = sum(
        lax.dot_general(block, matrix, (((1,), (1,)), ((), ())), preferred_element_type=jnp.float32)
        for matrix in matrices
    )
    found = [jnp.sum(product[3 * k : 3 * k + 3, :], axis=0, keepdims=True) for k in range(len(rows))]
    return found if len(rows) > 1 else found[0]


def info_kernel(
    maps_hbm,
    stencil_hbm,
    observed_hbm,
    active_hbm,
    mine_ref,
    theirs_ref,
    maps,
    stencil_ref,
    observed_ref,
    active_ref,
    taps,
    map_sems,
    sems,
):
    steps, rows, cells = maps.shape
    slots = observed_ref.shape[1]
    side, _, channels = stencil_ref.shape
    half = side // 2
    small = []
    for i, (source, target) in enumerate(
        ((stencil_hbm, stencil_ref), (observed_hbm, observed_ref), (active_hbm, active_ref))
    ):
        small.append(pltpu.make_async_copy(source, target, sems.at[i]))
        small[-1].start()
    part = rows // MAP_COPIES
    copies = []
    for t in range(steps):
        for i in range(MAP_COPIES):
            at = pl.ds(i * part, part)
            copies.append(
                pltpu.make_async_copy(maps_hbm.at[t, at], maps.at[t, at], map_sems.at[t, i])
            )
            copies[-1].start()

    repeat = jnp.where(
        lax.broadcasted_iota(jnp.int32, (channels, rows), 1) % channels
        == lax.broadcasted_iota(jnp.int32, (channels, rows), 0),
        1.0,
        0.0,
    ).astype(jnp.bfloat16)
    taps[...] = jnp.zeros_like(taps)
    spread = jnp.where(
        lax.broadcasted_iota(jnp.int32, (slots, rows), 1) // channels
        == lax.broadcasted_iota(jnp.int32, (slots, rows), 0),
        1.0,
        0.0,
    ).astype(jnp.bfloat16)

    cell = lax.broadcasted_iota(jnp.int32, (8, cells), 1)
    width = cells // GH
    down = cell // width
    across = cell % width
    tap = lax.broadcasted_iota(jnp.int32, (8, cells), 0)
    column = across - tap + half
    column_inside = (column >= 0) & (column < width) & (tap < side)
    me = lax.axis_index("block")
    for copy in small:
        copy.wait()
    for p in range(side):
        taps[p * 8 : p * 8 + side, :] = jnp.dot(
            stencil_ref[p], repeat, preferred_element_type=jnp.float32
        )
    for t in range(steps):
        owner = lax.broadcasted_iota(jnp.int32, (8, slots), 0)
        slot = lax.broadcasted_iota(jnp.int32, (8, slots), 1)
        live = (observed_ref[t : t + 1, :] == owner) & (slot < active_ref[0:1, t : t + 1])
        weight = jnp.dot(
            jnp.where(live, 1.0, 0.0).astype(jnp.bfloat16), spread, preferred_element_type=jnp.float32
        )
        left = jnp.concatenate([taps[...] * weight[b : b + 1, :] for b in range(2)], axis=0)
        for copy in copies[t * MAP_COPIES : (t + 1) * MAP_COPIES]:
            copy.wait()
        shifted = jnp.dot(left.astype(jnp.bfloat16), maps[t], preferred_element_type=jnp.float32)
        found = []
        for b in range(2):
            total = jnp.zeros((8, cells), jnp.float32)
            for p in range(side):
                at = (b * side + p) * 8
                part = pltpu.roll(shifted[at : at + 8, :], ((p - half) * width) % cells, 1)
                row = down - p + half
                total = total + jnp.where((row >= 0) & (row < GH), part, 0.0)
            sides = jnp.zeros((8, cells), jnp.float32)
            for q in range(side):
                part = pltpu.roll(total, (q - half) % cells, 1)
                sides = jnp.where(column_inside & (tap == q), part, sides)
            found.append(jnp.sum(sides, axis=0, keepdims=True))
        mine_ref[t : t + 1, :] = jnp.where(me == 0, found[0], found[1])
        theirs_ref[t : t + 1, :] = jnp.where(me == 0, found[1], found[0])


def sensor_info(scaled_residual_maps, measurement_stencil, observed_partition, active_probe_total):
    steps, slots, channels, cells = scaled_residual_maps.shape
    side = measurement_stencil.shape[1]
    mine, theirs = pl.pallas_call(
        info_kernel,
        out_shape=[jax.ShapeDtypeStruct((steps, cells), jnp.float32)] * 2,
        in_specs=[pl.BlockSpec(memory_space=pltpu.HBM)] * 4,
        out_specs=[VMEM] * 2,
        scratch_shapes=[
            pltpu.VMEM((steps, slots * channels, cells), jnp.bfloat16),
            pltpu.VMEM((side, side, channels), jnp.bfloat16),
            pltpu.VMEM((steps, slots), jnp.int32),
            pltpu.VMEM((1, steps), jnp.int32),
            pltpu.VMEM((side * 8, slots * channels), jnp.float32),
            pltpu.SemaphoreType.DMA((steps, MAP_COPIES)),
            pltpu.SemaphoreType.DMA((3,)),
        ],
        compiler_params=PARAMS,
        name="sensor_info",
    )(
        *(
            pltpu.with_memory_space_constraint(array, pltpu.HBM)
            for array in (
                scaled_residual_maps.reshape(steps, slots * channels, cells),
                measurement_stencil.transpose(1, 2, 0),
                observed_partition,
                active_probe_total.T,
            )
        )
    )
    return mine, lax.ppermute(theirs, "block", [(0, 1), (1, 0)])


def inputs_kernel(mine_ref, other_ref, covariance_ref, operator_ref, start_ref, inputs_ref, states_ref, send_ref):
    state = start_ref[...]
    for t in range(mine_ref.shape[0]):
        drive = times([covariance_ref[t]], mine_ref[t : t + 1, :] + other_ref[t : t + 1, :])
        inputs_ref[t : t + 1, :] = drive
        state = times([operator_ref[t]], state) + drive
        states_ref[t : t + 1, :] = state
    send_ref[...] = state


def hop_kernel(turn, came_ref, matrices_ref, offsets_ref, kept_ref, states_ref, send_ref):
    here = lax.axis_index("tm") == turn

    @pl.when(here)
    def _():
        state = came_ref[...]
        for t in range(matrices_ref.shape[0]):
            state = times([matrices_ref[t]], state) + offsets_ref[t : t + 1, :]
            states_ref[t : t + 1, :] = state
        send_ref[...] = state

    @pl.when(jnp.logical_not(here))
    def _():
        states_ref[...] = kept_ref[...]
        send_ref[...] = came_ref[...]


def compose_kernel(after_ref, gain_ref, composed_ref):
    del after_ref
    steps = gain_ref.shape[0]
    product = gain_ref[0].astype(jnp.float32)
    for t in range(1, steps):
        product = sum(
            jnp.dot(part, gain_ref[t], preferred_element_type=jnp.float32)
            for part in (halves(product) if t > 1 else [gain_ref[0]])
        )
    composed_ref[...] = product


def halves(matrix):
    high = matrix.astype(jnp.bfloat16)
    return [high, (matrix - high.astype(jnp.float32)).astype(jnp.bfloat16)]


def split_kernel(near_ref, far_ref, means_ref, near_parts_ref, far_parts_ref, result_ref):
    for source, target in ((near_ref, near_parts_ref), (far_ref, far_parts_ref)):
        target[0], target[1] = halves(source[...])
    for t in range(means_ref.shape[0]):
        result_ref[t] = means_ref[t : t + 1, :]


def offsets_kernel(last, means_ref, gain_ref, propagator_ref, offsets_ref, send_ref):
    @pl.when(lax.axis_index("tm") != last)
    def _():
        steps = means_ref.shape[0]
        means = [means_ref[t : t + 1, :] for t in range(steps)]
        moved = times([propagator_ref[...]], *means)
        state = jnp.zeros_like(means[0])
        for t in reversed(range(steps)):
            left, state = times([gain_ref[t]], moved[t], state)
            offsets_ref[t : t + 1, :] = means[t] - left
            state = state + offsets_ref[t : t + 1, :]
        send_ref[...] = state

    @pl.when(lax.axis_index("tm") == last)
    def _():
        offsets_ref[...] = means_ref[...]
        send_ref[...] = means_ref[0:1, :]


def turn_kernel(last, means_ref, gain_ref, propagator_ref, states_ref, send_ref):
    @pl.when(lax.axis_index("tm") == last)
    def _():
        steps = means_ref.shape[0]
        means = [means_ref[t : t + 1, :] for t in range(steps)]
        moved = times([propagator_ref[...]], *means)
        state = means[-1]
        states_ref[steps - 1 : steps, :] = state
        for t in reversed(range(steps - 1)):
            left, state = times([gain_ref[t]], moved[t], state)
            state = state + (means[t] - left)
            states_ref[t : t + 1, :] = state
        send_ref[...] = state

    @pl.when(lax.axis_index("tm") != last)
    def _():
        states_ref[...] = means_ref[...]
        send_ref[...] = means_ref[0:1, :]


def smooth(state, gain_ref, offsets_ref, states_ref, send_ref):
    steps = gain_ref.shape[0]
    for t in reversed(range(steps)):
        state = times([gain_ref[t]], state) + offsets_ref[t : t + 1, :]
        if len(states_ref.shape) == 3:
            states_ref[t] = state
        else:
            states_ref[t : t + 1, :] = state
    send_ref[...] = state


def first_back_kernel(
    places, last_ref, far_ref, near_ref, far_parts_ref, near_parts_ref, gain_ref, offsets_ref, kept_ref,
    came_ref, states_ref, send_ref,
):
    here = lax.axis_index("tm") == places - 4

    @pl.when(here)
    def _():
        state = times([far_parts_ref[0], far_parts_ref[1]], last_ref[...]) + far_ref[...]
        state = times([near_parts_ref[0], near_parts_ref[1]], state) + near_ref[...]
        smooth(state, gain_ref, offsets_ref, states_ref, send_ref)

    @pl.when(jnp.logical_not(here))
    def _():
        states_ref[...] = kept_ref[...]
        send_ref[...] = came_ref[...]


def back_kernel(
    target, stray, two_ref, one_ref, near_ref, near_parts_ref, gain_ref, offsets_ref, kept_ref,
    came_ref, states_ref, send_ref,
):
    here = lax.axis_index("tm")

    @pl.when(here == target)
    def _():
        state = times([near_parts_ref[0], near_parts_ref[1]], two_ref[...]) + near_ref[...]
        smooth(state, gain_ref, offsets_ref, states_ref, send_ref)

    @pl.when((here == target + 1) | (here == stray))
    def _():
        state = jnp.where(here == stray, two_ref[...], one_ref[...])
        smooth(state, gain_ref, offsets_ref, states_ref, send_ref)

    @pl.when((here != target) & (here != target + 1) & (here != stray))
    def _():
        for t in range(kept_ref.shape[0]):
            if len(states_ref.shape) == 3:
                states_ref[t] = kept_ref[t : t + 1, :]
            else:
                states_ref[t : t + 1, :] = kept_ref[t : t + 1, :]
        send_ref[...] = came_ref[...]


def call(kernel, name, outs, *args, cost=1.0):
    return pl.pallas_call(
        kernel,
        out_shape=[
            jax.ShapeDtypeStruct(shape, jnp.bfloat16 if len(shape) == 3 and shape[1] > 1 else jnp.float32)
            for shape in outs
        ],
        in_specs=[VMEM] * len(args),
        out_specs=[VMEM] * len(outs),
        compiler_params=PARAMS,
        cost_estimate=pl.CostEstimate(flops=int(cost * 1e9), bytes_accessed=2**20, transcendentals=0),
        name=name,
    )(*args)


def pass_row(row, rings, places):
    route = {}
    for place in range(places):
        for core in range(2):
            route[place * 2 + core] = place * 2 + 1 - core
    for ring in rings:
        for i, place in enumerate(ring):
            for core in range(2):
                route[place * 2 + core] = ring[(i + 1) % len(ring)] * 2 + core
    return lax.ppermute(row, ("tm", "block"), sorted(route.items()))


def ring_up(place, places):
    if place == 0:
        return (0, 1, 3)
    if place == places - 3:
        return (place, place + 1, place + 2)
    if place % 2 or place == places - 2:
        return (place, place + 1)
    return (place, place + 1, place - 2)


def local(
    scaled_residual_maps,
    measurement_stencil,
    observed_partition,
    active_probe_total,
    filtering_operator,
    updated_covariance,
    backward_factor,
    propagator,
    initial_mean,
):
    steps, size = filtering_operator.shape[0], filtering_operator.shape[-1]
    places = lax.axis_size("tm")
    many, one = (steps, size), (1, size)
    operator = filtering_operator.reshape(steps, size, size)
    covariance = updated_covariance.reshape(steps, size, size)
    gain = backward_factor.reshape(steps, size, size)
    mine, other = sensor_info(
        scaled_residual_maps, measurement_stencil, observed_partition, active_probe_total
    )
    inputs, means, send = call(
        inputs_kernel, "inputs", (many, many, one), mine, other, covariance, operator, initial_mean
    )
    composed = call(compose_kernel, "compose", ((size, size),), send, gain)[0]
    near = lax.ppermute(composed, "tm", [(place + 1, place) for place in range(0, places - 2, 2)])
    far = lax.ppermute(composed, "tm", [(places - 2, places - 4)])
    matrix = propagator.reshape(size, size)
    for place in range(1, places):
        came = pass_row(send, [ring_up(place - 1, places)], places)
        if place == places - 1:
            offsets, left = call(
                functools.partial(offsets_kernel, places - 1), "offsets", (many, one), means, gain, matrix
            )
            far_offset = pass_row(left, [(places - 2, places - 4)], places)
            near_offset = pass_row(left, [(at, at + 1) for at in range(0, places - 2, 2)], places)
        means, send = call(
            functools.partial(hop_kernel, place), "forward", (many, one), came, operator, inputs, means,
            cost=MATRIX_COST if place == 1 else 0.5,
        )
    states, send = call(
        functools.partial(turn_kernel, places - 1), "turn", (many, one), means, gain, matrix
    )
    last = pass_row(send, [(places - 1, places - 4)], places)
    parts = (2, size, size)
    result = (steps, 1, size)
    near_parts, far_parts, means = call(split_kernel, "split", (parts, parts, result), near, far, means)
    states, send = call(
        functools.partial(first_back_kernel, places),
        "first_back",
        (many, one),
        last,
        far_offset,
        near_offset,
        far_parts,
        near_parts,
        gain,
        offsets,
        states,
        send,
    )
    stray = places - 2
    for target in range(places - 6, -1, -2):
        rings = [(target + 2, target)] + ([(stray + 1, stray)] if stray > target + 2 else [])
        two = pass_row(send, rings, places)
        one_up = pass_row(send, [(target + 2, target + 1)], places)
        states, send = call(
            functools.partial(back_kernel, target, stray),
            "back",
            (many if target else result, one),
            two,
            one_up,
            near_offset,
            near_parts,
            gain,
            offsets,
            states,
            send,
        )
        stray = stray - 1 if stray == places - 2 else -1
    return means, states


def solution(mesh):
    placed = (
        P(("groups", "tm"), "block", None, None),
        P(),
        P(("groups", "tm"), "block"),
        P(("groups", "tm"), "block"),
        P(("groups", "tm"), "block", None, None),
        P(("groups", "tm"), "block", None, None),
        P(("groups", "tm"), "block", None, None),
        P("block", None, None),
        P(("groups", "block"), None),
    )
    return jax.shard_map(
        local,
        mesh=mesh,
        in_specs=placed,
        out_specs=(P(("groups", "tm"), "block", None), P(("groups", "tm"), "block", None)),
        check_vma=False,
    )
```

```python
import functools

import jax
import jax.numpy as jnp
from jax import lax
from jax.experimental import pallas as pl
from jax.experimental.pallas import tpu as pltpu
from jax.sharding import PartitionSpec as P

GH = 16
MAP_COPIES = 4
COSTS = (60.0, 2.5, 2.5, 6.0, 0.5)
VMEM = pl.BlockSpec(memory_space=pltpu.VMEM)
PARAMS = pltpu.CompilerParams(vmem_limit_bytes=16 * 2**20)


def pieces(rows, count=3):
    height = -(-len(rows) * count // 8) * 8
    at = lax.broadcasted_iota(jnp.int32, (height, rows[0].shape[1]), 0)
    block = jnp.zeros(at.shape, jnp.float32)
    for k, rest in enumerate(rows):
        for i in range(count):
            piece = rest.astype(jnp.bfloat16).astype(jnp.float32)
            block = jnp.where(at == k * count + i, piece, block)
            rest = rest - piece
    return block.astype(jnp.bfloat16)


def times(matrices, *rows):
    block = pieces(rows)
    product = sum(
        lax.dot_general(block, matrix, (((1,), (1,)), ((), ())), preferred_element_type=jnp.float32)
        for matrix in matrices
    )
    found = [jnp.sum(product[3 * k : 3 * k + 3, :], axis=0, keepdims=True) for k in range(len(rows))]
    return found if len(rows) > 1 else found[0]


def info_kernel(
    maps_hbm,
    stencil_hbm,
    observed_hbm,
    active_hbm,
    mine_ref,
    theirs_ref,
    maps,
    stencil_ref,
    observed_ref,
    active_ref,
    taps,
    map_sems,
    sems,
):
    steps, rows, cells = maps.shape
    slots = observed_ref.shape[1]
    side, _, channels = stencil_ref.shape
    half = side // 2
    small = []
    for i, (source, target) in enumerate(
        ((stencil_hbm, stencil_ref), (observed_hbm, observed_ref), (active_hbm, active_ref))
    ):
        small.append(pltpu.make_async_copy(source, target, sems.at[i]))
        small[-1].start()
    part = rows // MAP_COPIES
    copies = []
    for t in range(steps):
        for i in range(MAP_COPIES):
            at = pl.ds(i * part, part)
            copies.append(
                pltpu.make_async_copy(maps_hbm.at[t, at], maps.at[t, at], map_sems.at[t, i])
            )
            copies[-1].start()

    repeat = jnp.where(
        lax.broadcasted_iota(jnp.int32, (channels, rows), 1) % channels
        == lax.broadcasted_iota(jnp.int32, (channels, rows), 0),
        1.0,
        0.0,
    ).astype(jnp.bfloat16)
    taps[...] = jnp.zeros_like(taps)
    spread = jnp.where(
        lax.broadcasted_iota(jnp.int32, (slots, rows), 1) // channels
        == lax.broadcasted_iota(jnp.int32, (slots, rows), 0),
        1.0,
        0.0,
    ).astype(jnp.bfloat16)

    cell = lax.broadcasted_iota(jnp.int32, (8, cells), 1)
    width = cells // GH
    down = cell // width
    across = cell % width
    tap = lax.broadcasted_iota(jnp.int32, (8, cells), 0)
    column = across - tap + half
    column_inside = (column >= 0) & (column < width) & (tap < side)
    me = lax.axis_index("block")
    for copy in small:
        copy.wait()
    for p in range(side):
        taps[p * 8 : p * 8 + side, :] = jnp.dot(
            stencil_ref[p], repeat, preferred_element_type=jnp.float32
        )
    for t in range(steps):
        owner = lax.broadcasted_iota(jnp.int32, (8, slots), 0)
        slot = lax.broadcasted_iota(jnp.int32, (8, slots), 1)
        live = (observed_ref[t : t + 1, :] == owner) & (slot < active_ref[0:1, t : t + 1])
        weight = jnp.dot(
            jnp.where(live, 1.0, 0.0).astype(jnp.bfloat16), spread, preferred_element_type=jnp.float32
        )
        left = jnp.concatenate([taps[...] * weight[b : b + 1, :] for b in range(2)], axis=0)
        for copy in copies[t * MAP_COPIES : (t + 1) * MAP_COPIES]:
            copy.wait()
        shifted = jnp.dot(left.astype(jnp.bfloat16), maps[t], preferred_element_type=jnp.float32)
        found = []
        for b in range(2):
            total = jnp.zeros((8, cells), jnp.float32)
            for p in range(side):
                at = (b * side + p) * 8
                part = pltpu.roll(shifted[at : at + 8, :], ((p - half) * width) % cells, 1)
                row = down - p + half
                total = total + jnp.where((row >= 0) & (row < GH), part, 0.0)
            sides = jnp.zeros((8, cells), jnp.float32)
            for q in range(side):
                part = pltpu.roll(total, (q - half) % cells, 1)
                sides = jnp.where(column_inside & (tap == q), part, sides)
            found.append(jnp.sum(sides, axis=0, keepdims=True))
        mine_ref[t : t + 1, :] = jnp.where(me == 0, found[0], found[1])
        theirs_ref[t : t + 1, :] = jnp.where(me == 0, found[1], found[0])


def sensor_info(scaled_residual_maps, measurement_stencil, observed_partition, active_probe_total):
    steps, slots, channels, cells = scaled_residual_maps.shape
    side = measurement_stencil.shape[1]
    mine, theirs = pl.pallas_call(
        info_kernel,
        out_shape=[jax.ShapeDtypeStruct((steps, cells), jnp.float32)] * 2,
        in_specs=[pl.BlockSpec(memory_space=pltpu.HBM)] * 4,
        out_specs=[VMEM] * 2,
        scratch_shapes=[
            pltpu.VMEM((steps, slots * channels, cells), jnp.bfloat16),
            pltpu.VMEM((side, side, channels), jnp.bfloat16),
            pltpu.VMEM((steps, slots), jnp.int32),
            pltpu.VMEM((1, steps), jnp.int32),
            pltpu.VMEM((side * 8, slots * channels), jnp.float32),
            pltpu.SemaphoreType.DMA((steps, MAP_COPIES)),
            pltpu.SemaphoreType.DMA((3,)),
        ],
        compiler_params=PARAMS,
        name="sensor_info",
    )(
        *(
            pltpu.with_memory_space_constraint(array, pltpu.HBM)
            for array in (
                scaled_residual_maps.reshape(steps, slots * channels, cells),
                measurement_stencil.transpose(1, 2, 0),
                observed_partition,
                active_probe_total.T,
            )
        )
    )
    return mine, lax.ppermute(theirs, "block", [(0, 1), (1, 0)])


def inputs_kernel(mine_ref, other_ref, covariance_ref, operator_ref, start_ref, inputs_ref, states_ref, send_ref):
    state = start_ref[...]
    for t in range(mine_ref.shape[0]):
        drive = times([covariance_ref[t]], mine_ref[t : t + 1, :] + other_ref[t : t + 1, :])
        inputs_ref[t : t + 1, :] = drive
        state = times([operator_ref[t]], state) + drive
        states_ref[t : t + 1, :] = state
    send_ref[...] = state


def hop_kernel(turn, came_ref, matrices_ref, offsets_ref, kept_ref, states_ref, send_ref):
    here = lax.axis_index("tm") == turn

    @pl.when(here)
    def _():
        state = came_ref[...]
        for t in range(matrices_ref.shape[0]):
            state = times([matrices_ref[t]], state) + offsets_ref[t : t + 1, :]
            states_ref[t : t + 1, :] = state
        send_ref[...] = state

    @pl.when(jnp.logical_not(here))
    def _():
        states_ref[...] = kept_ref[...]
        send_ref[...] = came_ref[...]


def halves(matrix):
    high = matrix.astype(jnp.bfloat16)
    return [high, (matrix - high.astype(jnp.float32)).astype(jnp.bfloat16)]


def composed(gain_ref):
    product = gain_ref[0]
    for t in range(1, gain_ref.shape[0]):
        product = sum(
            jnp.dot(part, gain_ref[t], preferred_element_type=jnp.float32)
            for part in (halves(product) if t > 1 else [product])
        )
    return product.astype(jnp.float32)


def compose_kernel(senders, after_ref, gain_ref, composed_ref):
    del after_ref
    here = lax.axis_index("tm")
    sends = functools.reduce(jnp.logical_or, [here == place for place in senders])

    @pl.when(sends)
    def _():
        composed_ref[...] = composed(gain_ref)


def late_kernel(senders, means_ref, gain_ref, propagator_ref, composed_ref):
    size = gain_ref.shape[1]
    here = lax.axis_index("tm")
    sends = functools.reduce(jnp.logical_or, [here == place for place in senders])

    @pl.when(sends)
    def _():
        composed_ref[:size, :] = composed(gain_ref)
        composed_ref[size:, :] = jnp.zeros((composed_ref.shape[0] - size, size), jnp.float32)
        composed_ref[size : size + 1, :] = offsets(means_ref, gain_ref, propagator_ref)[0]


def offsets(means_ref, gain_ref, propagator_ref):
    steps = means_ref.shape[0]
    means = [means_ref[t : t + 1, :] for t in range(steps)]
    moved = times([propagator_ref[...]], *means)
    state = jnp.zeros_like(means[0])
    found = [None] * steps
    for t in reversed(range(steps)):
        left, state = times([gain_ref[t]], moved[t], state)
        found[t] = means[t] - left
        state = state + found[t]
    return state, found


def pair_kernel(
    places,
    skip_place,
    near_ref,
    skip_ref,
    gain_ref,
    left_ref,
    near_offset_ref,
    near_parts_ref,
    pair_parts_ref,
    pair_offset_ref,
    skip_parts_ref,
):
    here = lax.axis_index("tm")

    @pl.when(functools.reduce(jnp.logical_or, [here == place for place in places]))
    def _():
        near = halves(near_ref[...])
        own = halves(composed(gain_ref))
        near_parts_ref[0], near_parts_ref[1] = near
        pair_parts_ref[0], pair_parts_ref[1] = halves(
            jnp.dot(own[0], near[0], preferred_element_type=jnp.float32)
            + jnp.dot(own[0], near[1], preferred_element_type=jnp.float32)
            + jnp.dot(own[1], near[0], preferred_element_type=jnp.float32)
        )
        pair_offset_ref[...] = times(own, near_offset_ref[...]) + left_ref[...]

    @pl.when(here == skip_place)
    def _():
        skip_parts_ref[0], skip_parts_ref[1] = halves(skip_ref[...])


def late_split_kernel(place, late_ref, after_ref, parts_ref, offset_ref):
    del after_ref
    size = late_ref.shape[1]

    @pl.when(lax.axis_index("tm") == place)
    def _():
        parts_ref[0], parts_ref[1] = halves(late_ref[:size, :])
        offset_ref[...] = late_ref[size : size + 1, :]


def split_kernel(place, matrix_ref, left_ref, parts_ref, again_ref):
    again_ref[...] = left_ref[...]

    @pl.when(lax.axis_index("tm") == place)
    def _():
        parts_ref[0], parts_ref[1] = halves(matrix_ref[...])


def offsets_kernel(last, means_ref, gain_ref, propagator_ref, offsets_ref, send_ref, own_parts_ref):
    here = lax.axis_index("tm") == last

    @pl.when(lax.axis_index("tm") == last - 2)
    def _():
        own_parts_ref[0], own_parts_ref[1] = halves(composed(gain_ref))

    @pl.when(jnp.logical_not(here))
    def _():
        send_ref[...], found = offsets(means_ref, gain_ref, propagator_ref)
        for t, row in enumerate(found):
            offsets_ref[t : t + 1, :] = row

    @pl.when(here)
    def _():
        offsets_ref[...] = means_ref[...]
        send_ref[...] = means_ref[0:1, :]


def last_kernel(
    last, came_ref, operator_ref, inputs_ref, kept_ref, gain_ref, propagator_ref,
    means_ref, states_ref, send_ref,
):
    @pl.when(lax.axis_index("tm") == last)
    def _():
        steps = operator_ref.shape[0]
        state = came_ref[...]
        means, moved = [], []
        for t in range(steps):
            state = times([operator_ref[t]], state) + inputs_ref[t : t + 1, :]
            means_ref[t : t + 1, :] = state
            means.append(state)
            if t < steps - 1:
                moved.append(times([propagator_ref[...]], state))
        states_ref[steps - 1 : steps, :] = state
        for t in reversed(range(steps - 1)):
            left, state = times([gain_ref[t]], moved[t], state)
            state = state + (means[t] - left)
            states_ref[t : t + 1, :] = state
        send_ref[...] = state

    @pl.when(lax.axis_index("tm") != last)
    def _():
        means_ref[...] = kept_ref[...]
        states_ref[...] = kept_ref[...]
        send_ref[...] = came_ref[...]


def smooth(state, gain_ref, offsets_ref, put):
    for t in reversed(range(gain_ref.shape[0])):
        state = times([gain_ref[t]], state) + offsets_ref[t : t + 1, :]
        put(t, state)


def parts_times(parts_ref, row_ref):
    return times([parts_ref[0], parts_ref[1]], row_ref[...])


def first_back_kernel(
    place, last_ref, far_offset_ref, far_parts_ref, own_parts_ref, left_ref, came_ref, entry_ref, send_ref
):
    here = lax.axis_index("tm") == place

    @pl.when(here)
    def _():
        entry_ref[...] = parts_times(far_parts_ref, last_ref) + far_offset_ref[...]
        send_ref[...] = parts_times(own_parts_ref, entry_ref) + left_ref[...]

    @pl.when(jnp.logical_not(here))
    def _():
        entry_ref[...] = last_ref[...]
        send_ref[...] = came_ref[...]


def second_back_kernel(
    last,
    three_ref,
    one_ref,
    entry_ref,
    skip_offset_ref,
    skip_parts_ref,
    pair_parts_ref,
    pair_offset_ref,
    gain_ref,
    offsets_ref,
    kept_ref,
    came_ref,
    states_ref,
    next_ref,
    send_ref,
):
    here = lax.axis_index("tm")

    def put(t, state):
        states_ref[t : t + 1, :] = state

    @pl.when(here == last - 5)
    def _():
        state = parts_times(skip_parts_ref, three_ref) + skip_offset_ref[...]
        next_ref[...] = state
        send_ref[...] = times([pair_parts_ref[0], pair_parts_ref[1]], state) + pair_offset_ref[...]
        states_ref[...] = kept_ref[...]

    @pl.when(here != last - 5)
    def _():
        send_ref[...] = came_ref[...]
        next_ref[...] = entry_ref[...]

    @pl.when(here == last - 2)
    def _():
        smooth(entry_ref[...], gain_ref, offsets_ref, put)

    @pl.when((here == last - 3) | (here == last - 1))
    def _():
        smooth(jnp.where(here == last - 1, three_ref[...], one_ref[...]), gain_ref, offsets_ref, put)
        send_ref[...] = states_ref[0:1, :]

    @pl.when((here == last) | (here == last - 4) | (here < last - 5))
    def _():
        states_ref[...] = kept_ref[...]


def back_kernel(
    target,
    stray,
    two_ref,
    one_ref,
    entry_ref,
    near_offset_ref,
    near_parts_ref,
    pair_parts_ref,
    pair_offset_ref,
    gain_ref,
    offsets_ref,
    kept_ref,
    came_ref,
    states_ref,
    next_ref,
    send_ref,
):
    here = lax.axis_index("tm")

    def put(t, state):
        states_ref[t : t + 1, :] = state

    @pl.when(here == target)
    def _():
        send_ref[...] = times([pair_parts_ref[0], pair_parts_ref[1]], two_ref[...]) + pair_offset_ref[...]
        next_ref[...] = two_ref[...]
        states_ref[...] = kept_ref[...]

    @pl.when(here != target)
    def _():
        send_ref[...] = came_ref[...]
        next_ref[...] = entry_ref[...]

    @pl.when(here == target + 2)
    def _():
        state = times([near_parts_ref[0], near_parts_ref[1]], entry_ref[...]) + near_offset_ref[...]
        smooth(state, gain_ref, offsets_ref, put)

    @pl.when((here == target + 1) | (here == stray))
    def _():
        smooth(jnp.where(here == stray, two_ref[...], one_ref[...]), gain_ref, offsets_ref, put)
        send_ref[...] = states_ref[0:1, :]

    @pl.when((here > target + 2) & (here != stray) | (here < target))
    def _():
        states_ref[...] = kept_ref[...]


def final_kernel(
    stray,
    two_ref,
    one_ref,
    entry_ref,
    near_offset_ref,
    near_parts_ref,
    late_offset_ref,
    late_parts_ref,
    gain_ref,
    offsets_ref,
    kept_ref,
    means_ref,
    result_ref,
    states_ref,
):
    here = lax.axis_index("tm")
    for t in range(means_ref.shape[0]):
        result_ref[t] = means_ref[t : t + 1, :]

    def put(t, state):
        states_ref[t] = state

    @pl.when(here == 0)
    def _():
        smooth(parts_times(late_parts_ref, two_ref) + late_offset_ref[...], gain_ref, offsets_ref, put)

    @pl.when(here == 2)
    def _():
        state = times([near_parts_ref[0], near_parts_ref[1]], entry_ref[...]) + near_offset_ref[...]
        smooth(state, gain_ref, offsets_ref, put)

    @pl.when((here == 1) | (here == stray))
    def _():
        smooth(jnp.where(here == stray, two_ref[...], one_ref[...]), gain_ref, offsets_ref, put)

    @pl.when((here > 2) & (here != stray))
    def _():
        for t in range(kept_ref.shape[0]):
            states_ref[t] = kept_ref[t : t + 1, :]


def call(kernel, name, outs, *args, cost=1.0):
    return pl.pallas_call(
        kernel,
        out_shape=[
            jax.ShapeDtypeStruct(shape, jnp.bfloat16 if len(shape) == 3 and shape[1] > 1 else jnp.float32)
            for shape in outs
        ],
        in_specs=[VMEM] * len(args),
        out_specs=[VMEM] * len(outs),
        compiler_params=PARAMS,
        cost_estimate=pl.CostEstimate(flops=int(cost * 1e9), bytes_accessed=2**20, transcendentals=0),
        name=name,
    )(*args)


def pass_row(row, rings, places):
    route = {}
    for place in range(places):
        for core in range(2):
            route[place * 2 + core] = place * 2 + 1 - core
    for ring in rings:
        for i, place in enumerate(ring):
            for core in range(2):
                route[place * 2 + core] = ring[(i + 1) % len(ring)] * 2 + core
    return lax.ppermute(row, ("tm", "block"), sorted(route.items()))


def ring_up(place, places):
    if place == 0:
        return (0, 1, 3)
    if place % 2 and place >= places - 5 and place < places - 1:
        return (place, place + 1, place + 2)
    if place % 2 or place == places - 2:
        return (place, place + 1)
    return (place, place + 1, place - 2)


def local(
    scaled_residual_maps,
    measurement_stencil,
    observed_partition,
    active_probe_total,
    filtering_operator,
    updated_covariance,
    backward_factor,
    propagator,
    initial_mean,
):
    steps, size = filtering_operator.shape[0], filtering_operator.shape[-1]
    places = lax.axis_size("tm")
    many, one = (steps, size), (1, size)
    operator = filtering_operator.reshape(steps, size, size)
    covariance = updated_covariance.reshape(steps, size, size)
    gain = backward_factor.reshape(steps, size, size)
    last = places - 1
    matrix = propagator.reshape(size, size)
    square, parts, result = (size, size), (2, size, size), (steps, 1, size)
    mine, other = sensor_info(
        scaled_residual_maps, measurement_stencil, observed_partition, active_probe_total
    )

    def compose(after, *senders):
        return call(functools.partial(compose_kernel, senders), "compose", (square,), after, gain, cost=0.5)[0]

    near_senders = range(3, last - 3, 2)
    first = lax.ppermute(
        compose(mine, last - 1, *near_senders), "tm", [(place, place - 1) for place in (*near_senders, last - 1)]
    )
    inputs, means, send = call(
        inputs_kernel, "inputs", (many, many, one), mine, other, covariance, operator, initial_mean,
        cost=COSTS[0],
    )
    skip = lax.ppermute(compose(send, last - 3), "tm", [(last - 3, last - 5)])
    for place in range(1, places):
        came = pass_row(send, [ring_up(place - 1, places)], places)
        if place == 2:
            late = call(
                functools.partial(late_kernel, (1,)), "late", ((size + 8, size),), means, gain, matrix,
                cost=0.5,
            )[0]
            late = lax.ppermute(late, "tm", [(1, 0)])
        if place < last:
            means, send = call(
                functools.partial(hop_kernel, place), "forward", (many, one), came, operator, inputs, means,
                cost={1: COSTS[1], 2: COSTS[2]}.get(place, 0.5),
            )
    offset_rows, left, own_parts = call(
        functools.partial(offsets_kernel, last), "offsets", (many, one, parts), means, gain, matrix
    )
    other_offset = pass_row(left, [(last - 1, last - 2), (last - 3, last - 5)], places)
    means, states, send = call(
        functools.partial(last_kernel, last),
        "last",
        (many, many, one),
        came,
        operator,
        inputs,
        means,
        gain,
        matrix,
        cost=0.5,
    )
    came = pass_row(send, [(last, last - 2)], places)

    far_parts, again = call(
        functools.partial(split_kernel, last - 2), "split", (parts, one), first, left, cost=0.05
    )
    near_offset = pass_row(again, [(place - 1, place) for place in near_senders], places)
    entry, send = call(
        functools.partial(first_back_kernel, last - 2), "first_back", (one, one),
        came, other_offset, far_parts, own_parts, left, send,
        cost=COSTS[3],
    )
    one_up = pass_row(send, [(last - 2, last - 3)], places)
    three = pass_row(send, [(last - 2, last - 5), (last, last - 1)], places)
    near_parts, pair_parts, pair_offset, skip_parts = call(
        functools.partial(pair_kernel, tuple(place - 1 for place in near_senders), last - 5),
        "pair",
        (parts, parts, one, parts),
        first,
        skip,
        gain,
        left,
        near_offset,
        cost=0.05,
    )
    states, entry, send = call(
        functools.partial(second_back_kernel, last),
        "second_back",
        (many, one, one),
        three,
        one_up,
        entry,
        other_offset,
        skip_parts,
        pair_parts,
        pair_offset,
        gain,
        offset_rows,
        states,
        send,
        cost=COSTS[4],
    )
    stray = last - 4
    for target in range(last - 7, -1, -2):
        rings = [(target + 2, target)] + ([(stray + 1, stray)] if stray > 0 else [])
        one_up = pass_row(send, [(target + 2, target + 1)], places)
        two = pass_row(send, rings, places)
        if target:
            states, entry, send = call(
                functools.partial(back_kernel, target, stray), "back", (many, one, one),
                two, one_up, entry, near_offset, near_parts, pair_parts, pair_offset, gain, offset_rows, states,
                send,
            )
        else:
            late_parts, late_offset = call(
                functools.partial(late_split_kernel, 0), "late_split", (parts, one), late, send, cost=0.05
            )
            means, states = call(
                functools.partial(final_kernel, stray), "final", (result, result),
                two, one_up, entry, near_offset, near_parts, late_offset, late_parts, gain, offset_rows, states, means,
            )
        stray = -1
    return means, states


def solution(mesh):
    placed = (
        P(("groups", "tm"), "block", None, None),
        P(),
        P(("groups", "tm"), "block"),
        P(("groups", "tm"), "block"),
        P(("groups", "tm"), "block", None, None),
        P(("groups", "tm"), "block", None, None),
        P(("groups", "tm"), "block", None, None),
        P("block", None, None),
        P(("groups", "block"), None),
    )
    return jax.shard_map(
        local,
        mesh=mesh,
        in_specs=placed,
        out_specs=(P(("groups", "tm"), "block", None), P(("groups", "tm"), "block", None)),
        check_vma=False,
    )
```

```python
import functools

import jax
import jax.numpy as jnp
from jax import lax
from jax.experimental import pallas as pl
from jax.experimental.pallas import tpu as pltpu
from jax.sharding import PartitionSpec as P

GH = 16
MAP_COPIES = 4
COSTS = (60.0, 2.5, 2.5, 6.0, 0.5)
VMEM = pl.BlockSpec(memory_space=pltpu.VMEM)
PARAMS = pltpu.CompilerParams(vmem_limit_bytes=16 * 2**20)


def pieces(rows, count=3):
    height = -(-len(rows) * count // 8) * 8
    at = lax.broadcasted_iota(jnp.int32, (height, rows[0].shape[1]), 0)
    block = jnp.zeros(at.shape, jnp.float32)
    for k, rest in enumerate(rows):
        for i in range(count):
            piece = rest.astype(jnp.bfloat16).astype(jnp.float32)
            block = jnp.where(at == k * count + i, piece, block)
            rest = rest - piece
    return block.astype(jnp.bfloat16)


def times(matrices, *rows):
    block = pieces(rows)
    product = sum(
        lax.dot_general(block, matrix, (((1,), (1,)), ((), ())), preferred_element_type=jnp.float32)
        for matrix in matrices
    )
    found = [jnp.sum(product[3 * k : 3 * k + 3, :], axis=0, keepdims=True) for k in range(len(rows))]
    return found if len(rows) > 1 else found[0]


def info_kernel(zero, *refs):
    @pl.when((lax.axis_index("tm") == 0) == zero)
    def _():
        place_info(*(refs if zero else refs[1:]))


def place_info(
    maps_hbm,
    stencil_hbm,
    observed_hbm,
    active_hbm,
    mine_ref,
    theirs_ref,
    maps,
    stencil_ref,
    observed_ref,
    active_ref,
    taps,
    map_sems,
    sems,
):
    steps, rows, cells = maps.shape
    slots = observed_ref.shape[1]
    side, _, channels = stencil_ref.shape
    half = side // 2
    small = []
    for i, (source, target) in enumerate(
        ((stencil_hbm, stencil_ref), (observed_hbm, observed_ref), (active_hbm, active_ref))
    ):
        small.append(pltpu.make_async_copy(source, target, sems.at[i]))
        small[-1].start()
    part = rows // MAP_COPIES
    copies = []
    for t in range(steps):
        for i in range(MAP_COPIES):
            at = pl.ds(i * part, part)
            copies.append(
                pltpu.make_async_copy(maps_hbm.at[t, at], maps.at[t, at], map_sems.at[t, i])
            )
            copies[-1].start()

    repeat = jnp.where(
        lax.broadcasted_iota(jnp.int32, (channels, rows), 1) % channels
        == lax.broadcasted_iota(jnp.int32, (channels, rows), 0),
        1.0,
        0.0,
    ).astype(jnp.bfloat16)
    taps[...] = jnp.zeros_like(taps)
    spread = jnp.where(
        lax.broadcasted_iota(jnp.int32, (slots, rows), 1) // channels
        == lax.broadcasted_iota(jnp.int32, (slots, rows), 0),
        1.0,
        0.0,
    ).astype(jnp.bfloat16)

    cell = lax.broadcasted_iota(jnp.int32, (8, cells), 1)
    width = cells // GH
    down = cell // width
    across = cell % width
    tap = lax.broadcasted_iota(jnp.int32, (8, cells), 0)
    column = across - tap + half
    column_inside = (column >= 0) & (column < width) & (tap < side)
    me = lax.axis_index("block")
    for copy in small:
        copy.wait()
    for p in range(side):
        taps[p * 8 : p * 8 + side, :] = jnp.dot(
            stencil_ref[p], repeat, preferred_element_type=jnp.float32
        )
    for t in range(steps):
        owner = lax.broadcasted_iota(jnp.int32, (8, slots), 0)
        slot = lax.broadcasted_iota(jnp.int32, (8, slots), 1)
        live = (observed_ref[t : t + 1, :] == owner) & (slot < active_ref[0:1, t : t + 1])
        weight = jnp.dot(
            jnp.where(live, 1.0, 0.0).astype(jnp.bfloat16), spread, preferred_element_type=jnp.float32
        )
        left = jnp.concatenate([taps[...] * weight[b : b + 1, :] for b in range(2)], axis=0)
        for copy in copies[t * MAP_COPIES : (t + 1) * MAP_COPIES]:
            copy.wait()
        shifted = jnp.dot(left.astype(jnp.bfloat16), maps[t], preferred_element_type=jnp.float32)
        found = []
        for b in range(2):
            total = jnp.zeros((8, cells), jnp.float32)
            for p in range(side):
                at = (b * side + p) * 8
                part = pltpu.roll(shifted[at : at + 8, :], ((p - half) * width) % cells, 1)
                row = down - p + half
                total = total + jnp.where((row >= 0) & (row < GH), part, 0.0)
            sides = jnp.zeros((8, cells), jnp.float32)
            for q in range(side):
                part = pltpu.roll(total, (q - half) % cells, 1)
                sides = jnp.where(column_inside & (tap == q), part, sides)
            found.append(jnp.sum(sides, axis=0, keepdims=True))
        mine_ref[t : t + 1, :] = jnp.where(me == 0, found[0], found[1])
        theirs_ref[t : t + 1, :] = jnp.where(me == 0, found[1], found[0])


def sensor_info(after, scaled_residual_maps, measurement_stencil, observed_partition, active_probe_total):
    zero = not after
    steps, slots, channels, cells = scaled_residual_maps.shape
    side = measurement_stencil.shape[1]
    mine, theirs = pl.pallas_call(
        functools.partial(info_kernel, zero),
        out_shape=[jax.ShapeDtypeStruct((steps, cells), jnp.float32)] * 2,
        in_specs=[VMEM] * len(after) + [pl.BlockSpec(memory_space=pltpu.HBM)] * 4,
        out_specs=[VMEM] * 2,
        scratch_shapes=[
            pltpu.VMEM((steps, slots * channels, cells), jnp.bfloat16),
            pltpu.VMEM((side, side, channels), jnp.bfloat16),
            pltpu.VMEM((steps, slots), jnp.int32),
            pltpu.VMEM((1, steps), jnp.int32),
            pltpu.VMEM((side * 8, slots * channels), jnp.float32),
            pltpu.SemaphoreType.DMA((steps, MAP_COPIES)),
            pltpu.SemaphoreType.DMA((3,)),
        ],
        compiler_params=PARAMS,
        cost_estimate=pl.CostEstimate(flops=10**6 if zero else int(COSTS[0] * 1e9), bytes_accessed=2**12, transcendentals=0),
        name="sensor_info",
    )(
        *after,
        *(
            pltpu.with_memory_space_constraint(array, pltpu.HBM)
            for array in (
                scaled_residual_maps.reshape(steps, slots * channels, cells),
                measurement_stencil.transpose(1, 2, 0),
                observed_partition,
                active_probe_total.T,
            )
        )
    )
    return mine, lax.ppermute(theirs, "block", [(0, 1), (1, 0)])


def start_kernel(mine_ref, other_ref, covariance_ref, operator_ref, start_ref, inputs_ref, states_ref, send_ref):
    here = lax.axis_index("tm") == 0

    @pl.when(here)
    def _():
        state = start_ref[...]
        for t in range(mine_ref.shape[0]):
            drive = times([covariance_ref[t]], mine_ref[t : t + 1, :] + other_ref[t : t + 1, :])
            inputs_ref[t : t + 1, :] = drive
            state = times([operator_ref[t]], state) + drive
            states_ref[t : t + 1, :] = state
        send_ref[...] = jnp.broadcast_to(state, send_ref.shape)

    @pl.when(jnp.logical_not(here))
    def _():
        inputs_ref[...] = jnp.zeros_like(inputs_ref)
        states_ref[...] = jnp.zeros_like(states_ref)
        send_ref[...] = jnp.zeros_like(send_ref)


def first_hop_kernel(
    came_ref, mine_ref, other_ref, covariance_ref, operator_ref, kept_inputs_ref, kept_ref,
    inputs_ref, states_ref, send_ref,
):
    here = lax.axis_index("tm")

    @pl.when(here == 0)
    def _():
        inputs_ref[...] = kept_inputs_ref[...]

    @pl.when(here != 0)
    def _():
        for t in range(mine_ref.shape[0]):
            info = mine_ref[t : t + 1, :] + other_ref[t : t + 1, :]
            inputs_ref[t : t + 1, :] = times([covariance_ref[t]], info)

    @pl.when(here == 1)
    def _():
        state = came_ref[0:1, :]
        for t in range(operator_ref.shape[0]):
            state = times([operator_ref[t]], state) + inputs_ref[t : t + 1, :]
            states_ref[t : t + 1, :] = state
        send_ref[...] = state

    @pl.when(here != 1)
    def _():
        states_ref[...] = kept_ref[...]
        send_ref[...] = came_ref[0:1, :]


def hop_kernel(turn, came_ref, matrices_ref, offsets_ref, kept_ref, states_ref, send_ref):
    here = lax.axis_index("tm") == turn

    @pl.when(here)
    def _():
        state = came_ref[...]
        for t in range(matrices_ref.shape[0]):
            state = times([matrices_ref[t]], state) + offsets_ref[t : t + 1, :]
            states_ref[t : t + 1, :] = state
        send_ref[...] = state

    @pl.when(jnp.logical_not(here))
    def _():
        states_ref[...] = kept_ref[...]
        send_ref[...] = came_ref[...]


def halves(matrix):
    high = matrix.astype(jnp.bfloat16)
    return [high, (matrix - high.astype(jnp.float32)).astype(jnp.bfloat16)]


def composed(gain_ref):
    product = gain_ref[0]
    for t in range(1, gain_ref.shape[0]):
        product = sum(
            jnp.dot(part, gain_ref[t], preferred_element_type=jnp.float32)
            for part in (halves(product) if t > 1 else [product])
        )
    return product.astype(jnp.float32)


def compose_kernel(senders, after_ref, gain_ref, composed_ref):
    del after_ref
    here = lax.axis_index("tm")
    sends = functools.reduce(jnp.logical_or, [here == place for place in senders])

    @pl.when(sends)
    def _():
        composed_ref[...] = composed(gain_ref)


def late_kernel(senders, means_ref, gain_ref, propagator_ref, composed_ref):
    size = gain_ref.shape[1]
    here = lax.axis_index("tm")
    sends = functools.reduce(jnp.logical_or, [here == place for place in senders])

    @pl.when(sends)
    def _():
        composed_ref[:size, :] = composed(gain_ref)
        composed_ref[size:, :] = jnp.zeros((composed_ref.shape[0] - size, size), jnp.float32)
        composed_ref[size : size + 1, :] = offsets(means_ref, gain_ref, propagator_ref)[0]


def offsets(means_ref, gain_ref, propagator_ref):
    steps = means_ref.shape[0]
    means = [means_ref[t : t + 1, :] for t in range(steps)]
    moved = times([propagator_ref[...]], *means)
    state = jnp.zeros_like(means[0])
    found = [None] * steps
    for t in reversed(range(steps)):
        left, state = times([gain_ref[t]], moved[t], state)
        found[t] = means[t] - left
        state = state + found[t]
    return state, found


def pair_kernel(
    places,
    skip_place,
    near_ref,
    skip_ref,
    gain_ref,
    left_ref,
    near_offset_ref,
    near_parts_ref,
    pair_parts_ref,
    pair_offset_ref,
    skip_parts_ref,
):
    here = lax.axis_index("tm")

    @pl.when(functools.reduce(jnp.logical_or, [here == place for place in places]))
    def _():
        near = halves(near_ref[...])
        own = halves(composed(gain_ref))
        near_parts_ref[0], near_parts_ref[1] = near
        pair_parts_ref[0], pair_parts_ref[1] = halves(
            jnp.dot(own[0], near[0], preferred_element_type=jnp.float32)
            + jnp.dot(own[0], near[1], preferred_element_type=jnp.float32)
            + jnp.dot(own[1], near[0], preferred_element_type=jnp.float32)
        )
        pair_offset_ref[...] = times(own, near_offset_ref[...]) + left_ref[...]

    @pl.when(here == skip_place)
    def _():
        skip_parts_ref[0], skip_parts_ref[1] = halves(skip_ref[...])


def late_split_kernel(place, late_ref, after_ref, parts_ref, offset_ref):
    del after_ref
    size = late_ref.shape[1]

    @pl.when(lax.axis_index("tm") == place)
    def _():
        parts_ref[0], parts_ref[1] = halves(late_ref[:size, :])
        offset_ref[...] = late_ref[size : size + 1, :]


def split_kernel(place, matrix_ref, left_ref, parts_ref, again_ref):
    again_ref[...] = left_ref[...]

    @pl.when(lax.axis_index("tm") == place)
    def _():
        parts_ref[0], parts_ref[1] = halves(matrix_ref[...])


def offsets_kernel(last, means_ref, gain_ref, propagator_ref, offsets_ref, send_ref, own_parts_ref):
    here = lax.axis_index("tm") == last

    @pl.when(lax.axis_index("tm") == last - 2)
    def _():
        own_parts_ref[0], own_parts_ref[1] = halves(composed(gain_ref))

    @pl.when(jnp.logical_not(here))
    def _():
        send_ref[...], found = offsets(means_ref, gain_ref, propagator_ref)
        for t, row in enumerate(found):
            offsets_ref[t : t + 1, :] = row

    @pl.when(here)
    def _():
        offsets_ref[...] = means_ref[...]
        send_ref[...] = means_ref[0:1, :]


def last_kernel(
    last, came_ref, operator_ref, inputs_ref, kept_ref, gain_ref, propagator_ref,
    means_ref, states_ref, send_ref,
):
    @pl.when(lax.axis_index("tm") == last)
    def _():
        steps = operator_ref.shape[0]
        state = came_ref[...]
        means, moved = [], []
        for t in range(steps):
            state = times([operator_ref[t]], state) + inputs_ref[t : t + 1, :]
            means_ref[t : t + 1, :] = state
            means.append(state)
            if t < steps - 1:
                moved.append(times([propagator_ref[...]], state))
        states_ref[steps - 1 : steps, :] = state
        for t in reversed(range(steps - 1)):
            left, state = times([gain_ref[t]], moved[t], state)
            state = state + (means[t] - left)
            states_ref[t : t + 1, :] = state
        send_ref[...] = state

    @pl.when(lax.axis_index("tm") != last)
    def _():
        means_ref[...] = kept_ref[...]
        states_ref[...] = kept_ref[...]
        send_ref[...] = came_ref[...]


def smooth(state, gain_ref, offsets_ref, put):
    for t in reversed(range(gain_ref.shape[0])):
        state = times([gain_ref[t]], state) + offsets_ref[t : t + 1, :]
        put(t, state)


def parts_times(parts_ref, row_ref):
    return times([parts_ref[0], parts_ref[1]], row_ref[...])


def first_back_kernel(
    place, last_ref, far_offset_ref, far_parts_ref, own_parts_ref, left_ref, came_ref, entry_ref, send_ref
):
    here = lax.axis_index("tm") == place

    @pl.when(here)
    def _():
        entry_ref[...] = parts_times(far_parts_ref, last_ref) + far_offset_ref[...]
        send_ref[...] = parts_times(own_parts_ref, entry_ref) + left_ref[...]

    @pl.when(jnp.logical_not(here))
    def _():
        entry_ref[...] = last_ref[...]
        send_ref[...] = came_ref[...]


def second_back_kernel(
    last,
    three_ref,
    one_ref,
    entry_ref,
    skip_offset_ref,
    skip_parts_ref,
    pair_parts_ref,
    pair_offset_ref,
    gain_ref,
    offsets_ref,
    kept_ref,
    came_ref,
    states_ref,
    next_ref,
    send_ref,
):
    here = lax.axis_index("tm")

    def put(t, state):
        states_ref[t : t + 1, :] = state

    @pl.when(here == last - 5)
    def _():
        state = parts_times(skip_parts_ref, three_ref) + skip_offset_ref[...]
        next_ref[...] = state
        send_ref[...] = times([pair_parts_ref[0], pair_parts_ref[1]], state) + pair_offset_ref[...]
        states_ref[...] = kept_ref[...]

    @pl.when(here != last - 5)
    def _():
        send_ref[...] = came_ref[...]
        next_ref[...] = entry_ref[...]

    @pl.when(here == last - 2)
    def _():
        smooth(entry_ref[...], gain_ref, offsets_ref, put)

    @pl.when((here == last - 3) | (here == last - 1))
    def _():
        smooth(jnp.where(here == last - 1, three_ref[...], one_ref[...]), gain_ref, offsets_ref, put)
        send_ref[...] = states_ref[0:1, :]

    @pl.when((here == last) | (here == last - 4) | (here < last - 5))
    def _():
        states_ref[...] = kept_ref[...]


def back_kernel(
    target,
    stray,
    two_ref,
    one_ref,
    entry_ref,
    near_offset_ref,
    near_parts_ref,
    pair_parts_ref,
    pair_offset_ref,
    gain_ref,
    offsets_ref,
    kept_ref,
    came_ref,
    states_ref,
    next_ref,
    send_ref,
):
    here = lax.axis_index("tm")

    def put(t, state):
        states_ref[t : t + 1, :] = state

    @pl.when(here == target)
    def _():
        send_ref[...] = times([pair_parts_ref[0], pair_parts_ref[1]], two_ref[...]) + pair_offset_ref[...]
        next_ref[...] = two_ref[...]
        states_ref[...] = kept_ref[...]

    @pl.when(here != target)
    def _():
        send_ref[...] = came_ref[...]
        next_ref[...] = entry_ref[...]

    @pl.when(here == target + 2)
    def _():
        state = times([near_parts_ref[0], near_parts_ref[1]], entry_ref[...]) + near_offset_ref[...]
        smooth(state, gain_ref, offsets_ref, put)

    @pl.when((here == target + 1) | (here == stray))
    def _():
        smooth(jnp.where(here == stray, two_ref[...], one_ref[...]), gain_ref, offsets_ref, put)
        send_ref[...] = states_ref[0:1, :]

    @pl.when((here > target + 2) & (here != stray) | (here < target))
    def _():
        states_ref[...] = kept_ref[...]


def final_kernel(
    stray,
    two_ref,
    one_ref,
    entry_ref,
    near_offset_ref,
    near_parts_ref,
    late_offset_ref,
    late_parts_ref,
    gain_ref,
    offsets_ref,
    kept_ref,
    means_ref,
    result_ref,
    states_ref,
):
    here = lax.axis_index("tm")
    for t in range(means_ref.shape[0]):
        result_ref[t] = means_ref[t : t + 1, :]

    def put(t, state):
        states_ref[t] = state

    @pl.when(here == 0)
    def _():
        smooth(parts_times(late_parts_ref, two_ref) + late_offset_ref[...], gain_ref, offsets_ref, put)

    @pl.when(here == 2)
    def _():
        state = times([near_parts_ref[0], near_parts_ref[1]], entry_ref[...]) + near_offset_ref[...]
        smooth(state, gain_ref, offsets_ref, put)

    @pl.when((here == 1) | (here == stray))
    def _():
        smooth(jnp.where(here == stray, two_ref[...], one_ref[...]), gain_ref, offsets_ref, put)

    @pl.when((here > 2) & (here != stray))
    def _():
        for t in range(kept_ref.shape[0]):
            states_ref[t] = kept_ref[t : t + 1, :]


def call(kernel, name, outs, *args, cost=1.0):
    return pl.pallas_call(
        kernel,
        out_shape=[
            jax.ShapeDtypeStruct(shape, jnp.bfloat16 if len(shape) == 3 and shape[1] > 1 else jnp.float32)
            for shape in outs
        ],
        in_specs=[VMEM] * len(args),
        out_specs=[VMEM] * len(outs),
        compiler_params=PARAMS,
        cost_estimate=pl.CostEstimate(flops=int(cost * 1e9), bytes_accessed=2**12, transcendentals=0),
        name=name,
    )(*args)


def pass_row(row, rings, places):
    route = {}
    for place in range(places):
        for core in range(2):
            route[place * 2 + core] = place * 2 + 1 - core
    for ring in rings:
        for i, place in enumerate(ring):
            for core in range(2):
                route[place * 2 + core] = ring[(i + 1) % len(ring)] * 2 + core
    return lax.ppermute(row, ("tm", "block"), sorted(route.items()))


def ring_up(place, places):
    if place == 0:
        return (0, 1, 3)
    if place % 2 and place >= places - 5 and place < places - 1:
        return (place, place + 1, place + 2)
    if place % 2 or place == places - 2:
        return (place, place + 1)
    return (place, place + 1, place - 2)


def local(
    scaled_residual_maps,
    measurement_stencil,
    observed_partition,
    active_probe_total,
    filtering_operator,
    updated_covariance,
    backward_factor,
    propagator,
    initial_mean,
):
    steps, size = filtering_operator.shape[0], filtering_operator.shape[-1]
    places = lax.axis_size("tm")
    many, one = (steps, size), (1, size)
    operator = filtering_operator.reshape(steps, size, size)
    covariance = updated_covariance.reshape(steps, size, size)
    gain = backward_factor.reshape(steps, size, size)
    last = places - 1
    matrix = propagator.reshape(size, size)
    square, parts, result = (size, size), (2, size, size), (steps, 1, size)
    sensors = (scaled_residual_maps, measurement_stencil, observed_partition, active_probe_total)
    mine, other = sensor_info((), *sensors)

    def compose(after, *senders):
        return call(functools.partial(compose_kernel, senders), "compose", (square,), after, gain, cost=0.01)[0]

    near_senders = range(3, last - 3, 2)
    inputs, means, send = call(
        start_kernel, "start", (many, many, (8, size)), mine, other, covariance, operator, initial_mean, cost=0.5
    )
    first = lax.ppermute(
        compose(send, last - 1, *near_senders), "tm", [(place, place - 1) for place in (*near_senders, last - 1)]
    )
    skip = lax.ppermute(compose(send, last - 3), "tm", [(last - 3, last - 5)])
    for place in range(1, places):
        came = pass_row(send, [ring_up(place - 1, places)], places)
        if place == 1:
            mine, other = sensor_info((send,), *sensors)
            inputs, means, send = call(
                first_hop_kernel, "forward", (many, many, one),
                came, mine, other, covariance, operator, inputs, means, cost=COSTS[1],
            )
            continue
        if place == 2:
            late = call(
                functools.partial(late_kernel, (1,)), "late", ((size + 8, size),), means, gain, matrix,
                cost=0.5,
            )[0]
            late = lax.ppermute(late, "tm", [(1, 0)])
        if place < last:
            means, send = call(
                functools.partial(hop_kernel, place), "forward", (many, one), came, operator, inputs, means,
                cost=COSTS[2] if place == 2 else 0.5,
            )
    offset_rows, left, own_parts = call(
        functools.partial(offsets_kernel, last), "offsets", (many, one, parts), means, gain, matrix
    )
    first_offset = pass_row(left, [(place - 1, place) for place in (*near_senders, last - 1)], places)
    means, states, send = call(
        functools.partial(last_kernel, last),
        "last",
        (many, many, one),
        came,
        operator,
        inputs,
        means,
        gain,
        matrix,
        cost=0.5,
    )
    came = pass_row(send, [(last, last - 2)], places)

    far_parts, again = call(
        functools.partial(split_kernel, last - 2), "split", (parts, one), first, left, cost=0.05
    )
    skip_offset = pass_row(again, [(last - 3, last - 5)], places)
    entry, send = call(
        functools.partial(first_back_kernel, last - 2), "first_back", (one, one),
        came, first_offset, far_parts, own_parts, left, send,
        cost=COSTS[3],
    )
    one_up = pass_row(send, [(last - 2, last - 3)], places)
    three = pass_row(send, [(last - 2, last - 5), (last, last - 1)], places)
    near_parts, pair_parts, pair_offset, skip_parts = call(
        functools.partial(pair_kernel, tuple(place - 1 for place in near_senders), last - 5),
        "pair",
        (parts, parts, one, parts),
        first,
        skip,
        gain,
        left,
        first_offset,
        cost=0.05,
    )
    states, entry, send = call(
        functools.partial(second_back_kernel, last),
        "second_back",
        (many, one, one),
        three,
        one_up,
        entry,
        skip_offset,
        skip_parts,
        pair_parts,
        pair_offset,
        gain,
        offset_rows,
        states,
        send,
        cost=COSTS[4],
    )
    stray = last - 4
    for target in range(last - 7, -1, -2):
        rings = [(target + 2, target)] + ([(stray + 1, stray)] if stray > 0 else [])
        one_up = pass_row(send, [(target + 2, target + 1)], places)
        two = pass_row(send, rings, places)
        if target:
            states, entry, send = call(
                functools.partial(back_kernel, target, stray), "back", (many, one, one),
                two, one_up, entry, first_offset, near_parts, pair_parts, pair_offset, gain, offset_rows, states,
                send,
            )
        else:
            late_parts, late_offset = call(
                functools.partial(late_split_kernel, 0), "late_split", (parts, one), late, send, cost=0.05
            )
            means, states = call(
                functools.partial(final_kernel, stray), "final", (result, result),
                two, one_up, entry, first_offset, near_parts, late_offset, late_parts, gain, offset_rows, states, means,
            )
        stray = -1
    return means, states


def solution(mesh):
    placed = (
        P(("groups", "tm"), "block", None, None),
        P(),
        P(("groups", "tm"), "block"),
        P(("groups", "tm"), "block"),
        P(("groups", "tm"), "block", None, None),
        P(("groups", "tm"), "block", None, None),
        P(("groups", "tm"), "block", None, None),
        P("block", None, None),
        P(("groups", "block"), None),
    )
    return jax.shard_map(
        local,
        mesh=mesh,
        in_specs=placed,
        out_specs=(P(("groups", "tm"), "block", None), P(("groups", "tm"), "block", None)),
        check_vma=False,
    )
```

```python
import functools

import jax
import jax.numpy as jnp
from jax import lax
from jax.experimental import pallas as pl
from jax.experimental.pallas import tpu as pltpu
from jax.sharding import PartitionSpec as P

GH = 16
MAP_COPIES = 4
COSTS = (60.0, 2.5, 2.5, 6.0, 0.5)
VMEM = pl.BlockSpec(memory_space=pltpu.VMEM)
PARAMS = pltpu.CompilerParams(vmem_limit_bytes=16 * 2**20)


def pieces(rows, count=3):
    height = -(-len(rows) * count // 8) * 8
    at = lax.broadcasted_iota(jnp.int32, (height, rows[0].shape[1]), 0)
    block = jnp.zeros(at.shape, jnp.float32)
    for k, rest in enumerate(rows):
        for i in range(count):
            piece = rest.astype(jnp.bfloat16).astype(jnp.float32)
            block = jnp.where(at == k * count + i, piece, block)
            rest = rest - piece
    return block.astype(jnp.bfloat16)


def times(matrices, *rows):
    block = pieces(rows)
    product = sum(
        lax.dot_general(block, matrix, (((1,), (1,)), ((), ())), preferred_element_type=jnp.float32)
        for matrix in matrices
    )
    found = [jnp.sum(product[3 * k : 3 * k + 3, :], axis=0, keepdims=True) for k in range(len(rows))]
    return found if len(rows) > 1 else found[0]


def info_kernel(zero, *refs):
    @pl.when((lax.axis_index("tm") == 0) == zero)
    def _():
        place_info(*(refs if zero else refs[1:]))


def place_info(
    maps_hbm,
    stencil_hbm,
    observed_hbm,
    active_hbm,
    mine_ref,
    theirs_ref,
    maps,
    stencil_ref,
    observed_ref,
    active_ref,
    taps,
    map_sems,
    sems,
):
    steps, rows, cells = maps.shape
    slots = observed_ref.shape[1]
    side, _, channels = stencil_ref.shape
    half = side // 2
    small = []
    for i, (source, target) in enumerate(
        ((stencil_hbm, stencil_ref), (observed_hbm, observed_ref), (active_hbm, active_ref))
    ):
        small.append(pltpu.make_async_copy(source, target, sems.at[i]))
        small[-1].start()
    part = rows // MAP_COPIES
    copies = []
    for t in range(steps):
        for i in range(MAP_COPIES):
            at = pl.ds(i * part, part)
            copies.append(
                pltpu.make_async_copy(maps_hbm.at[t, at], maps.at[t, at], map_sems.at[t, i])
            )
            copies[-1].start()

    repeat = jnp.where(
        lax.broadcasted_iota(jnp.int32, (channels, rows), 1) % channels
        == lax.broadcasted_iota(jnp.int32, (channels, rows), 0),
        1.0,
        0.0,
    ).astype(jnp.bfloat16)
    taps[...] = jnp.zeros_like(taps)
    spread = jnp.where(
        lax.broadcasted_iota(jnp.int32, (slots, rows), 1) // channels
        == lax.broadcasted_iota(jnp.int32, (slots, rows), 0),
        1.0,
        0.0,
    ).astype(jnp.bfloat16)

    cell = lax.broadcasted_iota(jnp.int32, (8, cells), 1)
    width = cells // GH
    down = cell // width
    across = cell % width
    tap = lax.broadcasted_iota(jnp.int32, (8, cells), 0)
    column = across - tap + half
    column_inside = (column >= 0) & (column < width) & (tap < side)
    me = lax.axis_index("block")
    for copy in small:
        copy.wait()
    for p in range(side):
        taps[p * 8 : p * 8 + side, :] = jnp.dot(
            stencil_ref[p], repeat, preferred_element_type=jnp.float32
        )
    for t in range(steps):
        owner = lax.broadcasted_iota(jnp.int32, (8, slots), 0)
        slot = lax.broadcasted_iota(jnp.int32, (8, slots), 1)
        live = (observed_ref[t : t + 1, :] == owner) & (slot < active_ref[0:1, t : t + 1])
        weight = jnp.dot(
            jnp.where(live, 1.0, 0.0).astype(jnp.bfloat16), spread, preferred_element_type=jnp.float32
        )
        left = jnp.concatenate([taps[...] * weight[b : b + 1, :] for b in range(2)], axis=0)
        for copy in copies[t * MAP_COPIES : (t + 1) * MAP_COPIES]:
            copy.wait()
        shifted = jnp.dot(left.astype(jnp.bfloat16), maps[t], preferred_element_type=jnp.float32)
        found = []
        for b in range(2):
            total = jnp.zeros((8, cells), jnp.float32)
            for p in range(side):
                at = (b * side + p) * 8
                part = pltpu.roll(shifted[at : at + 8, :], ((p - half) * width) % cells, 1)
                row = down - p + half
                total = total + jnp.where((row >= 0) & (row < GH), part, 0.0)
            sides = jnp.zeros((8, cells), jnp.float32)
            for q in range(side):
                part = pltpu.roll(total, (q - half) % cells, 1)
                sides = jnp.where(column_inside & (tap == q), part, sides)
            found.append(jnp.sum(sides, axis=0, keepdims=True))
        mine_ref[t : t + 1, :] = jnp.where(me == 0, found[0], found[1])
        theirs_ref[t : t + 1, :] = jnp.where(me == 0, found[1], found[0])


def sensor_info(after, scaled_residual_maps, measurement_stencil, observed_partition, active_probe_total):
    zero = not after
    steps, slots, channels, cells = scaled_residual_maps.shape
    side = measurement_stencil.shape[1]
    mine, theirs = pl.pallas_call(
        functools.partial(info_kernel, zero),
        out_shape=[jax.ShapeDtypeStruct((steps, cells), jnp.float32)] * 2,
        in_specs=[VMEM] * len(after) + [pl.BlockSpec(memory_space=pltpu.HBM)] * 4,
        out_specs=[VMEM] * 2,
        scratch_shapes=[
            pltpu.VMEM((steps, slots * channels, cells), jnp.bfloat16),
            pltpu.VMEM((side, side, channels), jnp.bfloat16),
            pltpu.VMEM((steps, slots), jnp.int32),
            pltpu.VMEM((1, steps), jnp.int32),
            pltpu.VMEM((side * 8, slots * channels), jnp.float32),
            pltpu.SemaphoreType.DMA((steps, MAP_COPIES)),
            pltpu.SemaphoreType.DMA((3,)),
        ],
        compiler_params=PARAMS,
        cost_estimate=pl.CostEstimate(flops=10**6 if zero else int(COSTS[0] * 1e9), bytes_accessed=2**12, transcendentals=0),
        name="sensor_info",
    )(
        *after,
        *(
            pltpu.with_memory_space_constraint(array, pltpu.HBM)
            for array in (
                scaled_residual_maps.reshape(steps, slots * channels, cells),
                measurement_stencil.transpose(1, 2, 0),
                observed_partition,
                active_probe_total.T,
            )
        )
    )
    return mine, lax.ppermute(theirs, "block", [(0, 1), (1, 0)])


def start_kernel(mine_ref, other_ref, covariance_ref, operator_ref, start_ref, inputs_ref, states_ref, send_ref):
    here = lax.axis_index("tm") == 0

    @pl.when(here)
    def _():
        state = start_ref[...]
        for t in range(mine_ref.shape[0]):
            drive = times([covariance_ref[t]], mine_ref[t : t + 1, :] + other_ref[t : t + 1, :])
            inputs_ref[t : t + 1, :] = drive
            state = times([operator_ref[t]], state) + drive
            states_ref[t : t + 1, :] = state
        send_ref[...] = jnp.broadcast_to(state, send_ref.shape)

    @pl.when(jnp.logical_not(here))
    def _():
        inputs_ref[...] = jnp.zeros_like(inputs_ref)
        states_ref[...] = jnp.zeros_like(states_ref)
        send_ref[...] = jnp.zeros_like(send_ref)


def first_hop_kernel(
    came_ref, mine_ref, other_ref, covariance_ref, operator_ref, kept_inputs_ref, kept_ref,
    inputs_ref, states_ref, send_ref,
):
    here = lax.axis_index("tm")

    @pl.when(here == 0)
    def _():
        inputs_ref[...] = kept_inputs_ref[...]

    @pl.when(here != 0)
    def _():
        for t in range(mine_ref.shape[0]):
            info = mine_ref[t : t + 1, :] + other_ref[t : t + 1, :]
            inputs_ref[t : t + 1, :] = times([covariance_ref[t]], info)

    @pl.when(here == 1)
    def _():
        state = came_ref[0:1, :]
        for t in range(operator_ref.shape[0]):
            state = times([operator_ref[t]], state) + inputs_ref[t : t + 1, :]
            states_ref[t : t + 1, :] = state
        send_ref[...] = state

    @pl.when(here != 1)
    def _():
        states_ref[...] = kept_ref[...]
        send_ref[...] = came_ref[0:1, :]


def hop_kernel(turn, came_ref, matrices_ref, offsets_ref, kept_ref, states_ref, send_ref):
    here = lax.axis_index("tm") == turn

    @pl.when(here)
    def _():
        state = came_ref[...]
        for t in range(matrices_ref.shape[0]):
            state = times([matrices_ref[t]], state) + offsets_ref[t : t + 1, :]
            states_ref[t : t + 1, :] = state
        send_ref[...] = state

    @pl.when(jnp.logical_not(here))
    def _():
        states_ref[...] = kept_ref[...]
        send_ref[...] = came_ref[...]


def halves(matrix):
    high = matrix.astype(jnp.bfloat16)
    return [high, (matrix - high.astype(jnp.float32)).astype(jnp.bfloat16)]


def composed(gain_ref):
    product = gain_ref[0]
    for t in range(1, gain_ref.shape[0]):
        product = sum(
            jnp.dot(part, gain_ref[t], preferred_element_type=jnp.float32)
            for part in (halves(product) if t > 1 else [product])
        )
    return product.astype(jnp.float32)


def compose_kernel(senders, after_ref, gain_ref, composed_ref):
    del after_ref
    here = lax.axis_index("tm")
    sends = functools.reduce(jnp.logical_or, [here == place for place in senders])

    @pl.when(sends)
    def _():
        composed_ref[...] = composed(gain_ref)


def late_kernel(senders, means_ref, gain_ref, propagator_ref, composed_ref):
    size = gain_ref.shape[1]
    here = lax.axis_index("tm")
    sends = functools.reduce(jnp.logical_or, [here == place for place in senders])

    @pl.when(sends)
    def _():
        composed_ref[:size, :] = composed(gain_ref)
        composed_ref[size:, :] = jnp.zeros((composed_ref.shape[0] - size, size), jnp.float32)
        composed_ref[size : size + 1, :] = offsets(means_ref, gain_ref, propagator_ref)[0]


def offsets(means_ref, gain_ref, propagator_ref):
    steps = means_ref.shape[0]
    means = [means_ref[t : t + 1, :] for t in range(steps)]
    moved = times([propagator_ref[...]], *means)
    state = jnp.zeros_like(means[0])
    found = [None] * steps
    for t in reversed(range(steps)):
        left, state = times([gain_ref[t]], moved[t], state)
        found[t] = means[t] - left
        state = state + found[t]
    return state, found


def pair_kernel(
    places,
    skip_place,
    near_ref,
    skip_ref,
    gain_ref,
    left_ref,
    near_offset_ref,
    near_parts_ref,
    pair_parts_ref,
    pair_offset_ref,
    skip_parts_ref,
):
    here = lax.axis_index("tm")

    @pl.when(functools.reduce(jnp.logical_or, [here == place for place in places]))
    def _():
        near = halves(near_ref[...])
        own = halves(composed(gain_ref))
        near_parts_ref[0], near_parts_ref[1] = near
        pair_parts_ref[0], pair_parts_ref[1] = halves(
            jnp.dot(own[0], near[0], preferred_element_type=jnp.float32)
            + jnp.dot(own[0], near[1], preferred_element_type=jnp.float32)
            + jnp.dot(own[1], near[0], preferred_element_type=jnp.float32)
        )
        pair_offset_ref[...] = times(own, near_offset_ref[...]) + left_ref[...]

    @pl.when(here == skip_place)
    def _():
        skip_parts_ref[0], skip_parts_ref[1] = halves(skip_ref[...])


def late_split_kernel(place, late_ref, after_ref, parts_ref, offset_ref):
    del after_ref
    size = late_ref.shape[1]

    @pl.when(lax.axis_index("tm") == place)
    def _():
        parts_ref[0], parts_ref[1] = halves(late_ref[:size, :])
        offset_ref[...] = late_ref[size : size + 1, :]


def split_kernel(place, matrix_ref, parts_ref):
    @pl.when(lax.axis_index("tm") == place)
    def _():
        parts_ref[0], parts_ref[1] = halves(matrix_ref[...])


def offsets_kernel(last, means_ref, gain_ref, propagator_ref, offsets_ref, send_ref, own_parts_ref):
    here = lax.axis_index("tm") == last

    @pl.when(lax.axis_index("tm") == last - 2)
    def _():
        own_parts_ref[0], own_parts_ref[1] = halves(composed(gain_ref))

    @pl.when(jnp.logical_not(here))
    def _():
        send_ref[...], found = offsets(means_ref, gain_ref, propagator_ref)
        for t, row in enumerate(found):
            offsets_ref[t : t + 1, :] = row

    @pl.when(here)
    def _():
        offsets_ref[...] = means_ref[...]
        send_ref[...] = means_ref[0:1, :]


def last_kernel(
    last, came_ref, operator_ref, inputs_ref, kept_ref, gain_ref, propagator_ref,
    means_ref, states_ref, send_ref,
):
    @pl.when(lax.axis_index("tm") == last)
    def _():
        steps = operator_ref.shape[0]
        state = came_ref[...]
        means, moved = [], []
        for t in range(steps):
            state = times([operator_ref[t]], state) + inputs_ref[t : t + 1, :]
            means_ref[t : t + 1, :] = state
            means.append(state)
            if t < steps - 1:
                moved.append(times([propagator_ref[...]], state))
        states_ref[steps - 1 : steps, :] = state
        for t in reversed(range(steps - 1)):
            left, state = times([gain_ref[t]], moved[t], state)
            state = state + (means[t] - left)
            states_ref[t : t + 1, :] = state
        send_ref[...] = state

    @pl.when(lax.axis_index("tm") != last)
    def _():
        means_ref[...] = kept_ref[...]
        states_ref[...] = kept_ref[...]
        send_ref[...] = came_ref[...]


def smooth(state, gain_ref, offsets_ref, put):
    for t in reversed(range(gain_ref.shape[0])):
        state = times([gain_ref[t]], state) + offsets_ref[t : t + 1, :]
        put(t, state)


def parts_times(parts_ref, row_ref):
    return times([parts_ref[0], parts_ref[1]], row_ref[...])


def first_back_kernel(
    place, last_ref, far_offset_ref, far_parts_ref, own_parts_ref, left_ref, came_ref, entry_ref, send_ref
):
    here = lax.axis_index("tm")

    @pl.when(here == place)
    def _():
        entry_ref[...] = parts_times(far_parts_ref, last_ref) + far_offset_ref[...]
        send_ref[...] = parts_times(own_parts_ref, entry_ref) + left_ref[...]

    @pl.when(here != place)
    def _():
        entry_ref[...] = last_ref[...]
        send_ref[...] = jnp.where(here == place - 1, left_ref[...], came_ref[...])


def second_back_kernel(
    last,
    three_ref,
    one_ref,
    entry_ref,
    skip_parts_ref,
    pair_parts_ref,
    pair_offset_ref,
    gain_ref,
    offsets_ref,
    kept_ref,
    came_ref,
    states_ref,
    next_ref,
    send_ref,
):
    here = lax.axis_index("tm")

    def put(t, state):
        states_ref[t : t + 1, :] = state

    @pl.when(here == last - 5)
    def _():
        state = parts_times(skip_parts_ref, three_ref) + one_ref[...]
        next_ref[...] = state
        send_ref[...] = times([pair_parts_ref[0], pair_parts_ref[1]], state) + pair_offset_ref[...]
        states_ref[...] = kept_ref[...]

    @pl.when(here != last - 5)
    def _():
        send_ref[...] = came_ref[...]
        next_ref[...] = entry_ref[...]

    @pl.when(here == last - 2)
    def _():
        smooth(entry_ref[...], gain_ref, offsets_ref, put)

    @pl.when((here == last - 3) | (here == last - 1))
    def _():
        smooth(jnp.where(here == last - 1, three_ref[...], one_ref[...]), gain_ref, offsets_ref, put)
        send_ref[...] = states_ref[0:1, :]

    @pl.when((here == last) | (here == last - 4) | (here < last - 5))
    def _():
        states_ref[...] = kept_ref[...]


def back_kernel(
    target,
    stray,
    two_ref,
    one_ref,
    entry_ref,
    near_offset_ref,
    near_parts_ref,
    pair_parts_ref,
    pair_offset_ref,
    gain_ref,
    offsets_ref,
    kept_ref,
    came_ref,
    states_ref,
    next_ref,
    send_ref,
):
    here = lax.axis_index("tm")

    def put(t, state):
        states_ref[t : t + 1, :] = state

    @pl.when(here == target)
    def _():
        send_ref[...] = times([pair_parts_ref[0], pair_parts_ref[1]], two_ref[...]) + pair_offset_ref[...]
        next_ref[...] = two_ref[...]
        states_ref[...] = kept_ref[...]

    @pl.when(here != target)
    def _():
        send_ref[...] = came_ref[...]
        next_ref[...] = entry_ref[...]

    @pl.when(here == target + 2)
    def _():
        state = times([near_parts_ref[0], near_parts_ref[1]], entry_ref[...]) + near_offset_ref[...]
        smooth(state, gain_ref, offsets_ref, put)

    @pl.when((here == target + 1) | (here == stray))
    def _():
        smooth(jnp.where(here == stray, two_ref[...], one_ref[...]), gain_ref, offsets_ref, put)
        send_ref[...] = states_ref[0:1, :]

    @pl.when((here > target + 2) & (here != stray) | (here < target))
    def _():
        states_ref[...] = kept_ref[...]


def final_kernel(
    stray,
    two_ref,
    one_ref,
    entry_ref,
    near_offset_ref,
    near_parts_ref,
    late_offset_ref,
    late_parts_ref,
    gain_ref,
    offsets_ref,
    kept_ref,
    means_ref,
    result_ref,
    states_ref,
):
    here = lax.axis_index("tm")
    for t in range(means_ref.shape[0]):
        result_ref[t] = means_ref[t : t + 1, :]

    def put(t, state):
        states_ref[t] = state

    @pl.when(here == 0)
    def _():
        smooth(parts_times(late_parts_ref, two_ref) + late_offset_ref[...], gain_ref, offsets_ref, put)

    @pl.when(here == 2)
    def _():
        state = times([near_parts_ref[0], near_parts_ref[1]], entry_ref[...]) + near_offset_ref[...]
        smooth(state, gain_ref, offsets_ref, put)

    @pl.when((here == 1) | (here == stray))
    def _():
        smooth(jnp.where(here == stray, two_ref[...], one_ref[...]), gain_ref, offsets_ref, put)

    @pl.when((here > 2) & (here != stray))
    def _():
        for t in range(kept_ref.shape[0]):
            states_ref[t] = kept_ref[t : t + 1, :]


def call(kernel, name, outs, *args, cost=1.0):
    return pl.pallas_call(
        kernel,
        out_shape=[
            jax.ShapeDtypeStruct(shape, jnp.bfloat16 if len(shape) == 3 and shape[1] > 1 else jnp.float32)
            for shape in outs
        ],
        in_specs=[VMEM] * len(args),
        out_specs=[VMEM] * len(outs),
        compiler_params=PARAMS,
        cost_estimate=pl.CostEstimate(flops=int(cost * 1e9), bytes_accessed=2**12, transcendentals=0),
        name=name,
    )(*args)


def pass_row(row, rings, places):
    route = {}
    for place in range(places):
        for core in range(2):
            route[place * 2 + core] = place * 2 + 1 - core
    for ring in rings:
        for i, place in enumerate(ring):
            for core in range(2):
                route[place * 2 + core] = ring[(i + 1) % len(ring)] * 2 + core
    return lax.ppermute(row, ("tm", "block"), sorted(route.items()))


def ring_up(place, places):
    if place % 2 and place >= places - 5 and place < places - 1:
        return (place, place + 1, place + 2)
    if place % 2 or place == places - 2:
        return (place, place + 1)
    return (place, place + 1, place - 2)


def local(
    scaled_residual_maps,
    measurement_stencil,
    observed_partition,
    active_probe_total,
    filtering_operator,
    updated_covariance,
    backward_factor,
    propagator,
    initial_mean,
):
    steps, size = filtering_operator.shape[0], filtering_operator.shape[-1]
    places = lax.axis_size("tm")
    many, one = (steps, size), (1, size)
    operator = filtering_operator.reshape(steps, size, size)
    covariance = updated_covariance.reshape(steps, size, size)
    gain = backward_factor.reshape(steps, size, size)
    last = places - 1
    matrix = propagator.reshape(size, size)
    square, parts, result = (size, size), (2, size, size), (steps, 1, size)
    sensors = (scaled_residual_maps, measurement_stencil, observed_partition, active_probe_total)
    mine, other = sensor_info((), *sensors)

    def compose(after, *senders):
        return call(functools.partial(compose_kernel, senders), "compose", (square,), after, gain, cost=0.01)[0]

    near_senders = range(3, last - 3, 2)
    inputs, means, send = call(
        start_kernel, "start", (many, many, (8, size)), mine, other, covariance, operator, initial_mean, cost=0.5
    )
    first = lax.ppermute(
        compose(send, last - 1, *near_senders), "tm", [(place, place - 1) for place in (*near_senders, last - 1)]
    )
    skip = lax.ppermute(compose(send, last - 3), "tm", [(last - 3, last - 5)])
    for place in range(1, places):
        if place == 1:
            came = lax.ppermute(send, "tm", [(0, 1)])
            mine, other = sensor_info((send,), *sensors)
            inputs, means, send = call(
                first_hop_kernel, "forward", (many, many, one),
                came, mine, other, covariance, operator, inputs, means, cost=COSTS[1],
            )
            continue
        came = pass_row(send, [ring_up(place - 1, places)], places)
        if place == 2:
            late = call(
                functools.partial(late_kernel, (1,)), "late", ((size + 8, size),), means, gain, matrix,
                cost=0.5,
            )[0]
            late = lax.ppermute(late, "tm", [(1, 0)])
        if place < last:
            means, send = call(
                functools.partial(hop_kernel, place), "forward", (many, one), came, operator, inputs, means,
                cost=COSTS[2] if place == 2 else 0.5,
            )
    offset_rows, left, own_parts = call(
        functools.partial(offsets_kernel, last), "offsets", (many, one, parts), means, gain, matrix
    )
    first_offset = pass_row(left, [(place - 1, place) for place in (*near_senders, last - 1)], places)
    means, states, send = call(
        functools.partial(last_kernel, last),
        "last",
        (many, many, one),
        came,
        operator,
        inputs,
        means,
        gain,
        matrix,
        cost=0.5,
    )
    came = pass_row(send, [(last, last - 2)], places)

    (far_parts,) = call(functools.partial(split_kernel, last - 2), "split", (parts,), first, cost=0.05)
    entry, send = call(
        functools.partial(first_back_kernel, last - 2), "first_back", (one, one),
        came, first_offset, far_parts, own_parts, left, send,
        cost=COSTS[3],
    )
    one_up = pass_row(send, [(last - 2, last - 3, last - 5, last - 4)], places)
    three = pass_row(send, [(last - 2, last - 5), (last, last - 1)], places)
    near_parts, pair_parts, pair_offset, skip_parts = call(
        functools.partial(pair_kernel, tuple(place - 1 for place in near_senders), last - 5),
        "pair",
        (parts, parts, one, parts),
        first,
        skip,
        gain,
        left,
        first_offset,
        cost=0.05,
    )
    states, entry, send = call(
        functools.partial(second_back_kernel, last),
        "second_back",
        (many, one, one),
        three,
        one_up,
        entry,
        skip_parts,
        pair_parts,
        pair_offset,
        gain,
        offset_rows,
        states,
        send,
        cost=COSTS[4],
    )
    stray = last - 4
    for target in range(last - 7, -1, -2):
        rings = [(target + 2, target)] + ([(stray + 1, stray)] if stray > 0 else [])
        one_up = pass_row(send, [(target + 2, target + 1)], places)
        two = pass_row(send, rings, places)
        if target:
            states, entry, send = call(
                functools.partial(back_kernel, target, stray), "back", (many, one, one),
                two, one_up, entry, first_offset, near_parts, pair_parts, pair_offset, gain, offset_rows, states,
                send,
            )
        else:
            late_parts, late_offset = call(
                functools.partial(late_split_kernel, 0), "late_split", (parts, one), late, send, cost=0.05
            )
            means, states = call(
                functools.partial(final_kernel, stray), "final", (result, result),
                two, one_up, entry, first_offset, near_parts, late_offset, late_parts, gain, offset_rows, states, means,
            )
        stray = -1
    return means, states


def solution(mesh):
    placed = (
        P(("groups", "tm"), "block", None, None),
        P(),
        P(("groups", "tm"), "block"),
        P(("groups", "tm"), "block"),
        P(("groups", "tm"), "block", None, None),
        P(("groups", "tm"), "block", None, None),
        P(("groups", "tm"), "block", None, None),
        P("block", None, None),
        P(("groups", "block"), None),
    )
    return jax.shard_map(
        local,
        mesh=mesh,
        in_specs=placed,
        out_specs=(P(("groups", "tm"), "block", None), P(("groups", "tm"), "block", None)),
        check_vma=False,
    )
```

```python
import functools

import jax
import jax.numpy as jnp
from jax import lax
from jax.experimental import pallas as pl
from jax.experimental.pallas import tpu as pltpu
from jax.sharding import PartitionSpec as P

GH = 16
COSTS = (60.0, 2.5, 2.5, 6.0, 0.5)
VMEM = pl.BlockSpec(memory_space=pltpu.VMEM)
PARAMS = pltpu.CompilerParams(vmem_limit_bytes=16 * 2**20)


def pieces(rows, count=3):
    height = -(-len(rows) * count // 8) * 8
    at = lax.broadcasted_iota(jnp.int32, (height, rows[0].shape[1]), 0)
    block = jnp.zeros(at.shape, jnp.float32)
    for k, rest in enumerate(rows):
        for i in range(count):
            piece = rest.astype(jnp.bfloat16).astype(jnp.float32)
            block = jnp.where(at == k * count + i, piece, block)
            rest = rest - piece
    return block.astype(jnp.bfloat16)


def times(matrices, *rows):
    block = pieces(rows)
    product = sum(
        lax.dot_general(block, matrix, (((1,), (1,)), ((), ())), preferred_element_type=jnp.float32)
        for matrix in matrices
    )
    found = [jnp.sum(product[3 * k : 3 * k + 3, :], axis=0, keepdims=True) for k in range(len(rows))]
    return found if len(rows) > 1 else found[0]


def info_kernel(stencil_hbm, observed_hbm, active_hbm, maps_hbm, mine_ref, theirs_ref, *scratch):
    stencil_ref, observed_ref, active_ref, maps, taps, sems = scratch

    @pl.when(lax.axis_index("tm") == 0)
    def _():
        copies = []
        for i, (source, target) in enumerate(
            ((stencil_hbm, stencil_ref), (observed_hbm, observed_ref), (active_hbm, active_ref))
        ):
            copies.append(pltpu.make_async_copy(source, target, sems.at[i]))
        for t in range(maps.shape[0]):
            copies.append(pltpu.make_async_copy(maps_hbm.at[t], maps.at[t], sems.at[3 + t]))
        for copy in copies:
            copy.start()
        place_info(stencil_ref, observed_ref, active_ref, maps, mine_ref, theirs_ref, taps, copies)


def staged_info_kernel(after_ref, *refs):
    del after_ref

    @pl.when(lax.axis_index("tm") != 0)
    def _():
        place_info(*refs, [])


def place_info(stencil_ref, observed_ref, active_ref, maps, mine_ref, theirs_ref, taps, copies):
    steps, rows, cells = maps.shape
    slots = observed_ref.shape[1]
    side, _, channels = stencil_ref.shape
    half = side // 2

    repeat = jnp.where(
        lax.broadcasted_iota(jnp.int32, (channels, rows), 1) % channels
        == lax.broadcasted_iota(jnp.int32, (channels, rows), 0),
        1.0,
        0.0,
    ).astype(jnp.bfloat16)
    taps[...] = jnp.zeros_like(taps)
    spread = jnp.where(
        lax.broadcasted_iota(jnp.int32, (slots, rows), 1) // channels
        == lax.broadcasted_iota(jnp.int32, (slots, rows), 0),
        1.0,
        0.0,
    ).astype(jnp.bfloat16)

    cell = lax.broadcasted_iota(jnp.int32, (8, cells), 1)
    width = cells // GH
    down = cell // width
    across = cell % width
    tap = lax.broadcasted_iota(jnp.int32, (8, cells), 0)
    column = across - tap + half
    column_inside = (column >= 0) & (column < width) & (tap < side)
    me = lax.axis_index("block")
    for copy in copies[:3]:
        copy.wait()
    for p in range(side):
        taps[p * 8 : p * 8 + side, :] = jnp.dot(
            stencil_ref[p], repeat, preferred_element_type=jnp.float32
        )
    for t in range(steps):
        owner = lax.broadcasted_iota(jnp.int32, (8, slots), 0)
        slot = lax.broadcasted_iota(jnp.int32, (8, slots), 1)
        live = (observed_ref[t : t + 1, :] == owner) & (slot < active_ref[0:1, t : t + 1])
        weight = jnp.dot(
            jnp.where(live, 1.0, 0.0).astype(jnp.bfloat16), spread, preferred_element_type=jnp.float32
        )
        left = jnp.concatenate([taps[...] * weight[b : b + 1, :] for b in range(2)], axis=0)
        for copy in copies[3 + t : 4 + t]:
            copy.wait()
        shifted = jnp.dot(left.astype(jnp.bfloat16), maps[t], preferred_element_type=jnp.float32)
        found = []
        for b in range(2):
            total = jnp.zeros((8, cells), jnp.float32)
            for p in range(side):
                at = (b * side + p) * 8
                part = pltpu.roll(shifted[at : at + 8, :], ((p - half) * width) % cells, 1)
                row = down - p + half
                total = total + jnp.where((row >= 0) & (row < GH), part, 0.0)
            sides = jnp.zeros((8, cells), jnp.float32)
            for q in range(side):
                part = pltpu.roll(total, (q - half) % cells, 1)
                sides = jnp.where(column_inside & (tap == q), part, sides)
            found.append(jnp.sum(sides, axis=0, keepdims=True))
        mine_ref[t : t + 1, :] = jnp.where(me == 0, found[0], found[1])
        theirs_ref[t : t + 1, :] = jnp.where(me == 0, found[1], found[0])


def sensor_info(after, scaled_residual_maps, measurement_stencil, observed_partition, active_probe_total):
    steps, slots, channels, cells = scaled_residual_maps.shape
    side = measurement_stencil.shape[1]
    operands = (
        measurement_stencil.transpose(1, 2, 0),
        observed_partition,
        active_probe_total.T,
        scaled_residual_maps.reshape(steps, slots * channels, cells),
    )
    taps = pltpu.VMEM((side * 8, slots * channels), jnp.float32)
    if after:
        kernel, specs, scratch, cost = staged_info_kernel, [VMEM] * 5, [taps], int(COSTS[0] * 1e9)
    else:
        kernel, specs, cost = info_kernel, [pl.BlockSpec(memory_space=pltpu.HBM)] * 4, 10**6
        scratch = [
            *(pltpu.VMEM(array.shape, array.dtype) for array in operands),
            taps,
            pltpu.SemaphoreType.DMA((3 + steps,)),
        ]
        operands = [pltpu.with_memory_space_constraint(array, pltpu.HBM) for array in operands]
    mine, theirs = pl.pallas_call(
        kernel,
        out_shape=[jax.ShapeDtypeStruct((steps, cells), jnp.float32)] * 2,
        in_specs=specs,
        out_specs=[VMEM] * 2,
        scratch_shapes=scratch,
        compiler_params=PARAMS,
        cost_estimate=pl.CostEstimate(flops=cost, bytes_accessed=2**12, transcendentals=0),
        name="sensor_info",
    )(*after, *operands)
    return mine, lax.ppermute(theirs, "block", [(0, 1), (1, 0)])


def start_kernel(mine_ref, other_ref, covariance_ref, operator_ref, start_ref, inputs_ref, states_ref, send_ref):
    here = lax.axis_index("tm") == 0

    @pl.when(here)
    def _():
        state = start_ref[...]
        for t in range(mine_ref.shape[0]):
            drive = times([covariance_ref[t]], mine_ref[t : t + 1, :] + other_ref[t : t + 1, :])
            inputs_ref[t : t + 1, :] = drive
            state = times([operator_ref[t]], state) + drive
            states_ref[t : t + 1, :] = state
        send_ref[...] = jnp.broadcast_to(state, send_ref.shape)

    @pl.when(jnp.logical_not(here))
    def _():
        inputs_ref[...] = jnp.zeros_like(inputs_ref)
        states_ref[...] = jnp.zeros_like(states_ref)
        send_ref[...] = jnp.zeros_like(send_ref)


def first_hop_kernel(
    came_ref, mine_ref, other_ref, covariance_ref, operator_ref, kept_inputs_ref, kept_ref,
    inputs_ref, states_ref, send_ref,
):
    here = lax.axis_index("tm")

    @pl.when(here == 0)
    def _():
        inputs_ref[...] = kept_inputs_ref[...]

    @pl.when(here != 0)
    def _():
        for t in range(mine_ref.shape[0]):
            info = mine_ref[t : t + 1, :] + other_ref[t : t + 1, :]
            inputs_ref[t : t + 1, :] = times([covariance_ref[t]], info)

    @pl.when(here == 1)
    def _():
        state = came_ref[0:1, :]
        for t in range(operator_ref.shape[0]):
            state = times([operator_ref[t]], state) + inputs_ref[t : t + 1, :]
            states_ref[t : t + 1, :] = state
        send_ref[...] = state

    @pl.when(here != 1)
    def _():
        states_ref[...] = kept_ref[...]
        send_ref[...] = came_ref[0:1, :]


def hop_kernel(turn, came_ref, matrices_ref, offsets_ref, kept_ref, states_ref, send_ref):
    here = lax.axis_index("tm") == turn

    @pl.when(here)
    def _():
        state = came_ref[...]
        for t in range(matrices_ref.shape[0]):
            state = times([matrices_ref[t]], state) + offsets_ref[t : t + 1, :]
            states_ref[t : t + 1, :] = state
        send_ref[...] = state

    @pl.when(jnp.logical_not(here))
    def _():
        states_ref[...] = kept_ref[...]
        send_ref[...] = came_ref[...]


def halves(matrix):
    high = matrix.astype(jnp.bfloat16)
    return [high, (matrix - high.astype(jnp.float32)).astype(jnp.bfloat16)]


def composed(gain_ref):
    product = gain_ref[0]
    for t in range(1, gain_ref.shape[0]):
        product = sum(
            jnp.dot(part, gain_ref[t], preferred_element_type=jnp.float32)
            for part in (halves(product) if t > 1 else [product])
        )
    return product.astype(jnp.float32)


def compose_kernel(senders, after_ref, gain_ref, composed_ref):
    del after_ref
    here = lax.axis_index("tm")
    sends = functools.reduce(jnp.logical_or, [here == place for place in senders])

    @pl.when(sends)
    def _():
        composed_ref[...] = composed(gain_ref)


def late_kernel(senders, means_ref, gain_ref, propagator_ref, composed_ref):
    size = gain_ref.shape[1]
    here = lax.axis_index("tm")
    sends = functools.reduce(jnp.logical_or, [here == place for place in senders])

    @pl.when(sends)
    def _():
        composed_ref[:size, :] = composed(gain_ref)
        composed_ref[size:, :] = jnp.zeros((composed_ref.shape[0] - size, size), jnp.float32)
        composed_ref[size : size + 1, :] = offsets(means_ref, gain_ref, propagator_ref)[0]


def offsets(means_ref, gain_ref, propagator_ref):
    steps = means_ref.shape[0]
    means = [means_ref[t : t + 1, :] for t in range(steps)]
    moved = times([propagator_ref[...]], *means)
    state = jnp.zeros_like(means[0])
    found = [None] * steps
    for t in reversed(range(steps)):
        left, state = times([gain_ref[t]], moved[t], state)
        found[t] = means[t] - left
        state = state + found[t]
    return state, found


def pair_kernel(
    places,
    skip_place,
    near_ref,
    skip_ref,
    gain_ref,
    left_ref,
    near_offset_ref,
    near_parts_ref,
    pair_parts_ref,
    pair_offset_ref,
    skip_parts_ref,
):
    here = lax.axis_index("tm")

    @pl.when(functools.reduce(jnp.logical_or, [here == place for place in places]))
    def _():
        near = halves(near_ref[...])
        own = halves(composed(gain_ref))
        near_parts_ref[0], near_parts_ref[1] = near
        pair_parts_ref[0], pair_parts_ref[1] = halves(
            jnp.dot(own[0], near[0], preferred_element_type=jnp.float32)
            + jnp.dot(own[0], near[1], preferred_element_type=jnp.float32)
            + jnp.dot(own[1], near[0], preferred_element_type=jnp.float32)
        )
        pair_offset_ref[...] = times(own, near_offset_ref[...]) + left_ref[...]

    @pl.when(here == skip_place)
    def _():
        skip_parts_ref[0], skip_parts_ref[1] = halves(skip_ref[...])


def late_split_kernel(place, late_ref, after_ref, parts_ref, offset_ref):
    del after_ref
    size = late_ref.shape[1]

    @pl.when(lax.axis_index("tm") == place)
    def _():
        parts_ref[0], parts_ref[1] = halves(late_ref[:size, :])
        offset_ref[...] = late_ref[size : size + 1, :]


def split_kernel(place, matrix_ref, parts_ref):
    @pl.when(lax.axis_index("tm") == place)
    def _():
        parts_ref[0], parts_ref[1] = halves(matrix_ref[...])


def offsets_kernel(last, means_ref, gain_ref, propagator_ref, offsets_ref, send_ref, own_parts_ref):
    here = lax.axis_index("tm") == last

    @pl.when(lax.axis_index("tm") == last - 2)
    def _():
        own_parts_ref[0], own_parts_ref[1] = halves(composed(gain_ref))

    @pl.when(jnp.logical_not(here))
    def _():
        send_ref[...], found = offsets(means_ref, gain_ref, propagator_ref)
        for t, row in enumerate(found):
            offsets_ref[t : t + 1, :] = row

    @pl.when(here)
    def _():
        offsets_ref[...] = means_ref[...]
        send_ref[...] = means_ref[0:1, :]


def last_kernel(
    last, came_ref, operator_ref, inputs_ref, kept_ref, gain_ref, propagator_ref,
    means_ref, states_ref, send_ref,
):
    @pl.when(lax.axis_index("tm") == last)
    def _():
        steps = operator_ref.shape[0]
        state = came_ref[...]
        means, moved = [], []
        for t in range(steps):
            state = times([operator_ref[t]], state) + inputs_ref[t : t + 1, :]
            means_ref[t : t + 1, :] = state
            means.append(state)
            if t < steps - 1:
                moved.append(times([propagator_ref[...]], state))
        states_ref[steps - 1 : steps, :] = state
        for t in reversed(range(steps - 1)):
            left, state = times([gain_ref[t]], moved[t], state)
            state = state + (means[t] - left)
            states_ref[t : t + 1, :] = state
        send_ref[...] = state

    @pl.when(lax.axis_index("tm") != last)
    def _():
        means_ref[...] = kept_ref[...]
        states_ref[...] = kept_ref[...]
        send_ref[...] = came_ref[...]


def smooth(state, gain_ref, offsets_ref, put):
    for t in reversed(range(gain_ref.shape[0])):
        state = times([gain_ref[t]], state) + offsets_ref[t : t + 1, :]
        put(t, state)


def parts_times(parts_ref, row_ref):
    return times([parts_ref[0], parts_ref[1]], row_ref[...])


def first_back_kernel(
    place, last_ref, far_offset_ref, far_parts_ref, own_parts_ref, left_ref, came_ref, entry_ref, send_ref
):
    here = lax.axis_index("tm")

    @pl.when(here == place)
    def _():
        entry_ref[...] = parts_times(far_parts_ref, last_ref) + far_offset_ref[...]
        send_ref[...] = parts_times(own_parts_ref, entry_ref) + left_ref[...]

    @pl.when(here != place)
    def _():
        entry_ref[...] = last_ref[...]
        send_ref[...] = jnp.where(here == place - 1, left_ref[...], came_ref[...])


def second_back_kernel(
    last,
    three_ref,
    one_ref,
    entry_ref,
    skip_parts_ref,
    pair_parts_ref,
    pair_offset_ref,
    gain_ref,
    offsets_ref,
    kept_ref,
    came_ref,
    states_ref,
    next_ref,
    send_ref,
):
    here = lax.axis_index("tm")

    def put(t, state):
        states_ref[t : t + 1, :] = state

    @pl.when(here == last - 5)
    def _():
        state = parts_times(skip_parts_ref, three_ref) + one_ref[...]
        next_ref[...] = state
        send_ref[...] = times([pair_parts_ref[0], pair_parts_ref[1]], state) + pair_offset_ref[...]
        states_ref[...] = kept_ref[...]

    @pl.when(here != last - 5)
    def _():
        send_ref[...] = came_ref[...]
        next_ref[...] = entry_ref[...]

    @pl.when(here == last - 2)
    def _():
        smooth(entry_ref[...], gain_ref, offsets_ref, put)

    @pl.when((here == last - 3) | (here == last - 1))
    def _():
        smooth(jnp.where(here == last - 1, three_ref[...], one_ref[...]), gain_ref, offsets_ref, put)
        send_ref[...] = states_ref[0:1, :]

    @pl.when((here == last) | (here == last - 4) | (here < last - 5))
    def _():
        states_ref[...] = kept_ref[...]


def back_kernel(
    target,
    stray,
    two_ref,
    one_ref,
    entry_ref,
    near_offset_ref,
    near_parts_ref,
    pair_parts_ref,
    pair_offset_ref,
    gain_ref,
    offsets_ref,
    kept_ref,
    came_ref,
    states_ref,
    next_ref,
    send_ref,
):
    here = lax.axis_index("tm")

    def put(t, state):
        states_ref[t : t + 1, :] = state

    @pl.when(here == target)
    def _():
        send_ref[...] = times([pair_parts_ref[0], pair_parts_ref[1]], two_ref[...]) + pair_offset_ref[...]
        next_ref[...] = two_ref[...]
        states_ref[...] = kept_ref[...]

    @pl.when(here != target)
    def _():
        send_ref[...] = came_ref[...]
        next_ref[...] = entry_ref[...]

    @pl.when(here == target + 2)
    def _():
        state = times([near_parts_ref[0], near_parts_ref[1]], entry_ref[...]) + near_offset_ref[...]
        smooth(state, gain_ref, offsets_ref, put)

    @pl.when((here == target + 1) | (here == stray))
    def _():
        smooth(jnp.where(here == stray, two_ref[...], one_ref[...]), gain_ref, offsets_ref, put)
        send_ref[...] = states_ref[0:1, :]

    @pl.when((here > target + 2) & (here != stray) | (here < target))
    def _():
        states_ref[...] = kept_ref[...]


def final_kernel(
    stray,
    two_ref,
    one_ref,
    entry_ref,
    near_offset_ref,
    near_parts_ref,
    late_offset_ref,
    late_parts_ref,
    gain_ref,
    offsets_ref,
    kept_ref,
    means_ref,
    result_ref,
    states_ref,
):
    here = lax.axis_index("tm")
    for t in range(means_ref.shape[0]):
        result_ref[t] = means_ref[t : t + 1, :]

    def put(t, state):
        states_ref[t] = state

    @pl.when(here == 0)
    def _():
        smooth(parts_times(late_parts_ref, two_ref) + late_offset_ref[...], gain_ref, offsets_ref, put)

    @pl.when(here == 2)
    def _():
        state = times([near_parts_ref[0], near_parts_ref[1]], entry_ref[...]) + near_offset_ref[...]
        smooth(state, gain_ref, offsets_ref, put)

    @pl.when((here == 1) | (here == stray))
    def _():
        smooth(jnp.where(here == stray, two_ref[...], one_ref[...]), gain_ref, offsets_ref, put)

    @pl.when((here > 2) & (here != stray))
    def _():
        for t in range(kept_ref.shape[0]):
            states_ref[t] = kept_ref[t : t + 1, :]


def call(kernel, name, outs, *args, cost=1.0):
    return pl.pallas_call(
        kernel,
        out_shape=[
            jax.ShapeDtypeStruct(shape, jnp.bfloat16 if len(shape) == 3 and shape[1] > 1 else jnp.float32)
            for shape in outs
        ],
        in_specs=[VMEM] * len(args),
        out_specs=[VMEM] * len(outs),
        compiler_params=PARAMS,
        cost_estimate=pl.CostEstimate(flops=int(cost * 1e9), bytes_accessed=2**12, transcendentals=0),
        name=name,
    )(*args)


def pass_row(row, rings, places):
    route = {}
    for place in range(places):
        for core in range(2):
            route[place * 2 + core] = place * 2 + 1 - core
    for ring in rings:
        for i, place in enumerate(ring):
            for core in range(2):
                route[place * 2 + core] = ring[(i + 1) % len(ring)] * 2 + core
    return lax.ppermute(row, ("tm", "block"), sorted(route.items()))


def ring_up(place, places):
    if place % 2 and place >= places - 5 and place < places - 1:
        return (place, place + 1, place + 2)
    if place == 0:
        return (0, 1, 3)
    if place % 2 or place == places - 2:
        return (place, place + 1)
    return (place, place + 1, place - 2)


def local(
    scaled_residual_maps,
    measurement_stencil,
    observed_partition,
    active_probe_total,
    filtering_operator,
    updated_covariance,
    backward_factor,
    propagator,
    initial_mean,
):
    steps, size = filtering_operator.shape[0], filtering_operator.shape[-1]
    places = lax.axis_size("tm")
    many, one = (steps, size), (1, size)
    operator = filtering_operator.reshape(steps, size, size)
    covariance = updated_covariance.reshape(steps, size, size)
    gain = backward_factor.reshape(steps, size, size)
    last = places - 1
    matrix = propagator.reshape(size, size)
    square, parts, result = (size, size), (2, size, size), (steps, 1, size)
    sensors = (scaled_residual_maps, measurement_stencil, observed_partition, active_probe_total)
    mine, other = sensor_info((), *sensors)

    def compose(after, *senders):
        return call(functools.partial(compose_kernel, senders), "compose", (square,), after, gain, cost=0.01)[0]

    near_senders = range(3, last - 3, 2)
    inputs, means, send = call(
        start_kernel, "start", (many, many, (8, size)), mine, other, covariance, operator, initial_mean, cost=0.5
    )
    first = lax.ppermute(
        compose(send, last - 1, *near_senders), "tm", [(place, place - 1) for place in (*near_senders, last - 1)]
    )
    skip = lax.ppermute(compose(send, last - 3), "tm", [(last - 3, last - 5)])
    for place in range(1, places):
        if place == 1:
            came = pass_row(send, [ring_up(0, places)], places)
            mine, other = sensor_info((send,), *sensors)
            inputs, means, send = call(
                first_hop_kernel, "forward", (many, many, one),
                came, mine, other, covariance, operator, inputs, means, cost=COSTS[1],
            )
            continue
        came = pass_row(send, [ring_up(place - 1, places)], places)
        if place == 2:
            late = call(
                functools.partial(late_kernel, (1,)), "late", ((size + 8, size),), means, gain, matrix,
                cost=0.5,
            )[0]
            late = lax.ppermute(late, "tm", [(1, 0)])
        if place < last:
            means, send = call(
                functools.partial(hop_kernel, place), "forward", (many, one), came, operator, inputs, means,
                cost=COSTS[2] if place == 2 else 0.5,
            )
    offset_rows, left, own_parts = call(
        functools.partial(offsets_kernel, last), "offsets", (many, one, parts), means, gain, matrix
    )
    first_offset = pass_row(left, [(place - 1, place) for place in (*near_senders, last - 1)], places)
    means, states, send = call(
        functools.partial(last_kernel, last),
        "last",
        (many, many, one),
        came,
        operator,
        inputs,
        means,
        gain,
        matrix,
        cost=0.5,
    )
    came = pass_row(send, [(last, last - 2)], places)

    (far_parts,) = call(functools.partial(split_kernel, last - 2), "split", (parts,), first, cost=0.05)
    entry, send = call(
        functools.partial(first_back_kernel, last - 2), "first_back", (one, one),
        came, first_offset, far_parts, own_parts, left, send,
        cost=COSTS[3],
    )
    one_up = pass_row(send, [(last - 2, last - 3, last - 5, last - 4)], places)
    three = pass_row(send, [(last - 2, last - 5), (last, last - 1)], places)
    near_parts, pair_parts, pair_offset, skip_parts = call(
        functools.partial(pair_kernel, tuple(place - 1 for place in near_senders), last - 5),
        "pair",
        (parts, parts, one, parts),
        first,
        skip,
        gain,
        left,
        first_offset,
        cost=0.05,
    )
    states, entry, send = call(
        functools.partial(second_back_kernel, last),
        "second_back",
        (many, one, one),
        three,
        one_up,
        entry,
        skip_parts,
        pair_parts,
        pair_offset,
        gain,
        offset_rows,
        states,
        send,
        cost=COSTS[4],
    )
    stray = last - 4
    for target in range(last - 7, -1, -2):
        rings = [(target + 2, target)] + ([(stray + 1, stray)] if stray > 0 else [])
        one_up = pass_row(send, [(target + 2, target + 1)], places)
        two = pass_row(send, rings, places)
        if target:
            states, entry, send = call(
                functools.partial(back_kernel, target, stray), "back", (many, one, one),
                two, one_up, entry, first_offset, near_parts, pair_parts, pair_offset, gain, offset_rows, states,
                send,
            )
        else:
            late_parts, late_offset = call(
                functools.partial(late_split_kernel, 0), "late_split", (parts, one), late, send, cost=0.05
            )
            means, states = call(
                functools.partial(final_kernel, stray), "final", (result, result),
                two, one_up, entry, first_offset, near_parts, late_offset, late_parts, gain, offset_rows, states, means,
            )
        stray = -1
    return means, states


def solution(mesh):
    placed = (
        P(("groups", "tm"), "block", None, None),
        P(),
        P(("groups", "tm"), "block"),
        P(("groups", "tm"), "block"),
        P(("groups", "tm"), "block", None, None),
        P(("groups", "tm"), "block", None, None),
        P(("groups", "tm"), "block", None, None),
        P("block", None, None),
        P(("groups", "block"), None),
    )
    return jax.shard_map(
        local,
        mesh=mesh,
        in_specs=placed,
        out_specs=(P(("groups", "tm"), "block", None), P(("groups", "tm"), "block", None)),
        check_vma=False,
    )
```

```python
import functools

import jax
import jax.numpy as jnp
from jax import lax
from jax.experimental import pallas as pl
from jax.experimental.pallas import tpu as pltpu
from jax.sharding import PartitionSpec as P

GH = 16
COSTS = (60.0, 2.5, 2.5, 6.0, 0.5)
VMEM = pl.BlockSpec(memory_space=pltpu.VMEM)
PARAMS = pltpu.CompilerParams(vmem_limit_bytes=16 * 2**20)


def pieces(rows, count=3):
    height = -(-len(rows) * count // 8) * 8
    at = lax.broadcasted_iota(jnp.int32, (height, rows[0].shape[1]), 0)
    block = jnp.zeros(at.shape, jnp.float32)
    for k, rest in enumerate(rows):
        for i in range(count):
            piece = rest.astype(jnp.bfloat16).astype(jnp.float32)
            block = jnp.where(at == k * count + i, piece, block)
            rest = rest - piece
    return block.astype(jnp.bfloat16)


def times(matrices, *rows, turned=False):
    block = pieces(rows)
    product = sum(
        lax.dot_general(
            block, matrix, (((1,), (0 if turned else 1,)), ((), ())), preferred_element_type=jnp.float32
        )
        for matrix in matrices
    )
    found = [jnp.sum(product[3 * k : 3 * k + 3, :], axis=0, keepdims=True) for k in range(len(rows))]
    return found if len(rows) > 1 else found[0]


def info_kernel(stencil_hbm, observed_hbm, active_hbm, maps_hbm, mine_ref, theirs_ref, *scratch):
    stencil_ref, observed_ref, active_ref, maps, taps, sems = scratch

    @pl.when(lax.axis_index("tm") == 0)
    def _():
        copies = []
        for i, (source, target) in enumerate(
            ((stencil_hbm, stencil_ref), (observed_hbm, observed_ref), (active_hbm, active_ref))
        ):
            copies.append(pltpu.make_async_copy(source, target, sems.at[i]))
        for t in range(maps.shape[0]):
            copies.append(pltpu.make_async_copy(maps_hbm.at[t], maps.at[t], sems.at[3 + t]))
        for copy in copies:
            copy.start()
        place_info(stencil_ref, observed_ref, active_ref, maps, mine_ref, theirs_ref, taps, copies)


def staged_info_kernel(after_ref, *refs):
    del after_ref

    @pl.when(lax.axis_index("tm") != 0)
    def _():
        place_info(*refs, [])


def place_info(stencil_ref, observed_ref, active_ref, maps, mine_ref, theirs_ref, taps, copies):
    steps, rows, cells = maps.shape
    slots = observed_ref.shape[1]
    side, _, channels = stencil_ref.shape
    half = side // 2

    repeat = jnp.where(
        lax.broadcasted_iota(jnp.int32, (channels, rows), 1) % channels
        == lax.broadcasted_iota(jnp.int32, (channels, rows), 0),
        1.0,
        0.0,
    ).astype(jnp.bfloat16)
    taps[...] = jnp.zeros_like(taps)
    spread = jnp.where(
        lax.broadcasted_iota(jnp.int32, (slots, rows), 1) // channels
        == lax.broadcasted_iota(jnp.int32, (slots, rows), 0),
        1.0,
        0.0,
    ).astype(jnp.bfloat16)

    cell = lax.broadcasted_iota(jnp.int32, (8, cells), 1)
    width = cells // GH
    down = cell // width
    across = cell % width
    tap = lax.broadcasted_iota(jnp.int32, (8, cells), 0)
    column = across - tap + half
    column_inside = (column >= 0) & (column < width) & (tap < side)
    me = lax.axis_index("block")
    for copy in copies[:3]:
        copy.wait()
    for p in range(side):
        taps[p * 8 : p * 8 + side, :] = jnp.dot(
            stencil_ref[p], repeat, preferred_element_type=jnp.float32
        )
    for t in range(steps):
        owner = lax.broadcasted_iota(jnp.int32, (8, slots), 0)
        slot = lax.broadcasted_iota(jnp.int32, (8, slots), 1)
        live = (observed_ref[t : t + 1, :] == owner) & (slot < active_ref[0:1, t : t + 1])
        weight = jnp.dot(
            jnp.where(live, 1.0, 0.0).astype(jnp.bfloat16), spread, preferred_element_type=jnp.float32
        )
        left = jnp.concatenate([taps[...] * weight[b : b + 1, :] for b in range(2)], axis=0)
        for copy in copies[3 + t : 4 + t]:
            copy.wait()
        shifted = jnp.dot(left.astype(jnp.bfloat16), maps[t], preferred_element_type=jnp.float32)
        found = []
        for b in range(2):
            total = jnp.zeros((8, cells), jnp.float32)
            for p in range(side):
                at = (b * side + p) * 8
                part = pltpu.roll(shifted[at : at + 8, :], ((p - half) * width) % cells, 1)
                row = down - p + half
                total = total + jnp.where((row >= 0) & (row < GH), part, 0.0)
            sides = jnp.zeros((8, cells), jnp.float32)
            for q in range(side):
                part = pltpu.roll(total, (q - half) % cells, 1)
                sides = jnp.where(column_inside & (tap == q), part, sides)
            found.append(jnp.sum(sides, axis=0, keepdims=True))
        mine_ref[t : t + 1, :] = jnp.where(me == 0, found[0], found[1])
        theirs_ref[t : t + 1, :] = jnp.where(me == 0, found[1], found[0])


def sensor_info(after, scaled_residual_maps, measurement_stencil, observed_partition, active_probe_total):
    steps, slots, channels, cells = scaled_residual_maps.shape
    side = measurement_stencil.shape[1]
    operands = (
        measurement_stencil.transpose(1, 2, 0),
        observed_partition,
        active_probe_total.T,
        scaled_residual_maps.reshape(steps, slots * channels, cells),
    )
    taps = pltpu.VMEM((side * 8, slots * channels), jnp.float32)
    if after:
        kernel, specs, scratch, cost = staged_info_kernel, [VMEM] * 5, [taps], int(COSTS[0] * 1e9)
    else:
        kernel, specs, cost = info_kernel, [pl.BlockSpec(memory_space=pltpu.HBM)] * 4, 10**6
        scratch = [
            *(pltpu.VMEM(array.shape, array.dtype) for array in operands),
            taps,
            pltpu.SemaphoreType.DMA((3 + steps,)),
        ]
        operands = [pltpu.with_memory_space_constraint(array, pltpu.HBM) for array in operands]
    mine, theirs = pl.pallas_call(
        kernel,
        out_shape=[jax.ShapeDtypeStruct((steps, cells), jnp.float32)] * 2,
        in_specs=specs,
        out_specs=[VMEM] * 2,
        scratch_shapes=scratch,
        compiler_params=PARAMS,
        cost_estimate=pl.CostEstimate(flops=cost, bytes_accessed=2**12, transcendentals=0),
        name="sensor_info",
    )(*after, *operands)
    return mine, lax.ppermute(theirs, "block", [(0, 1), (1, 0)])


def start_kernel(mine_ref, other_ref, covariance_ref, operator_ref, start_ref, inputs_ref, states_ref, send_ref):
    here = lax.axis_index("tm") == 0

    @pl.when(here)
    def _():
        state = start_ref[...]
        for t in range(mine_ref.shape[0]):
            drive = times([covariance_ref[t]], mine_ref[t : t + 1, :] + other_ref[t : t + 1, :])
            inputs_ref[t : t + 1, :] = drive
            state = times([operator_ref[t]], state) + drive
            states_ref[t : t + 1, :] = state
        send_ref[...] = jnp.broadcast_to(state, send_ref.shape)

    @pl.when(jnp.logical_not(here))
    def _():
        inputs_ref[...] = jnp.zeros_like(inputs_ref)
        states_ref[...] = jnp.zeros_like(states_ref)
        send_ref[...] = jnp.zeros_like(send_ref)


def first_hop_kernel(
    came_ref, mine_ref, other_ref, covariance_ref, operator_ref, kept_inputs_ref, kept_ref,
    inputs_ref, states_ref, send_ref,
):
    here = lax.axis_index("tm")

    @pl.when(here == 0)
    def _():
        inputs_ref[...] = kept_inputs_ref[...]

    @pl.when(here != 0)
    def _():
        for t in range(mine_ref.shape[0]):
            info = mine_ref[t : t + 1, :] + other_ref[t : t + 1, :]
            inputs_ref[t : t + 1, :] = times([covariance_ref[t]], info)

    @pl.when(here == 1)
    def _():
        state = came_ref[0:1, :]
        for t in range(operator_ref.shape[0]):
            state = times([operator_ref[t]], state) + inputs_ref[t : t + 1, :]
            states_ref[t : t + 1, :] = state
        send_ref[...] = state

    @pl.when(here != 1)
    def _():
        states_ref[...] = kept_ref[...]
        send_ref[...] = came_ref[0:1, :]


def hop_kernel(turn, came_ref, matrices_ref, offsets_ref, kept_ref, states_ref, send_ref):
    here = lax.axis_index("tm") == turn

    @pl.when(here)
    def _():
        state = came_ref[...]
        for t in range(matrices_ref.shape[0]):
            state = times([matrices_ref[t]], state) + offsets_ref[t : t + 1, :]
            states_ref[t : t + 1, :] = state
        send_ref[...] = state

    @pl.when(jnp.logical_not(here))
    def _():
        states_ref[...] = kept_ref[...]
        send_ref[...] = came_ref[...]


def halves(matrix):
    high = matrix.astype(jnp.bfloat16)
    return [high, (matrix - high.astype(jnp.float32)).astype(jnp.bfloat16)]


def composed(gain_ref):
    product = gain_ref[0]
    for t in range(1, gain_ref.shape[0]):
        product = sum(
            lax.dot_general(
                gain_ref[t], part, (((0,), (0 if t > 1 else 1,)), ((), ())), preferred_element_type=jnp.float32
            )
            for part in (halves(product) if t > 1 else [product])
        )
    return product.astype(jnp.float32) if gain_ref.shape[0] > 1 else product.astype(jnp.float32).T


def compose_kernel(senders, after_ref, gain_ref, composed_ref):
    del after_ref
    here = lax.axis_index("tm")
    sends = functools.reduce(jnp.logical_or, [here == place for place in senders])

    @pl.when(sends)
    def _():
        composed_ref[...] = composed(gain_ref)


def late_kernel(senders, means_ref, gain_ref, propagator_ref, composed_ref):
    size = gain_ref.shape[1]
    here = lax.axis_index("tm")
    sends = functools.reduce(jnp.logical_or, [here == place for place in senders])

    @pl.when(sends)
    def _():
        composed_ref[:size, :] = composed(gain_ref)
        composed_ref[size:, :] = jnp.zeros((composed_ref.shape[0] - size, size), jnp.float32)
        composed_ref[size : size + 1, :] = offsets(means_ref, gain_ref, propagator_ref)[0]


def offsets(means_ref, gain_ref, propagator_ref):
    steps = means_ref.shape[0]
    means = [means_ref[t : t + 1, :] for t in range(steps)]
    moved = times([propagator_ref[...]], *means)
    state = jnp.zeros_like(means[0])
    found = [None] * steps
    for t in reversed(range(steps)):
        left, state = times([gain_ref[t]], moved[t], state)
        found[t] = means[t] - left
        state = state + found[t]
    return state, found


def pair_kernel(
    places,
    skip_place,
    near_ref,
    skip_ref,
    gain_ref,
    left_ref,
    near_offset_ref,
    near_parts_ref,
    pair_parts_ref,
    pair_offset_ref,
    skip_parts_ref,
):
    here = lax.axis_index("tm")

    @pl.when(functools.reduce(jnp.logical_or, [here == place for place in places]))
    def _():
        near = halves(near_ref[...])
        own = halves(composed(gain_ref))
        near_parts_ref[0], near_parts_ref[1] = near
        pair_parts_ref[0], pair_parts_ref[1] = halves(
            jnp.dot(near[0], own[0], preferred_element_type=jnp.float32)
            + jnp.dot(near[1], own[0], preferred_element_type=jnp.float32)
            + jnp.dot(near[0], own[1], preferred_element_type=jnp.float32)
        )
        pair_offset_ref[...] = times(own, near_offset_ref[...], turned=True) + left_ref[...]

    @pl.when(here == skip_place)
    def _():
        skip_parts_ref[0], skip_parts_ref[1] = halves(skip_ref[...])


def late_split_kernel(place, late_ref, after_ref, parts_ref, offset_ref):
    del after_ref
    size = late_ref.shape[1]

    @pl.when(lax.axis_index("tm") == place)
    def _():
        parts_ref[0], parts_ref[1] = halves(late_ref[:size, :])
        offset_ref[...] = late_ref[size : size + 1, :]


def split_kernel(place, matrix_ref, parts_ref):
    @pl.when(lax.axis_index("tm") == place)
    def _():
        parts_ref[0], parts_ref[1] = halves(matrix_ref[...])


def offsets_kernel(last, means_ref, gain_ref, propagator_ref, offsets_ref, send_ref, own_parts_ref):
    here = lax.axis_index("tm") == last

    @pl.when(lax.axis_index("tm") == last - 2)
    def _():
        own_parts_ref[0], own_parts_ref[1] = halves(composed(gain_ref))

    @pl.when(jnp.logical_not(here))
    def _():
        send_ref[...], found = offsets(means_ref, gain_ref, propagator_ref)
        for t, row in enumerate(found):
            offsets_ref[t : t + 1, :] = row

    @pl.when(here)
    def _():
        offsets_ref[...] = means_ref[...]
        send_ref[...] = means_ref[0:1, :]


def last_kernel(
    last, came_ref, operator_ref, inputs_ref, kept_ref, gain_ref, propagator_ref,
    means_ref, states_ref, send_ref,
):
    @pl.when(lax.axis_index("tm") == last)
    def _():
        steps = operator_ref.shape[0]
        state = came_ref[...]
        means, moved = [], []
        for t in range(steps):
            state = times([operator_ref[t]], state) + inputs_ref[t : t + 1, :]
            means_ref[t : t + 1, :] = state
            means.append(state)
            if t < steps - 1:
                moved.append(times([propagator_ref[...]], state))
        states_ref[steps - 1 : steps, :] = state
        for t in reversed(range(steps - 1)):
            left, state = times([gain_ref[t]], moved[t], state)
            state = state + (means[t] - left)
            states_ref[t : t + 1, :] = state
        send_ref[...] = state

    @pl.when(lax.axis_index("tm") != last)
    def _():
        means_ref[...] = kept_ref[...]
        states_ref[...] = kept_ref[...]
        send_ref[...] = came_ref[...]


def smooth(state, gain_ref, offsets_ref, put):
    for t in reversed(range(gain_ref.shape[0])):
        state = times([gain_ref[t]], state) + offsets_ref[t : t + 1, :]
        put(t, state)


def parts_times(parts_ref, row_ref):
    return times([parts_ref[0], parts_ref[1]], row_ref[...], turned=True)


def first_back_kernel(
    place, last_ref, far_offset_ref, far_parts_ref, own_parts_ref, left_ref, came_ref, entry_ref, send_ref
):
    here = lax.axis_index("tm")

    @pl.when(here == place)
    def _():
        entry_ref[...] = parts_times(far_parts_ref, last_ref) + far_offset_ref[...]
        send_ref[...] = parts_times(own_parts_ref, entry_ref) + left_ref[...]

    @pl.when(here != place)
    def _():
        entry_ref[...] = last_ref[...]
        send_ref[...] = jnp.where(here == place - 1, left_ref[...], came_ref[...])


def second_back_kernel(
    last,
    three_ref,
    one_ref,
    entry_ref,
    skip_parts_ref,
    pair_parts_ref,
    pair_offset_ref,
    gain_ref,
    offsets_ref,
    kept_ref,
    came_ref,
    states_ref,
    next_ref,
    send_ref,
):
    here = lax.axis_index("tm")

    def put(t, state):
        states_ref[t : t + 1, :] = state

    @pl.when(here == last - 5)
    def _():
        state = parts_times(skip_parts_ref, three_ref) + one_ref[...]
        next_ref[...] = state
        send_ref[...] = times([pair_parts_ref[0], pair_parts_ref[1]], state, turned=True) + pair_offset_ref[...]
        states_ref[...] = kept_ref[...]

    @pl.when(here != last - 5)
    def _():
        send_ref[...] = came_ref[...]
        next_ref[...] = entry_ref[...]

    @pl.when(here == last - 2)
    def _():
        smooth(entry_ref[...], gain_ref, offsets_ref, put)

    @pl.when((here == last - 3) | (here == last - 1))
    def _():
        smooth(jnp.where(here == last - 1, three_ref[...], one_ref[...]), gain_ref, offsets_ref, put)
        send_ref[...] = states_ref[0:1, :]

    @pl.when((here == last) | (here == last - 4) | (here < last - 5))
    def _():
        states_ref[...] = kept_ref[...]


def back_kernel(
    target,
    stray,
    two_ref,
    one_ref,
    entry_ref,
    near_offset_ref,
    near_parts_ref,
    pair_parts_ref,
    pair_offset_ref,
    gain_ref,
    offsets_ref,
    kept_ref,
    came_ref,
    states_ref,
    next_ref,
    send_ref,
):
    here = lax.axis_index("tm")

    def put(t, state):
        states_ref[t : t + 1, :] = state

    @pl.when(here == target)
    def _():
        send_ref[...] = parts_times(pair_parts_ref, two_ref) + pair_offset_ref[...]
        next_ref[...] = two_ref[...]
        states_ref[...] = kept_ref[...]

    @pl.when(here != target)
    def _():
        send_ref[...] = came_ref[...]
        next_ref[...] = entry_ref[...]

    @pl.when(here == target + 2)
    def _():
        state = parts_times(near_parts_ref, entry_ref) + near_offset_ref[...]
        smooth(state, gain_ref, offsets_ref, put)

    @pl.when((here == target + 1) | (here == stray))
    def _():
        smooth(jnp.where(here == stray, two_ref[...], one_ref[...]), gain_ref, offsets_ref, put)
        send_ref[...] = states_ref[0:1, :]

    @pl.when((here > target + 2) & (here != stray) | (here < target))
    def _():
        states_ref[...] = kept_ref[...]


def final_kernel(
    stray,
    two_ref,
    one_ref,
    entry_ref,
    near_offset_ref,
    near_parts_ref,
    late_offset_ref,
    late_parts_ref,
    gain_ref,
    offsets_ref,
    kept_ref,
    means_ref,
    result_ref,
    states_ref,
):
    here = lax.axis_index("tm")
    for t in range(means_ref.shape[0]):
        result_ref[t] = means_ref[t : t + 1, :]

    def put(t, state):
        states_ref[t] = state

    @pl.when(here == 0)
    def _():
        smooth(parts_times(late_parts_ref, two_ref) + late_offset_ref[...], gain_ref, offsets_ref, put)

    @pl.when(here == 2)
    def _():
        state = parts_times(near_parts_ref, entry_ref) + near_offset_ref[...]
        smooth(state, gain_ref, offsets_ref, put)

    @pl.when((here == 1) | (here == stray))
    def _():
        smooth(jnp.where(here == stray, two_ref[...], one_ref[...]), gain_ref, offsets_ref, put)

    @pl.when((here > 2) & (here != stray))
    def _():
        for t in range(kept_ref.shape[0]):
            states_ref[t] = kept_ref[t : t + 1, :]


def call(kernel, name, outs, *args, cost=1.0):
    return pl.pallas_call(
        kernel,
        out_shape=[
            jax.ShapeDtypeStruct(shape, jnp.bfloat16 if len(shape) == 3 and shape[1] > 1 else jnp.float32)
            for shape in outs
        ],
        in_specs=[VMEM] * len(args),
        out_specs=[VMEM] * len(outs),
        compiler_params=PARAMS,
        cost_estimate=pl.CostEstimate(flops=int(cost * 1e9), bytes_accessed=2**12, transcendentals=0),
        name=name,
    )(*args)


def pass_row(row, rings, places):
    route = {}
    for place in range(places):
        for core in range(2):
            route[place * 2 + core] = place * 2 + 1 - core
    for ring in rings:
        for i, place in enumerate(ring):
            for core in range(2):
                route[place * 2 + core] = ring[(i + 1) % len(ring)] * 2 + core
    return lax.ppermute(row, ("tm", "block"), sorted(route.items()))


def ring_up(place, places):
    if place % 2 and place >= places - 5 and place < places - 1:
        return (place, place + 1, place + 2)
    if place == 0:
        return (0, 1, 3)
    if place % 2 or place == places - 2:
        return (place, place + 1)
    return (place, place + 1, place - 2)


def local(
    scaled_residual_maps,
    measurement_stencil,
    observed_partition,
    active_probe_total,
    filtering_operator,
    updated_covariance,
    backward_factor,
    propagator,
    initial_mean,
):
    steps, size = filtering_operator.shape[0], filtering_operator.shape[-1]
    places = lax.axis_size("tm")
    many, one = (steps, size), (1, size)
    operator = filtering_operator.reshape(steps, size, size)
    covariance = updated_covariance.reshape(steps, size, size)
    gain = backward_factor.reshape(steps, size, size)
    last = places - 1
    matrix = propagator.reshape(size, size)
    square, parts, result = (size, size), (2, size, size), (steps, 1, size)
    sensors = (scaled_residual_maps, measurement_stencil, observed_partition, active_probe_total)
    mine, other = sensor_info((), *sensors)

    def compose(after, *senders):
        return call(functools.partial(compose_kernel, senders), "compose", (square,), after, gain, cost=0.01)[0]

    near_senders = range(3, last - 3, 2)
    inputs, means, send = call(
        start_kernel, "start", (many, many, (8, size)), mine, other, covariance, operator, initial_mean, cost=0.5
    )
    first = lax.ppermute(
        compose(send, last - 1, *near_senders), "tm", [(place, place - 1) for place in (*near_senders, last - 1)]
    )
    skip = lax.ppermute(compose(send, last - 3), "tm", [(last - 3, last - 5)])
    for place in range(1, places):
        if place == 1:
            came = pass_row(send, [ring_up(0, places)], places)
            mine, other = sensor_info((send,), *sensors)
            inputs, means, send = call(
                first_hop_kernel, "forward", (many, many, one),
                came, mine, other, covariance, operator, inputs, means, cost=COSTS[1],
            )
            continue
        came = pass_row(send, [ring_up(place - 1, places)], places)
        if place == 2:
            late = call(
                functools.partial(late_kernel, (1,)), "late", ((size + 8, size),), means, gain, matrix,
                cost=0.5,
            )[0]
            late = lax.ppermute(late, "tm", [(1, 0)])
        if place < last:
            means, send = call(
                functools.partial(hop_kernel, place), "forward", (many, one), came, operator, inputs, means,
                cost=COSTS[2] if place == 2 else 0.5,
            )
    offset_rows, left, own_parts = call(
        functools.partial(offsets_kernel, last), "offsets", (many, one, parts), means, gain, matrix
    )
    first_offset = pass_row(left, [(place - 1, place) for place in (*near_senders, last - 1)], places)
    means, states, send = call(
        functools.partial(last_kernel, last),
        "last",
        (many, many, one),
        came,
        operator,
        inputs,
        means,
        gain,
        matrix,
        cost=0.5,
    )
    came = pass_row(send, [(last, last - 2)], places)

    (far_parts,) = call(functools.partial(split_kernel, last - 2), "split", (parts,), first, cost=0.05)
    entry, send = call(
        functools.partial(first_back_kernel, last - 2), "first_back", (one, one),
        came, first_offset, far_parts, own_parts, left, send,
        cost=COSTS[3],
    )
    one_up = pass_row(send, [(last - 2, last - 3, last - 5, last - 4)], places)
    three = pass_row(send, [(last - 2, last - 5), (last, last - 1)], places)
    near_parts, pair_parts, pair_offset, skip_parts = call(
        functools.partial(pair_kernel, tuple(place - 1 for place in near_senders), last - 5),
        "pair",
        (parts, parts, one, parts),
        first,
        skip,
        gain,
        left,
        first_offset,
        cost=0.05,
    )
    states, entry, send = call(
        functools.partial(second_back_kernel, last),
        "second_back",
        (many, one, one),
        three,
        one_up,
        entry,
        skip_parts,
        pair_parts,
        pair_offset,
        gain,
        offset_rows,
        states,
        send,
        cost=COSTS[4],
    )
    stray = last - 4
    for target in range(last - 7, -1, -2):
        rings = [(target + 2, target)] + ([(stray + 1, stray)] if stray > 0 else [])
        one_up = pass_row(send, [(target + 2, target + 1)], places)
        two = pass_row(send, rings, places)
        if target:
            states, entry, send = call(
                functools.partial(back_kernel, target, stray), "back", (many, one, one),
                two, one_up, entry, first_offset, near_parts, pair_parts, pair_offset, gain, offset_rows, states,
                send,
            )
        else:
            late_parts, late_offset = call(
                functools.partial(late_split_kernel, 0), "late_split", (parts, one), late, send, cost=0.05
            )
            means, states = call(
                functools.partial(final_kernel, stray), "final", (result, result),
                two, one_up, entry, first_offset, near_parts, late_offset, late_parts, gain, offset_rows, states, means,
            )
        stray = -1
    return means, states


def solution(mesh):
    placed = (
        P(("groups", "tm"), "block", None, None),
        P(),
        P(("groups", "tm"), "block"),
        P(("groups", "tm"), "block"),
        P(("groups", "tm"), "block", None, None),
        P(("groups", "tm"), "block", None, None),
        P(("groups", "tm"), "block", None, None),
        P("block", None, None),
        P(("groups", "block"), None),
    )
    return jax.shard_map(
        local,
        mesh=mesh,
        in_specs=placed,
        out_specs=(P(("groups", "tm"), "block", None), P(("groups", "tm"), "block", None)),
        check_vma=False,
    )
```

```python
import functools

import jax
import jax.numpy as jnp
from jax import lax
from jax.experimental import pallas as pl
from jax.experimental.pallas import tpu as pltpu
from jax.sharding import PartitionSpec as P

GH = 16
COSTS = (60.0, 2.5, 2.5, 6.0, 0.5)
VMEM = pl.BlockSpec(memory_space=pltpu.VMEM)
PARAMS = pltpu.CompilerParams(vmem_limit_bytes=16 * 2**20)


def pieces(rows, count=3):
    height = -(-len(rows) * count // 8) * 8
    at = lax.broadcasted_iota(jnp.int32, (height, rows[0].shape[1]), 0)
    block = jnp.zeros(at.shape, jnp.float32)
    for k, rest in enumerate(rows):
        for i in range(count):
            piece = rest.astype(jnp.bfloat16).astype(jnp.float32)
            block = jnp.where(at == k * count + i, piece, block)
            rest = rest - piece
    return block.astype(jnp.bfloat16)


def times(matrices, *rows, turned=False):
    block = pieces(rows)
    product = sum(
        lax.dot_general(
            block, matrix, (((1,), (0 if turned else 1,)), ((), ())), preferred_element_type=jnp.float32
        )
        for matrix in matrices
    )
    found = [jnp.sum(product[3 * k : 3 * k + 3, :], axis=0, keepdims=True) for k in range(len(rows))]
    return found if len(rows) > 1 else found[0]


def info_kernel(stencil_hbm, observed_hbm, active_hbm, maps_hbm, mine_ref, theirs_ref, *scratch):
    stencil_ref, observed_ref, active_ref, maps, taps, sems = scratch

    @pl.when(lax.axis_index("tm") == 0)
    def _():
        copies = []
        for i, (source, target) in enumerate(
            ((stencil_hbm, stencil_ref), (observed_hbm, observed_ref), (active_hbm, active_ref))
        ):
            copies.append(pltpu.make_async_copy(source, target, sems.at[i]))
        for t in range(maps.shape[0]):
            copies.append(pltpu.make_async_copy(maps_hbm.at[t], maps.at[t], sems.at[3 + t]))
        for copy in copies:
            copy.start()
        place_info(stencil_ref, observed_ref, active_ref, maps, mine_ref, theirs_ref, taps, copies)


def staged_info_kernel(after_ref, *refs):
    del after_ref

    @pl.when(lax.axis_index("tm") != 0)
    def _():
        place_info(*refs, [])


def place_info(stencil_ref, observed_ref, active_ref, maps, mine_ref, theirs_ref, taps, copies):
    steps, rows, cells = maps.shape
    slots = observed_ref.shape[1]
    side, _, channels = stencil_ref.shape
    half = side // 2

    repeat = jnp.where(
        lax.broadcasted_iota(jnp.int32, (channels, rows), 1) % channels
        == lax.broadcasted_iota(jnp.int32, (channels, rows), 0),
        1.0,
        0.0,
    ).astype(jnp.bfloat16)
    taps[...] = jnp.zeros_like(taps)
    spread = jnp.where(
        lax.broadcasted_iota(jnp.int32, (slots, rows), 1) // channels
        == lax.broadcasted_iota(jnp.int32, (slots, rows), 0),
        1.0,
        0.0,
    ).astype(jnp.bfloat16)

    cell = lax.broadcasted_iota(jnp.int32, (8, cells), 1)
    width = cells // GH
    down = cell // width
    across = cell % width
    tap = lax.broadcasted_iota(jnp.int32, (8, cells), 0)
    column = across - tap + half
    column_inside = (column >= 0) & (column < width) & (tap < side)
    me = lax.axis_index("block")
    for copy in copies[:3]:
        copy.wait()
    for p in range(side):
        taps[p * 8 : p * 8 + side, :] = jnp.dot(
            stencil_ref[p], repeat, preferred_element_type=jnp.float32
        )
    for t in range(steps):
        owner = lax.broadcasted_iota(jnp.int32, (8, slots), 0)
        slot = lax.broadcasted_iota(jnp.int32, (8, slots), 1)
        live = (observed_ref[t : t + 1, :] == owner) & (slot < active_ref[0:1, t : t + 1])
        weight = jnp.dot(
            jnp.where(live, 1.0, 0.0).astype(jnp.bfloat16), spread, preferred_element_type=jnp.float32
        )
        left = jnp.concatenate([taps[...] * weight[b : b + 1, :] for b in range(2)], axis=0)
        for copy in copies[3 + t : 4 + t]:
            copy.wait()
        shifted = jnp.dot(left.astype(jnp.bfloat16), maps[t], preferred_element_type=jnp.float32)
        found = []
        for b in range(2):
            total = jnp.zeros((8, cells), jnp.float32)
            for p in range(side):
                at = (b * side + p) * 8
                part = pltpu.roll(shifted[at : at + 8, :], ((p - half) * width) % cells, 1)
                row = down - p + half
                total = total + jnp.where((row >= 0) & (row < GH), part, 0.0)
            sides = jnp.zeros((8, cells), jnp.float32)
            for q in range(side):
                part = pltpu.roll(total, (q - half) % cells, 1)
                sides = jnp.where(column_inside & (tap == q), part, sides)
            found.append(jnp.sum(sides, axis=0, keepdims=True))
        mine_ref[t : t + 1, :] = jnp.where(me == 0, found[0], found[1])
        theirs_ref[t : t + 1, :] = jnp.where(me == 0, found[1], found[0])


def sensor_info(after, scaled_residual_maps, measurement_stencil, observed_partition, active_probe_total):
    steps, slots, channels, cells = scaled_residual_maps.shape
    side = measurement_stencil.shape[1]
    operands = (
        measurement_stencil.transpose(1, 2, 0),
        observed_partition,
        active_probe_total.T,
        scaled_residual_maps.reshape(steps, slots * channels, cells),
    )
    taps = pltpu.VMEM((side * 8, slots * channels), jnp.float32)
    if after:
        kernel, specs, scratch, cost = staged_info_kernel, [VMEM] * 5, [taps], int(COSTS[0] * 1e9)
    else:
        kernel, specs, cost = info_kernel, [pl.BlockSpec(memory_space=pltpu.HBM)] * 4, 10**6
        scratch = [
            *(pltpu.VMEM(array.shape, array.dtype) for array in operands),
            taps,
            pltpu.SemaphoreType.DMA((3 + steps,)),
        ]
        operands = [pltpu.with_memory_space_constraint(array, pltpu.HBM) for array in operands]
    mine, theirs = pl.pallas_call(
        kernel,
        out_shape=[jax.ShapeDtypeStruct((steps, cells), jnp.float32)] * 2,
        in_specs=specs,
        out_specs=[VMEM] * 2,
        scratch_shapes=scratch,
        compiler_params=PARAMS,
        cost_estimate=pl.CostEstimate(flops=cost, bytes_accessed=2**12, transcendentals=0),
        name="sensor_info",
    )(*after, *operands)
    return mine, lax.ppermute(theirs, "block", [(0, 1), (1, 0)])


def start_kernel(mine_ref, other_ref, covariance_ref, operator_ref, start_ref, inputs_ref, states_ref, send_ref):
    here = lax.axis_index("tm") == 0

    @pl.when(here)
    def _():
        state = start_ref[...]
        for t in range(mine_ref.shape[0]):
            drive = times([covariance_ref[t]], mine_ref[t : t + 1, :] + other_ref[t : t + 1, :])
            inputs_ref[t : t + 1, :] = drive
            state = times([operator_ref[t]], state) + drive
            states_ref[t : t + 1, :] = state
        send_ref[...] = jnp.broadcast_to(state, send_ref.shape)

    @pl.when(jnp.logical_not(here))
    def _():
        inputs_ref[...] = jnp.zeros_like(inputs_ref)
        states_ref[...] = jnp.zeros_like(states_ref)
        send_ref[...] = jnp.zeros_like(send_ref)


def first_hop_kernel(
    came_ref, mine_ref, other_ref, covariance_ref, operator_ref, kept_inputs_ref, kept_ref,
    inputs_ref, states_ref, send_ref,
):
    here = lax.axis_index("tm")

    @pl.when(here == 0)
    def _():
        inputs_ref[...] = kept_inputs_ref[...]

    @pl.when(here != 0)
    def _():
        for t in range(mine_ref.shape[0]):
            info = mine_ref[t : t + 1, :] + other_ref[t : t + 1, :]
            inputs_ref[t : t + 1, :] = times([covariance_ref[t]], info)

    @pl.when(here == 1)
    def _():
        state = came_ref[0:1, :]
        for t in range(operator_ref.shape[0]):
            state = times([operator_ref[t]], state) + inputs_ref[t : t + 1, :]
            states_ref[t : t + 1, :] = state
        send_ref[...] = state

    @pl.when(here != 1)
    def _():
        states_ref[...] = kept_ref[...]
        send_ref[...] = came_ref[0:1, :]


def hop_kernel(turn, turned, came_ref, matrices_ref, offsets_ref, kept_ref, states_ref, send_ref):
    here = lax.axis_index("tm") == turn

    @pl.when(here)
    def _():
        state = came_ref[...]
        for t in range(matrices_ref.shape[0]):
            state = times([matrices_ref[t]], state, turned=turned) + offsets_ref[t : t + 1, :]
            states_ref[t : t + 1, :] = state
        send_ref[...] = state

    @pl.when(jnp.logical_not(here))
    def _():
        states_ref[...] = kept_ref[...]
        send_ref[...] = came_ref[...]


def halves(matrix):
    high = matrix.astype(jnp.bfloat16)
    return [high, (matrix - high.astype(jnp.float32)).astype(jnp.bfloat16)]


def composed(gain_ref):
    product = gain_ref[0]
    for t in range(1, gain_ref.shape[0]):
        product = sum(
            lax.dot_general(
                gain_ref[t], part, (((0,), (0 if t > 1 else 1,)), ((), ())), preferred_element_type=jnp.float32
            )
            for part in (halves(product) if t > 1 else [product])
        )
    return product.astype(jnp.float32) if gain_ref.shape[0] > 1 else product.astype(jnp.float32).T


def compose_kernel(senders, after_ref, gain_ref, composed_ref):
    del after_ref
    here = lax.axis_index("tm")
    sends = functools.reduce(jnp.logical_or, [here == place for place in senders])

    @pl.when(sends)
    def _():
        composed_ref[...] = composed(gain_ref)


def late_kernel(place, means_ref, gain_ref, propagator_ref, operator_ref, composed_ref, turned_ref):
    size = gain_ref.shape[1]
    here = lax.axis_index("tm")

    @pl.when(here == place)
    def _():
        composed_ref[:size, :] = composed(gain_ref)
        composed_ref[size:, :] = jnp.zeros((composed_ref.shape[0] - size, size), jnp.float32)
        composed_ref[size : size + 1, :] = offsets(means_ref, gain_ref, propagator_ref)[0]

    @pl.when(here > place + 1)
    def _():
        for t in range(operator_ref.shape[0]):
            turned_ref[t] = operator_ref[t].T


def offsets(means_ref, gain_ref, propagator_ref):
    steps = means_ref.shape[0]
    means = [means_ref[t : t + 1, :] for t in range(steps)]
    moved = times([propagator_ref[...]], *means)
    state = jnp.zeros_like(means[0])
    found = [None] * steps
    for t in reversed(range(steps)):
        left, state = times([gain_ref[t]], moved[t], state)
        found[t] = means[t] - left
        state = state + found[t]
    return state, found


def pair_kernel(
    places,
    skip_place,
    near_ref,
    skip_ref,
    own_parts_ref,
    left_ref,
    near_offset_ref,
    near_parts_ref,
    pair_parts_ref,
    pair_offset_ref,
    skip_parts_ref,
):
    here = lax.axis_index("tm")

    @pl.when(functools.reduce(jnp.logical_or, [here == place for place in places]))
    def _():
        near = halves(near_ref[...])
        own = [own_parts_ref[0], own_parts_ref[1]]
        near_parts_ref[0], near_parts_ref[1] = near
        pair_parts_ref[0], pair_parts_ref[1] = halves(
            jnp.dot(near[0], own[0], preferred_element_type=jnp.float32)
            + jnp.dot(near[1], own[0], preferred_element_type=jnp.float32)
            + jnp.dot(near[0], own[1], preferred_element_type=jnp.float32)
        )
        pair_offset_ref[...] = times(own, near_offset_ref[...], turned=True) + left_ref[...]

    @pl.when(here == skip_place)
    def _():
        skip_parts_ref[0], skip_parts_ref[1] = halves(skip_ref[...])


def beside_kernel(
    late_ref, after_ref, entry_ref, near_parts_ref, near_offset_ref, gain_ref, offsets_ref, kept_ref,
    parts_ref, offset_ref, states_ref,
):
    del after_ref
    size = late_ref.shape[1]
    here = lax.axis_index("tm")

    @pl.when(here == 0)
    def _():
        parts_ref[0], parts_ref[1] = halves(late_ref[:size, :])
        offset_ref[...] = late_ref[size : size + 1, :]

    @pl.when(here != 2)
    def _():
        states_ref[...] = kept_ref[...]

    @pl.when(here == 2)
    def _():
        def put(t, state):
            states_ref[t : t + 1, :] = state

        smooth(parts_times(near_parts_ref, entry_ref) + near_offset_ref[...], gain_ref, offsets_ref, put)


def split_kernel(place, matrix_ref, parts_ref):
    @pl.when(lax.axis_index("tm") == place)
    def _():
        parts_ref[0], parts_ref[1] = halves(matrix_ref[...])


def offsets_kernel(last, means_ref, gain_ref, propagator_ref, offsets_ref, send_ref, own_parts_ref):
    here = lax.axis_index("tm") == last

    @pl.when(jnp.logical_not(here))
    def _():
        own_parts_ref[0], own_parts_ref[1] = halves(composed(gain_ref))
        send_ref[...], found = offsets(means_ref, gain_ref, propagator_ref)
        for t, row in enumerate(found):
            offsets_ref[t : t + 1, :] = row

    @pl.when(here)
    def _():
        offsets_ref[...] = means_ref[...]
        send_ref[...] = means_ref[0:1, :]


def last_kernel(
    last, came_ref, turned_ref, inputs_ref, kept_ref, gain_ref, propagator_ref,
    means_ref, states_ref, send_ref,
):
    @pl.when(lax.axis_index("tm") == last)
    def _():
        steps = turned_ref.shape[0]
        state = came_ref[...]
        means, moved = [], []
        for t in range(steps):
            state = times([turned_ref[t]], state, turned=True) + inputs_ref[t : t + 1, :]
            means_ref[t : t + 1, :] = state
            means.append(state)
            if t < steps - 1:
                moved.append(times([propagator_ref[...]], state))
        states_ref[steps - 1 : steps, :] = state
        for t in reversed(range(steps - 1)):
            left, state = times([gain_ref[t]], moved[t], state)
            state = state + (means[t] - left)
            states_ref[t : t + 1, :] = state
        send_ref[...] = state

    @pl.when(lax.axis_index("tm") != last)
    def _():
        means_ref[...] = kept_ref[...]
        states_ref[...] = kept_ref[...]
        send_ref[...] = came_ref[...]


def smooth(state, gain_ref, offsets_ref, put, first=0):
    for t in reversed(range(first, gain_ref.shape[0])):
        state = times([gain_ref[t]], state) + offsets_ref[t : t + 1, :]
        put(t, state)


def parts_times(parts_ref, row_ref):
    return times([parts_ref[0], parts_ref[1]], row_ref[...], turned=True)


def first_back_kernel(
    place, last_ref, far_offset_ref, far_parts_ref, own_parts_ref, left_ref, came_ref, entry_ref, send_ref
):
    here = lax.axis_index("tm")

    @pl.when(here == place)
    def _():
        entry_ref[...] = parts_times(far_parts_ref, last_ref) + far_offset_ref[...]
        send_ref[...] = parts_times(own_parts_ref, entry_ref) + left_ref[...]

    @pl.when(here != place)
    def _():
        entry_ref[...] = last_ref[...]
        send_ref[...] = jnp.where(here == place - 1, left_ref[...], came_ref[...])


def second_back_kernel(
    last,
    three_ref,
    one_ref,
    entry_ref,
    skip_parts_ref,
    pair_parts_ref,
    pair_offset_ref,
    gain_ref,
    offsets_ref,
    kept_ref,
    came_ref,
    states_ref,
    next_ref,
    send_ref,
):
    here = lax.axis_index("tm")

    def put(t, state):
        states_ref[t : t + 1, :] = state

    @pl.when(here == last - 5)
    def _():
        state = parts_times(skip_parts_ref, three_ref) + one_ref[...]
        next_ref[...] = state
        send_ref[...] = times([pair_parts_ref[0], pair_parts_ref[1]], state, turned=True) + pair_offset_ref[...]
        states_ref[...] = kept_ref[...]

    @pl.when(here != last - 5)
    def _():
        send_ref[...] = came_ref[...]
        next_ref[...] = entry_ref[...]

    @pl.when(here == last - 2)
    def _():
        smooth(entry_ref[...], gain_ref, offsets_ref, put)

    @pl.when((here == last - 3) | (here == last - 1))
    def _():
        smooth(jnp.where(here == last - 1, three_ref[...], one_ref[...]), gain_ref, offsets_ref, put)
        send_ref[...] = states_ref[0:1, :]

    @pl.when((here == last) | (here == last - 4) | (here < last - 5))
    def _():
        states_ref[...] = kept_ref[...]


def back_kernel(
    target,
    stray,
    two_ref,
    one_ref,
    entry_ref,
    near_offset_ref,
    near_parts_ref,
    pair_parts_ref,
    pair_offset_ref,
    gain_ref,
    offsets_ref,
    kept_ref,
    came_ref,
    states_ref,
    next_ref,
    send_ref,
):
    here = lax.axis_index("tm")

    def put(t, state):
        states_ref[t : t + 1, :] = state

    @pl.when(here == target)
    def _():
        send_ref[...] = parts_times(pair_parts_ref, two_ref) + pair_offset_ref[...]
        next_ref[...] = two_ref[...]
        states_ref[...] = kept_ref[...]

    @pl.when(here != target)
    def _():
        send_ref[...] = came_ref[...]
        next_ref[...] = entry_ref[...]

    @pl.when(here == target + 2)
    def _():
        state = parts_times(near_parts_ref, entry_ref) + near_offset_ref[...]
        smooth(state, gain_ref, offsets_ref, put)

    @pl.when((here == target + 1) | (here == stray))
    def _():
        smooth(jnp.where(here == stray, two_ref[...], one_ref[...]), gain_ref, offsets_ref, put)
        send_ref[...] = states_ref[0:1, :]

    @pl.when((here > target + 2) & (here != stray) | (here < target))
    def _():
        states_ref[...] = kept_ref[...]


def final_kernel(
    stray,
    two_ref,
    one_ref,
    late_parts_ref,
    late_offset_ref,
    own_parts_ref,
    left_ref,
    gain_ref,
    offsets_ref,
    kept_ref,
    means_ref,
    result_ref,
    states_ref,
):
    here = lax.axis_index("tm")
    for t in range(means_ref.shape[0]):
        result_ref[t] = means_ref[t : t + 1, :]

    def put(t, state):
        states_ref[t] = state

    @pl.when(here == 0)
    def _():
        state = parts_times(late_parts_ref, two_ref) + late_offset_ref[...]
        smooth(state, gain_ref, offsets_ref, put, 1)
        put(0, times([own_parts_ref[0], own_parts_ref[1]], state, turned=True) + left_ref[...])

    @pl.when((here == 1) | (here == stray))
    def _():
        smooth(jnp.where(here == stray, two_ref[...], one_ref[...]), gain_ref, offsets_ref, put)

    @pl.when((here > 1) & (here != stray))
    def _():
        for t in range(kept_ref.shape[0]):
            states_ref[t] = kept_ref[t : t + 1, :]


def call(kernel, name, outs, *args, cost=1.0):
    return pl.pallas_call(
        kernel,
        out_shape=[
            jax.ShapeDtypeStruct(shape, jnp.bfloat16 if len(shape) == 3 and shape[1] > 1 else jnp.float32)
            for shape in outs
        ],
        in_specs=[VMEM] * len(args),
        out_specs=[VMEM] * len(outs),
        compiler_params=PARAMS,
        cost_estimate=pl.CostEstimate(flops=int(cost * 1e9), bytes_accessed=2**12, transcendentals=0),
        name=name,
    )(*args)


def pass_row(row, rings, places):
    route = {}
    for place in range(places):
        for core in range(2):
            route[place * 2 + core] = place * 2 + 1 - core
    for ring in rings:
        for i, place in enumerate(ring):
            for core in range(2):
                route[place * 2 + core] = ring[(i + 1) % len(ring)] * 2 + core
    return lax.ppermute(row, ("tm", "block"), sorted(route.items()))


def ring_up(place, places):
    if place % 2 and place >= places - 5 and place < places - 1:
        return (place, place + 1, place + 2)
    if place == 0:
        return (0, 1, 3)
    if place % 2 or place == places - 2:
        return (place, place + 1)
    return (place, place + 1, place - 2)


def local(
    scaled_residual_maps,
    measurement_stencil,
    observed_partition,
    active_probe_total,
    filtering_operator,
    updated_covariance,
    backward_factor,
    propagator,
    initial_mean,
):
    steps, size = filtering_operator.shape[0], filtering_operator.shape[-1]
    places = lax.axis_size("tm")
    many, one = (steps, size), (1, size)
    operator = filtering_operator.reshape(steps, size, size)
    covariance = updated_covariance.reshape(steps, size, size)
    gain = backward_factor.reshape(steps, size, size)
    last = places - 1
    matrix = propagator.reshape(size, size)
    square, parts, result = (size, size), (2, size, size), (steps, 1, size)
    sensors = (scaled_residual_maps, measurement_stencil, observed_partition, active_probe_total)
    mine, other = sensor_info((), *sensors)

    def compose(after, *senders):
        return call(functools.partial(compose_kernel, senders), "compose", (square,), after, gain, cost=0.01)[0]

    near_senders = range(3, last - 3, 2)
    inputs, means, send = call(
        start_kernel, "start", (many, many, (8, size)), mine, other, covariance, operator, initial_mean, cost=0.5
    )
    first = lax.ppermute(
        compose(send, last - 1, *near_senders), "tm", [(place, place - 1) for place in (*near_senders, last - 1)]
    )
    skip = lax.ppermute(compose(send, last - 3), "tm", [(last - 3, last - 5)])
    for place in range(1, places):
        if place == 1:
            came = pass_row(send, [ring_up(0, places)], places)
            mine, other = sensor_info((send,), *sensors)
            inputs, means, send = call(
                first_hop_kernel, "forward", (many, many, one),
                came, mine, other, covariance, operator, inputs, means, cost=COSTS[1],
            )
            continue
        came = pass_row(send, [ring_up(place - 1, places)], places)
        if place == 2:
            late, turned = call(
                functools.partial(late_kernel, 1), "late", ((size + 8, size), (steps, size, size)),
                means, gain, matrix, operator, cost=0.5,
            )
            late = lax.ppermute(late, "tm", [(1, 0)])
        if place < last:
            means, send = call(
                functools.partial(hop_kernel, place, place > 2),
                "forward",
                (many, one),
                came,
                turned if place > 2 else operator,
                inputs,
                means,
                cost=COSTS[2] if place == 2 else 0.5,
            )
    offset_rows, left, own_parts = call(
        functools.partial(offsets_kernel, last), "offsets", (many, one, parts), means, gain, matrix
    )
    first_offset = pass_row(left, [(place - 1, place) for place in (*near_senders, last - 1)], places)
    means, states, send = call(
        functools.partial(last_kernel, last),
        "last",
        (many, many, one),
        came,
        turned,
        inputs,
        means,
        gain,
        matrix,
        cost=0.5,
    )
    came = pass_row(send, [(last, last - 2)], places)

    (far_parts,) = call(functools.partial(split_kernel, last - 2), "split", (parts,), first, cost=0.05)
    entry, send = call(
        functools.partial(first_back_kernel, last - 2), "first_back", (one, one),
        came, first_offset, far_parts, own_parts, left, send,
        cost=COSTS[3],
    )
    one_up = pass_row(send, [(last - 2, last - 3, last - 5, last - 4)], places)
    three = pass_row(send, [(last - 2, last - 5), (last, last - 1)], places)
    near_parts, pair_parts, pair_offset, skip_parts = call(
        functools.partial(pair_kernel, tuple(place - 1 for place in near_senders), last - 5),
        "pair",
        (parts, parts, one, parts),
        first,
        skip,
        own_parts,
        left,
        first_offset,
        cost=0.05,
    )
    states, entry, send = call(
        functools.partial(second_back_kernel, last),
        "second_back",
        (many, one, one),
        three,
        one_up,
        entry,
        skip_parts,
        pair_parts,
        pair_offset,
        gain,
        offset_rows,
        states,
        send,
        cost=COSTS[4],
    )
    stray = last - 4
    for target in range(last - 7, -1, -2):
        rings = [(target + 2, target)] + ([(stray + 1, stray)] if stray > 0 else [])
        one_up = pass_row(send, [(target + 2, target + 1)], places)
        two = pass_row(send, rings, places)
        if target:
            states, entry, send = call(
                functools.partial(back_kernel, target, stray), "back", (many, one, one),
                two, one_up, entry, first_offset, near_parts, pair_parts, pair_offset, gain, offset_rows, states,
                send,
            )
        else:
            late_parts, late_offset, states = call(
                beside_kernel, "beside", (parts, one, many),
                late, send, entry, near_parts, first_offset, gain, offset_rows, states, cost=0.05,
            )
            means, states = call(
                functools.partial(final_kernel, stray), "final", (result, result),
                two, one_up, late_parts, late_offset, own_parts, left, gain, offset_rows, states, means,
            )
        stray = -1
    return means, states


def solution(mesh):
    placed = (
        P(("groups", "tm"), "block", None, None),
        P(),
        P(("groups", "tm"), "block"),
        P(("groups", "tm"), "block"),
        P(("groups", "tm"), "block", None, None),
        P(("groups", "tm"), "block", None, None),
        P(("groups", "tm"), "block", None, None),
        P("block", None, None),
        P(("groups", "block"), None),
    )
    return jax.shard_map(
        local,
        mesh=mesh,
        in_specs=placed,
        out_specs=(P(("groups", "tm"), "block", None), P(("groups", "tm"), "block", None)),
        check_vma=False,
    )
```

```python
import functools

import jax
import jax.numpy as jnp
from jax import lax
from jax.experimental import pallas as pl
from jax.experimental.pallas import tpu as pltpu
from jax.sharding import PartitionSpec as P

GH = 16
COSTS = (60.0, 2.5, 2.5, 6.0, 0.5)
VMEM = pl.BlockSpec(memory_space=pltpu.VMEM)
PARAMS = pltpu.CompilerParams(vmem_limit_bytes=16 * 2**20)


def pieces(rows, count=3):
    height = -(-len(rows) * count // 8) * 8
    at = lax.broadcasted_iota(jnp.int32, (height, rows[0].shape[1]), 0)
    block = jnp.zeros(at.shape, jnp.float32)
    for k, rest in enumerate(rows):
        for i in range(count):
            piece = rest.astype(jnp.bfloat16).astype(jnp.float32)
            block = jnp.where(at == k * count + i, piece, block)
            rest = rest - piece
    return block.astype(jnp.bfloat16)


def times(matrices, *rows, turned=False):
    block = pieces(rows)
    product = sum(
        lax.dot_general(
            block, matrix, (((1,), (0 if turned else 1,)), ((), ())), preferred_element_type=jnp.float32
        )
        for matrix in matrices
    )
    found = [jnp.sum(product[3 * k : 3 * k + 3, :], axis=0, keepdims=True) for k in range(len(rows))]
    return found if len(rows) > 1 else found[0]


def info_kernel(stencil_hbm, observed_hbm, active_hbm, maps_hbm, mine_ref, theirs_ref, *scratch):
    stencil_ref, observed_ref, active_ref, maps, taps, sems = scratch

    @pl.when(lax.axis_index("tm") == 0)
    def _():
        copies = []
        for i, (source, target) in enumerate(
            ((stencil_hbm, stencil_ref), (observed_hbm, observed_ref), (active_hbm, active_ref))
        ):
            copies.append(pltpu.make_async_copy(source, target, sems.at[i]))
        for t in range(maps.shape[0]):
            copies.append(pltpu.make_async_copy(maps_hbm.at[t], maps.at[t], sems.at[3 + t]))
        for copy in copies:
            copy.start()
        place_info(stencil_ref, observed_ref, active_ref, maps, mine_ref, theirs_ref, taps, copies)


def staged_info_kernel(after_ref, *refs):
    del after_ref

    @pl.when(lax.axis_index("tm") != 0)
    def _():
        place_info(*refs, [])


def place_info(stencil_ref, observed_ref, active_ref, maps, mine_ref, theirs_ref, taps, copies):
    steps, rows, cells = maps.shape
    slots = observed_ref.shape[1]
    side, _, channels = stencil_ref.shape
    half = side // 2

    repeat = jnp.where(
        lax.broadcasted_iota(jnp.int32, (channels, rows), 1) % channels
        == lax.broadcasted_iota(jnp.int32, (channels, rows), 0),
        1.0,
        0.0,
    ).astype(jnp.bfloat16)
    taps[...] = jnp.zeros_like(taps)
    spread = jnp.where(
        lax.broadcasted_iota(jnp.int32, (slots, rows), 1) // channels
        == lax.broadcasted_iota(jnp.int32, (slots, rows), 0),
        1.0,
        0.0,
    ).astype(jnp.bfloat16)

    cell = lax.broadcasted_iota(jnp.int32, (8, cells), 1)
    width = cells // GH
    down = cell // width
    across = cell % width
    tap = lax.broadcasted_iota(jnp.int32, (8, cells), 0)
    column = across - tap + half
    column_inside = (column >= 0) & (column < width) & (tap < side)
    me = lax.axis_index("block")
    for copy in copies[:3]:
        copy.wait()
    for p in range(side):
        taps[p * 8 : p * 8 + side, :] = jnp.dot(
            stencil_ref[p], repeat, preferred_element_type=jnp.float32
        )
    for t in range(steps):
        owner = lax.broadcasted_iota(jnp.int32, (8, slots), 0)
        slot = lax.broadcasted_iota(jnp.int32, (8, slots), 1)
        live = (observed_ref[t : t + 1, :] == owner) & (slot < active_ref[0:1, t : t + 1])
        weight = jnp.dot(
            jnp.where(live, 1.0, 0.0).astype(jnp.bfloat16), spread, preferred_element_type=jnp.float32
        )
        left = jnp.concatenate([taps[...] * weight[b : b + 1, :] for b in range(2)], axis=0)
        for copy in copies[3 + t : 4 + t]:
            copy.wait()
        shifted = jnp.dot(left.astype(jnp.bfloat16), maps[t], preferred_element_type=jnp.float32)
        found = []
        for b in range(2):
            total = jnp.zeros((8, cells), jnp.float32)
            for p in range(side):
                at = (b * side + p) * 8
                part = pltpu.roll(shifted[at : at + 8, :], ((p - half) * width) % cells, 1)
                row = down - p + half
                total = total + jnp.where((row >= 0) & (row < GH), part, 0.0)
            sides = jnp.zeros((8, cells), jnp.float32)
            for q in range(side):
                part = pltpu.roll(total, (q - half) % cells, 1)
                sides = jnp.where(column_inside & (tap == q), part, sides)
            found.append(jnp.sum(sides, axis=0, keepdims=True))
        mine_ref[t : t + 1, :] = jnp.where(me == 0, found[0], found[1])
        theirs_ref[t : t + 1, :] = jnp.where(me == 0, found[1], found[0])


def sensor_info(after, scaled_residual_maps, measurement_stencil, observed_partition, active_probe_total):
    steps, slots, channels, cells = scaled_residual_maps.shape
    side = measurement_stencil.shape[1]
    operands = (
        measurement_stencil.transpose(1, 2, 0),
        observed_partition,
        active_probe_total.T,
        scaled_residual_maps.reshape(steps, slots * channels, cells),
    )
    taps = pltpu.VMEM((side * 8, slots * channels), jnp.float32)
    if after:
        kernel, specs, scratch, cost = staged_info_kernel, [VMEM] * 5, [taps], int(COSTS[0] * 1e9)
    else:
        kernel, specs, cost = info_kernel, [pl.BlockSpec(memory_space=pltpu.HBM)] * 4, 10**6
        scratch = [
            *(pltpu.VMEM(array.shape, array.dtype) for array in operands),
            taps,
            pltpu.SemaphoreType.DMA((3 + steps,)),
        ]
        operands = [pltpu.with_memory_space_constraint(array, pltpu.HBM) for array in operands]
    mine, theirs = pl.pallas_call(
        kernel,
        out_shape=[jax.ShapeDtypeStruct((steps, cells), jnp.float32)] * 2,
        in_specs=specs,
        out_specs=[VMEM] * 2,
        scratch_shapes=scratch,
        compiler_params=PARAMS,
        cost_estimate=pl.CostEstimate(flops=cost, bytes_accessed=2**12, transcendentals=0),
        name="sensor_info",
    )(*after, *operands)
    return mine, lax.ppermute(theirs, "block", [(0, 1), (1, 0)])


def start_kernel(mine_ref, other_ref, covariance_ref, operator_ref, start_ref, inputs_ref, states_ref, send_ref):
    here = lax.axis_index("tm") == 0

    @pl.when(here)
    def _():
        state = start_ref[...]
        for t in range(mine_ref.shape[0]):
            drive = times([covariance_ref[t]], mine_ref[t : t + 1, :] + other_ref[t : t + 1, :])
            inputs_ref[t : t + 1, :] = drive
            state = times([operator_ref[t]], state) + drive
            states_ref[t : t + 1, :] = state
        send_ref[...] = jnp.broadcast_to(state, send_ref.shape)

    @pl.when(jnp.logical_not(here))
    def _():
        inputs_ref[...] = jnp.zeros_like(inputs_ref)
        states_ref[...] = jnp.zeros_like(states_ref)
        send_ref[...] = jnp.zeros_like(send_ref)


def drive(mine_ref, other_ref, covariance_ref, inputs_ref):
    for t in range(mine_ref.shape[0]):
        info = mine_ref[t : t + 1, :] + other_ref[t : t + 1, :]
        inputs_ref[t : t + 1, :] = times([covariance_ref[t]], info)


def first_hop_kernel(
    came_ref, mine_ref, other_ref, covariance_ref, operator_ref, kept_inputs_ref, kept_ref,
    inputs_ref, states_ref, send_ref,
):
    here = lax.axis_index("tm")

    @pl.when(here == 1)
    def _():
        drive(mine_ref, other_ref, covariance_ref, inputs_ref)
        state = came_ref[0:1, :]
        for t in range(operator_ref.shape[0]):
            state = times([operator_ref[t]], state) + inputs_ref[t : t + 1, :]
            states_ref[t : t + 1, :] = state
        send_ref[...] = state

    @pl.when(here != 1)
    def _():
        inputs_ref[...] = kept_inputs_ref[...]
        states_ref[...] = kept_ref[...]
        send_ref[...] = came_ref[0:1, :]


def hop_kernel(turn, turned, came_ref, matrices_ref, offsets_ref, kept_ref, states_ref, send_ref):
    here = lax.axis_index("tm") == turn

    @pl.when(here)
    def _():
        state = came_ref[...]
        for t in range(matrices_ref.shape[0]):
            state = times([matrices_ref[t]], state, turned=turned) + offsets_ref[t : t + 1, :]
            states_ref[t : t + 1, :] = state
        send_ref[...] = state

    @pl.when(jnp.logical_not(here))
    def _():
        states_ref[...] = kept_ref[...]
        send_ref[...] = came_ref[...]


def halves(matrix):
    high = matrix.astype(jnp.bfloat16)
    return [high, (matrix - high.astype(jnp.float32)).astype(jnp.bfloat16)]


def composed(gain_ref):
    product = gain_ref[0]
    for t in range(1, gain_ref.shape[0]):
        product = sum(
            lax.dot_general(
                gain_ref[t], part, (((0,), (0 if t > 1 else 1,)), ((), ())), preferred_element_type=jnp.float32
            )
            for part in (halves(product) if t > 1 else [product])
        )
    return product.astype(jnp.float32) if gain_ref.shape[0] > 1 else product.astype(jnp.float32).T


def compose_kernel(senders, after_ref, gain_ref, composed_ref):
    del after_ref
    here = lax.axis_index("tm")
    sends = functools.reduce(jnp.logical_or, [here == place for place in senders])

    @pl.when(sends)
    def _():
        composed_ref[...] = composed(gain_ref)


def late_kernel(
    place, means_ref, gain_ref, propagator_ref, operator_ref, mine_ref, other_ref, covariance_ref, kept_inputs_ref,
    composed_ref, turned_ref, inputs_ref,
):
    size = gain_ref.shape[1]
    here = lax.axis_index("tm")

    @pl.when(here == place)
    def _():
        composed_ref[:size, :] = composed(gain_ref)
        composed_ref[size:, :] = jnp.zeros((composed_ref.shape[0] - size, size), jnp.float32)
        composed_ref[size : size + 1, :] = offsets(means_ref, gain_ref, propagator_ref)[0]

    @pl.when(here <= place)
    def _():
        inputs_ref[...] = kept_inputs_ref[...]

    @pl.when(here > place)
    def _():
        drive(mine_ref, other_ref, covariance_ref, inputs_ref)

    @pl.when(here > place + 1)
    def _():
        for t in range(operator_ref.shape[0]):
            turned_ref[t] = operator_ref[t].T


def offsets(means_ref, gain_ref, propagator_ref):
    steps = means_ref.shape[0]
    means = [means_ref[t : t + 1, :] for t in range(steps)]
    moved = times([propagator_ref[...]], *means)
    state = jnp.zeros_like(means[0])
    found = [None] * steps
    for t in reversed(range(steps)):
        left, state = times([gain_ref[t]], moved[t], state)
        found[t] = means[t] - left
        state = state + found[t]
    return state, found


def pair_kernel(
    places,
    skip_place,
    near_ref,
    skip_ref,
    own_parts_ref,
    left_ref,
    near_offset_ref,
    near_parts_ref,
    pair_parts_ref,
    pair_offset_ref,
    skip_parts_ref,
):
    here = lax.axis_index("tm")

    @pl.when(functools.reduce(jnp.logical_or, [here == place for place in places]))
    def _():
        near = halves(near_ref[...])
        own = [own_parts_ref[0], own_parts_ref[1]]
        near_parts_ref[0], near_parts_ref[1] = near
        pair_parts_ref[0], pair_parts_ref[1] = halves(
            jnp.dot(near[0], own[0], preferred_element_type=jnp.float32)
            + jnp.dot(near[1], own[0], preferred_element_type=jnp.float32)
            + jnp.dot(near[0], own[1], preferred_element_type=jnp.float32)
        )
        pair_offset_ref[...] = times(own, near_offset_ref[...], turned=True) + left_ref[...]

    @pl.when(here == skip_place)
    def _():
        skip_parts_ref[0], skip_parts_ref[1] = halves(skip_ref[...])


def beside_kernel(
    late_ref, after_ref, entry_ref, near_parts_ref, near_offset_ref, gain_ref, offsets_ref, kept_ref,
    parts_ref, offset_ref, states_ref,
):
    del after_ref
    size = late_ref.shape[1]
    here = lax.axis_index("tm")

    @pl.when(here == 0)
    def _():
        parts_ref[0], parts_ref[1] = halves(late_ref[:size, :])
        offset_ref[...] = late_ref[size : size + 1, :]

    @pl.when(here != 2)
    def _():
        states_ref[...] = kept_ref[...]

    @pl.when(here == 2)
    def _():
        def put(t, state):
            states_ref[t : t + 1, :] = state

        smooth(parts_times(near_parts_ref, entry_ref) + near_offset_ref[...], gain_ref, offsets_ref, put)


def split_kernel(place, matrix_ref, parts_ref):
    @pl.when(lax.axis_index("tm") == place)
    def _():
        parts_ref[0], parts_ref[1] = halves(matrix_ref[...])


def offsets_kernel(last, means_ref, gain_ref, propagator_ref, offsets_ref, send_ref, own_parts_ref):
    here = lax.axis_index("tm") == last

    @pl.when(jnp.logical_not(here))
    def _():
        own_parts_ref[0], own_parts_ref[1] = halves(composed(gain_ref))
        send_ref[...], found = offsets(means_ref, gain_ref, propagator_ref)
        for t, row in enumerate(found):
            offsets_ref[t : t + 1, :] = row

    @pl.when(here)
    def _():
        offsets_ref[...] = means_ref[...]
        send_ref[...] = means_ref[0:1, :]


def last_kernel(
    last, came_ref, turned_ref, inputs_ref, kept_ref, gain_ref, propagator_ref,
    means_ref, states_ref, send_ref,
):
    @pl.when(lax.axis_index("tm") == last)
    def _():
        steps = turned_ref.shape[0]
        state = came_ref[...]
        means, moved = [], []
        for t in range(steps):
            state = times([turned_ref[t]], state, turned=True) + inputs_ref[t : t + 1, :]
            means_ref[t : t + 1, :] = state
            means.append(state)
            if t < steps - 1:
                moved.append(times([propagator_ref[...]], state))
        states_ref[steps - 1 : steps, :] = state
        for t in reversed(range(steps - 1)):
            left, state = times([gain_ref[t]], moved[t], state)
            state = state + (means[t] - left)
            states_ref[t : t + 1, :] = state
        send_ref[...] = state

    @pl.when(lax.axis_index("tm") != last)
    def _():
        means_ref[...] = kept_ref[...]
        states_ref[...] = kept_ref[...]
        send_ref[...] = came_ref[...]


def smooth(state, gain_ref, offsets_ref, put, first=0):
    for t in reversed(range(first, gain_ref.shape[0])):
        state = times([gain_ref[t]], state) + offsets_ref[t : t + 1, :]
        put(t, state)


def parts_times(parts_ref, row_ref):
    return times([parts_ref[0], parts_ref[1]], row_ref[...], turned=True)


def first_back_kernel(
    place, last_ref, far_offset_ref, far_parts_ref, own_parts_ref, left_ref, came_ref, entry_ref, send_ref
):
    here = lax.axis_index("tm")

    @pl.when(here == place)
    def _():
        entry_ref[...] = parts_times(far_parts_ref, last_ref) + far_offset_ref[...]
        send_ref[...] = parts_times(own_parts_ref, entry_ref) + left_ref[...]

    @pl.when(here != place)
    def _():
        entry_ref[...] = last_ref[...]
        send_ref[...] = jnp.where(here == place - 1, left_ref[...], came_ref[...])


def second_back_kernel(
    last,
    three_ref,
    one_ref,
    entry_ref,
    skip_parts_ref,
    pair_parts_ref,
    pair_offset_ref,
    gain_ref,
    offsets_ref,
    kept_ref,
    came_ref,
    states_ref,
    next_ref,
    send_ref,
):
    here = lax.axis_index("tm")

    def put(t, state):
        states_ref[t : t + 1, :] = state

    @pl.when(here == last - 5)
    def _():
        state = parts_times(skip_parts_ref, three_ref) + one_ref[...]
        next_ref[...] = state
        send_ref[...] = times([pair_parts_ref[0], pair_parts_ref[1]], state, turned=True) + pair_offset_ref[...]
        states_ref[...] = kept_ref[...]

    @pl.when(here != last - 5)
    def _():
        send_ref[...] = came_ref[...]
        next_ref[...] = entry_ref[...]

    @pl.when(here == last - 2)
    def _():
        smooth(entry_ref[...], gain_ref, offsets_ref, put)

    @pl.when((here == last - 3) | (here == last - 1))
    def _():
        smooth(jnp.where(here == last - 1, three_ref[...], one_ref[...]), gain_ref, offsets_ref, put)
        send_ref[...] = states_ref[0:1, :]

    @pl.when((here == last) | (here == last - 4) | (here < last - 5))
    def _():
        states_ref[...] = kept_ref[...]


def back_kernel(
    target,
    stray,
    two_ref,
    one_ref,
    entry_ref,
    near_offset_ref,
    near_parts_ref,
    pair_parts_ref,
    pair_offset_ref,
    gain_ref,
    offsets_ref,
    kept_ref,
    came_ref,
    states_ref,
    next_ref,
    send_ref,
):
    here = lax.axis_index("tm")

    def put(t, state):
        states_ref[t : t + 1, :] = state

    @pl.when(here == target)
    def _():
        send_ref[...] = parts_times(pair_parts_ref, two_ref) + pair_offset_ref[...]
        next_ref[...] = two_ref[...]
        states_ref[...] = kept_ref[...]

    @pl.when(here != target)
    def _():
        send_ref[...] = came_ref[...]
        next_ref[...] = entry_ref[...]

    @pl.when(here == target + 2)
    def _():
        state = parts_times(near_parts_ref, entry_ref) + near_offset_ref[...]
        smooth(state, gain_ref, offsets_ref, put)

    @pl.when((here == target + 1) | (here == stray))
    def _():
        smooth(jnp.where(here == stray, two_ref[...], one_ref[...]), gain_ref, offsets_ref, put)
        send_ref[...] = states_ref[0:1, :]

    @pl.when((here > target + 2) & (here != stray) | (here < target))
    def _():
        states_ref[...] = kept_ref[...]


def final_kernel(
    stray,
    two_ref,
    one_ref,
    late_parts_ref,
    late_offset_ref,
    own_parts_ref,
    left_ref,
    gain_ref,
    offsets_ref,
    kept_ref,
    means_ref,
    result_ref,
    states_ref,
):
    here = lax.axis_index("tm")
    for t in range(means_ref.shape[0]):
        result_ref[t] = means_ref[t : t + 1, :]

    def put(t, state):
        states_ref[t] = state

    @pl.when(here == 0)
    def _():
        state = parts_times(late_parts_ref, two_ref) + late_offset_ref[...]
        smooth(state, gain_ref, offsets_ref, put, 1)
        put(0, times([own_parts_ref[0], own_parts_ref[1]], state, turned=True) + left_ref[...])

    @pl.when((here == 1) | (here == stray))
    def _():
        smooth(jnp.where(here == stray, two_ref[...], one_ref[...]), gain_ref, offsets_ref, put)

    @pl.when((here > 1) & (here != stray))
    def _():
        for t in range(kept_ref.shape[0]):
            states_ref[t] = kept_ref[t : t + 1, :]


def call(kernel, name, outs, *args, cost=1.0):
    return pl.pallas_call(
        kernel,
        out_shape=[
            jax.ShapeDtypeStruct(shape, jnp.bfloat16 if len(shape) == 3 and shape[1] > 1 else jnp.float32)
            for shape in outs
        ],
        in_specs=[VMEM] * len(args),
        out_specs=[VMEM] * len(outs),
        compiler_params=PARAMS,
        cost_estimate=pl.CostEstimate(flops=int(cost * 1e9), bytes_accessed=2**12, transcendentals=0),
        name=name,
    )(*args)


def pass_row(row, rings, places):
    route = {}
    for place in range(places):
        for core in range(2):
            route[place * 2 + core] = place * 2 + 1 - core
    for ring in rings:
        for i, place in enumerate(ring):
            for core in range(2):
                route[place * 2 + core] = ring[(i + 1) % len(ring)] * 2 + core
    return lax.ppermute(row, ("tm", "block"), sorted(route.items()))


def ring_up(place, places):
    if place % 2 and place >= places - 5 and place < places - 1:
        return (place, place + 1, place + 2)
    if place == 0:
        return (0, 1, 3, places - 1)
    if place % 2 or place == places - 2:
        return (place, place + 1)
    return (place, place + 1, place - 2)


def local(
    scaled_residual_maps,
    measurement_stencil,
    observed_partition,
    active_probe_total,
    filtering_operator,
    updated_covariance,
    backward_factor,
    propagator,
    initial_mean,
):
    steps, size = filtering_operator.shape[0], filtering_operator.shape[-1]
    places = lax.axis_size("tm")
    many, one = (steps, size), (1, size)
    operator = filtering_operator.reshape(steps, size, size)
    covariance = updated_covariance.reshape(steps, size, size)
    gain = backward_factor.reshape(steps, size, size)
    last = places - 1
    matrix = propagator.reshape(size, size)
    square, parts, result = (size, size), (2, size, size), (steps, 1, size)
    sensors = (scaled_residual_maps, measurement_stencil, observed_partition, active_probe_total)
    mine, other = sensor_info((), *sensors)

    def compose(after, *senders):
        return call(functools.partial(compose_kernel, senders), "compose", (square,), after, gain, cost=0.01)[0]

    near_senders = range(3, last - 3, 2)
    inputs, means, send = call(
        start_kernel, "start", (many, many, (8, size)), mine, other, covariance, operator, initial_mean, cost=0.5
    )
    first = lax.ppermute(
        compose(send, last - 1, *near_senders), "tm", [(place, place - 1) for place in (*near_senders, last - 1)]
    )
    skip = lax.ppermute(compose(send, last - 3), "tm", [(last - 3, last - 5)])
    for place in range(1, places):
        if place == 1:
            came = pass_row(send, [ring_up(0, places)], places)
            mine, other = sensor_info((send,), *sensors)
            inputs, means, send = call(
                first_hop_kernel, "forward", (many, many, one),
                came, mine, other, covariance, operator, inputs, means, cost=COSTS[1],
            )
            continue
        came = pass_row(send, [ring_up(place - 1, places)], places)
        if place == 2:
            late, turned, inputs = call(
                functools.partial(late_kernel, 1), "late", ((size + 8, size), (steps, size, size), many),
                means, gain, matrix, operator, mine, other, covariance, inputs, cost=0.5,
            )
            late = lax.ppermute(late, "tm", [(1, 0)])
        if place < last:
            means, send = call(
                functools.partial(hop_kernel, place, place > 2),
                "forward",
                (many, one),
                came,
                turned if place > 2 else operator,
                inputs,
                means,
                cost=COSTS[2] if place == 2 else 0.5,
            )
    offset_rows, left, own_parts = call(
        functools.partial(offsets_kernel, last), "offsets", (many, one, parts), means, gain, matrix
    )
    first_offset = pass_row(left, [(place - 1, place) for place in (*near_senders, last - 1)], places)
    means, states, send = call(
        functools.partial(last_kernel, last),
        "last",
        (many, many, one),
        came,
        turned,
        inputs,
        means,
        gain,
        matrix,
        cost=0.5,
    )
    came = pass_row(send, [(last, last - 2)], places)

    (far_parts,) = call(functools.partial(split_kernel, last - 2), "split", (parts,), first, cost=0.05)
    entry, send = call(
        functools.partial(first_back_kernel, last - 2), "first_back", (one, one),
        came, first_offset, far_parts, own_parts, left, send,
        cost=COSTS[3],
    )
    one_up = pass_row(send, [(last - 2, last - 3, last - 5, last - 4)], places)
    three = pass_row(send, [(last - 2, last - 5), (last, last - 1)], places)
    near_parts, pair_parts, pair_offset, skip_parts = call(
        functools.partial(pair_kernel, tuple(place - 1 for place in near_senders), last - 5),
        "pair",
        (parts, parts, one, parts),
        first,
        skip,
        own_parts,
        left,
        first_offset,
        cost=0.05,
    )
    states, entry, send = call(
        functools.partial(second_back_kernel, last),
        "second_back",
        (many, one, one),
        three,
        one_up,
        entry,
        skip_parts,
        pair_parts,
        pair_offset,
        gain,
        offset_rows,
        states,
        send,
        cost=COSTS[4],
    )
    stray = last - 4
    for target in range(last - 7, -1, -2):
        rings = [(target + 2, target)] + ([(stray + 1, stray)] if stray > 0 else [])
        one_up = pass_row(send, [(target + 2, target + 1)], places)
        two = pass_row(send, rings, places)
        if target:
            states, entry, send = call(
                functools.partial(back_kernel, target, stray), "back", (many, one, one),
                two, one_up, entry, first_offset, near_parts, pair_parts, pair_offset, gain, offset_rows, states,
                send,
            )
        else:
            late_parts, late_offset, states = call(
                beside_kernel, "beside", (parts, one, many),
                late, send, entry, near_parts, first_offset, gain, offset_rows, states, cost=0.05,
            )
            means, states = call(
                functools.partial(final_kernel, stray), "final", (result, result),
                two, one_up, late_parts, late_offset, own_parts, left, gain, offset_rows, states, means,
            )
        stray = -1
    return means, states


def solution(mesh):
    placed = (
        P(("groups", "tm"), "block", None, None),
        P(),
        P(("groups", "tm"), "block"),
        P(("groups", "tm"), "block"),
        P(("groups", "tm"), "block", None, None),
        P(("groups", "tm"), "block", None, None),
        P(("groups", "tm"), "block", None, None),
        P("block", None, None),
        P(("groups", "block"), None),
    )
    return jax.shard_map(
        local,
        mesh=mesh,
        in_specs=placed,
        out_specs=(P(("groups", "tm"), "block", None), P(("groups", "tm"), "block", None)),
        check_vma=False,
    )
```
